32 devices in a mesh: shard: 4 (over z), head: 4 (over x, core), tensor: 2 (over y).
Axes of the slice: x: 2, y: 2, z: 4, core: 2. Of those that a mesh axis runs over, the one named last changes fastest.
Arguments:
- block_input: bfloat16 [192, 197, 512], P(('shard', 'head', 'tensor')), may hold values from -6 to 6
- cotangent: bfloat16 [192, 197, 512], P(('shard', 'head', 'tensor')), may hold values from -6 to 6
- routes: int32 [192, 197, 2], P(('shard', 'head', 'tensor')), may hold values from 0 to 3, all different within a row; in each aligned block of 1182 rows (0 to 1181, 1182 to 2363, ..., all dimensions but the last counted through in order) at most 738 rows name the same one
- priority: int32 [32, 2364], P(('shard', 'head', 'tensor')), may hold values from 0 to 2363, each once within a row
- norm_params: float32 [4, 512], replicated, may hold values from -0.4 to 1.3, as said below
- norm_moment: float32 [4, 512], replicated, may hold values from -112 to 112
- norm_square: float32 [4, 512], replicated, may hold values from 12.10368 to 192.9024
- qkv_weight: float32 [512, 3, 512], P(('shard', 'tensor'), None, 'head'), may hold values from -0.3125 to 0.3125
- qkv_moment: float32 [512, 3, 512], P(('shard', 'tensor'), None, 'head'), may hold values from -128 to 128
- qkv_square: float32 [512, 3, 512], P(('shard', 'tensor'), None, 'head'), may hold values from 18.912 to 302.592
- attn_weight: float32 [512, 512], P('head', ('shard', 'tensor')), may hold values from -0.75 to 0.75
- attn_moment: float32 [512, 512], P('head', ('shard', 'tensor')), may hold values from -48 to 48
- attn_square: float32 [512, 512], P('head', ('shard', 'tensor')), may hold values from 3.02592 to 49.1712
- router_weight: float32 [512, 4], replicated, may hold values from -0.1875 to 0.1875
- router_moment: float32 [512, 4], replicated, may hold values from -1024 to 1024
- router_square: float32 [512, 4], replicated, may hold values from 1210.368 to 19365.889
- expert_in: float32 [4, 512, 2048], P('shard', 'head', 'tensor'), may hold values from -0.25 to 0.25
- in_moment: float32 [4, 512, 2048], P('shard', 'head', 'tensor'), may hold values from -16 to 16
- in_square: float32 [4, 512, 2048], P('shard', 'head', 'tensor'), may hold values from 0.37824 to 6.05184
- expert_out: float32 [4, 2048, 512], P('shard', 'tensor', 'head'), may hold values from -0.4375 to 0.4375
- out_moment: float32 [4, 2048, 512], P('shard', 'tensor', 'head'), may hold values from -14 to 14
- out_square: float32 [4, 2048, 512], P('shard', 'tensor', 'head'), may hold values from 0.21276 to 3.4278
Outputs:
- block_output: bfloat16 [192, 197, 512], P(('shard', 'head', 'tensor'))
- input_grad: float32 [192, 197, 512], P(('shard', 'head', 'tensor'))
- new_norm: float32 [4, 512], replicated
- new_norm_moment: float32 [4, 512], replicated
- new_norm_square: float32 [4, 512], replicated
- new_qkv: float32 [512, 3, 512], P(('shard', 'tensor'), None, 'head')
- new_qkv_moment: float32 [512, 3, 512], P(('shard', 'tensor'), None, 'head')
- new_qkv_square: float32 [512, 3, 512], P(('shard', 'tensor'), None, 'head')
- new_attn: float32 [512, 512], P('head', ('shard', 'tensor'))
- new_attn_moment: float32 [512, 512], P('head', ('shard', 'tensor'))
- new_attn_square: float32 [512, 512], P('head', ('shard', 'tensor'))
- new_router: float32 [512, 4], replicated
- new_router_moment: float32 [512, 4], replicated
- new_router_square: float32 [512, 4], replicated
- new_in: float32 [4, 512, 2048], P('shard', 'head', 'tensor')
- new_in_moment: float32 [4, 512, 2048], P('shard', 'head', 'tensor')
- new_in_square: float32 [4, 512, 2048], P('shard', 'head', 'tensor')
- new_out: float32 [4, 2048, 512], P('shard', 'tensor', 'head')
- new_out_moment: float32 [4, 2048, 512], P('shard', 'tensor', 'head')
- new_out_square: float32 [4, 2048, 512], P('shard', 'tensor', 'head')
The draws below stay inside these ranges and needn't reach their ends.
Inputs may be any that keep to these rules, and one draw needn't show every extreme that they name: `routes`: A token's two experts differ; among the tokens of one routing group no expert is named more than 738 times. `priority`: row g ranks the pairs of routing group g (the tokens of images g * 6 to g * 6 + 5); pair 2 t + k is route k of the group's t-th token; each rank appears once. `norm_params`: rows 0 and 2 are the two norms' gains, rows 1 and 3 their biases.
All inputs are finite; a program needn't handle non-finite values.
Results may differ from the reference program's by a relative error of at most 0.025.
Values may be sent and summed in bfloat16 or wider, within the bound.
No kernel may reach another device: no remote copies, remote signals or barrier semaphores. Data moves between devices by JAX's collectives and lax.ppermute only.
A program may use at most 192 MiB of HBM per device.

```python
import math
from functools import partial
import jax
import jax.numpy as jnp
import numpy as np
from jax import lax

D = 512
HEADS = 8
HEAD_DIM = 64
FF = 2048
SEQ = 197
IMG_DEV = 6
STEP = 10
IMAGES = 192
TOKENS = 37824
EXPERTS = 4
SOURCES = 32
ROWS = 1182
CAP = 664
MOST = 738


def draw_norm_params(key, part):
    gain_key = jax.random.fold_in(key, 11)
    bias_key = jax.random.fold_in(key, 12)
    gain_rows = 1.0 + 0.3 * jax.random.uniform(gain_key, (2, D), jnp.float32, -1.0, 1.0)
    bias_rows = jnp.clip(0.1 * jax.random.normal(bias_key, (2, D), jnp.float32), -0.4, 0.4)
    return jnp.stack([gain_rows[0], bias_rows[0], gain_rows[1], bias_rows[1]]).astype(jnp.float32)


def with_spikes(values, stream_key, source, target, shards_of, factor):
    def block_of(axis_at):
        return (jnp.arange(values.shape[axis_at]) // (values.shape[axis_at] // shards_of)).reshape((-1,) + (1,) * (values.ndim - 1 - axis_at))

    first = jax.random.permutation(stream_key, shards_of)[block_of(target)]
    other_side = (block_of(target) + shards_of // 2) % shards_of
    return jnp.where((block_of(source) == first) | (block_of(source) == other_side), factor * values, values)


def steps_of(rng, dims, split, smallest, top_value):
    level = 1.0
    for dim, shards_of in split:
        steps = jax.random.uniform(jax.random.fold_in(jax.random.fold_in(rng, 6), dim), (shards_of,), jnp.float32, smallest / len(split), top_value / len(split))
        level = level * jnp.repeat(jnp.exp(steps), dims[dim] // shards_of).reshape((-1,) + (1,) * (len(dims) - 1 - dim))
    return level


def routed_block(rng, own, number, rows, number_of, top, reach, skew):
    ranking = jax.random.permutation(rng, number_of)
    crowded, usual = shares(number_of, rows * top, reach, skew, True), shares(number_of, rows * top, reach, skew, False)
    places = jnp.arange(number_of)

    def named(tallies, rotation):
        used = int((tallies > 0).sum())
        fixed = max(1, used // 4)
        passed = fixed + (places - fixed + rotation * (used - fixed)) % max(1, number_of - fixed)
        return jnp.zeros((number_of,), jnp.int32).at[ranking[jnp.where(places < fixed, places, passed)]].set(jnp.asarray(tallies, jnp.int32))

    tallies = jnp.where(number % 4 == 0, named(crowded, number // 4), named(usual, number - number // 4 - 1))
    mixed = jax.random.permutation(jax.random.fold_in(own, 3), number_of)
    giver, sink = mixed[0:number_of // 2 * 2:2], mixed[1:number_of // 2 * 2:2]
    slack = jnp.minimum(tallies[giver] - 1, reach - tallies[sink]) // 2
    slack = jnp.where((giver == ranking[0]) | (sink == ranking[0]) | (tallies[sink] == 0), 0, jnp.maximum(slack, 0))
    passed = jax.random.randint(jax.random.fold_in(own, 4), (number_of // 2,), 0, 1 << 20) % (slack + 1)
    tallies = tallies.at[giver].add(-passed).at[sink].add(passed)
    labels = jnp.searchsorted(jnp.cumsum(tallies), jnp.arange(rows * top), side="right").astype(jnp.int32)
    grid = labels.reshape(top, rows).T
    grid = grid[jax.random.permutation(jax.random.fold_in(own, 1), rows)]
    rotation = jax.random.randint(jax.random.fold_in(own, 2), (rows, 1), 0, top)
    return jnp.take_along_axis(grid, (jnp.arange(top)[None, :] + rotation) % top, axis=1)


def shares(number_of, total, bound, lean, full):
    loads = [(1 << 20) // math.isqrt(rank ** lean) + 1 for rank in range(1, number_of + 1)]
    largest = bound if full else min(bound, max(-(-total // number_of), total * loads[0] // sum(loads)))
    least = 1 if total - largest >= number_of - 1 else 0
    holding, surplus = [largest] + [least] * (number_of - 1), total - largest - least * (number_of - 1)
    while surplus > 0:
        candidates = [i for i in range(1, number_of) if holding[i] < largest] or [i for i in range(1, number_of) if holding[i] < bound]
        pool, left = sum([loads[i] for i in candidates]), surplus
        for i in candidates:
            more = min(bound - holding[i], max(1, left * loads[i] // pool), surplus)
            holding[i] = holding[i] + more
            surplus = surplus - more
    return np.array(holding)


def scatter_about(key, extent, deviation, most, pieces=(), kind=jnp.bfloat16):
    factor_of = steps_of(key, extent, pieces, -0.22, 0.18) if pieces else 1.0
    array = jax.random.normal(key, extent, jnp.float32) * deviation * factor_of
    return jnp.minimum(jnp.maximum(array, -most), most).astype(kind)


def heavy_noise(stream_key, dims, scale, most, pieces, heavy, held_as=jnp.bfloat16):
    entries = scale * jax.random.normal(stream_key, dims, jnp.float32)
    if pieces:
        entries = entries * steps_of(stream_key, dims, pieces, -0.22, 0.18)
    return jnp.clip(with_spikes(entries, jax.random.fold_in(stream_key, 3), *heavy), -most, most).astype(held_as)


def setup_inputs(seed: int = 0) -> dict:
    key_of = jax.random.split(jax.random.key(seed), 23)
    block_input = scatter_about(key_of[0], (IMAGES, SEQ, D), 1.0, 6.0, ((0, 32),))
    cotangent = heavy_noise(key_of[1], (IMAGES, SEQ, D), 1.0, 6.0, ((0, 32),), (0, 2, 32, 2.75))
    routes_keys = jax.random.split(jax.random.fold_in(key_of[2], 1), IMAGES * SEQ // ROWS)
    routes_turns = jax.random.permutation(jax.random.fold_in(key_of[2], 3), IMAGES * SEQ // ROWS)
    routes = jax.vmap(lambda own, number: routed_block(jax.random.fold_in(key_of[2], 2), own, number, ROWS, EXPERTS, 2, MOST, 1))(routes_keys, routes_turns).reshape((IMAGES, SEQ, 2))
    priority = jax.vmap(lambda own: jax.random.permutation(own, 2 * ROWS))(jax.random.split(key_of[3], SOURCES)).reshape((SOURCES, 2 * ROWS)).astype(jnp.int32)
    norm_params = draw_norm_params(jax.random.fold_in(key_of[22], 71), 0)
    norm_moment = scatter_about(key_of[5], (4, D), (0.09 * TOKENS ** 0.5), 112.0, (), jnp.float32)
    norm_square = jnp.clip(jnp.exp(jax.random.uniform(key_of[6], (4, D), jnp.float32, math.log(12.10368), math.log(192.9024))), 12.10368, 192.9024)
    qkv_weight = scatter_about(key_of[7], (D, 3, D), (1.3 / D ** 0.5), 0.3125, ((0, 8), (2, 4)), jnp.float32)
    qkv_moment = scatter_about(key_of[8], (D, 3, D), (0.11 * TOKENS ** 0.5), 128.0, ((0, 8), (2, 4)), jnp.float32)
    qkv_square = jnp.clip(jnp.exp(math.log(302.592) - 2.7725887 * jax.random.uniform(key_of[9], (D, 3, D), jnp.float32) ** steps_of(key_of[9], (D, 3, D), ((0, 8), (2, 4)), -0.2, 0.2)), 18.912, 302.592)
    attn_weight = scatter_about(key_of[10], (D, D), (3.0 / D ** 0.5), 0.75, ((0, 4), (1, 8)), jnp.float32)
    attn_moment = scatter_about(key_of[11], (D, D), (0.044 * TOKENS ** 0.5), 48.0, ((0, 4), (1, 8)), jnp.float32)
    attn_square = jnp.clip(jnp.exp(math.log(49.1712) - 2.7880929 * jax.random.uniform(key_of[12], (D, D), jnp.float32) ** steps_of(key_of[12], (D, D), ((0, 4), (1, 8)), -0.2, 0.2)), 3.02592, 49.1712)
    router_weight = scatter_about(key_of[13], (D, EXPERTS), (0.75 / D ** 0.5), 0.1875, (), jnp.float32)
    router_moment = scatter_about(key_of[14], (D, EXPERTS), (0.055 * (2 * D * TOKENS / EXPERTS) ** 0.5), 1024.0, (), jnp.float32)
    router_square = jnp.clip(jnp.exp(jax.random.uniform(key_of[15], (D, EXPERTS), jnp.float32, math.log(1210.368), math.log(19365.889))), 1210.368, 19365.889)
    expert_in = scatter_about(key_of[16], (EXPERTS, D, FF), D ** -0.5, 0.25, ((0, 4), (1, 4), (2, 2)), jnp.float32)
    in_moment = scatter_about(key_of[17], (EXPERTS, D, FF), (0.022 * (2 * TOKENS / EXPERTS) ** 0.5), 16.0, ((0, 4), (1, 4), (2, 2)), jnp.float32)
    in_square = jnp.clip(jnp.exp(math.log(6.05184) - 2.7725887 * jax.random.uniform(key_of[18], (EXPERTS, D, FF), jnp.float32) ** steps_of(key_of[18], (EXPERTS, D, FF), ((0, 4), (1, 4), (2, 2)), -0.2, 0.2)), 0.37824, 6.05184)
    expert_out = scatter_about(key_of[19], (EXPERTS, FF, D), (0.8 * EXPERTS / FF ** 0.5), 0.4375, ((0, 4), (1, 2), (2, 4)), jnp.float32)
    out_moment = scatter_about(key_of[20], (EXPERTS, FF, D), (0.066 * (2 * TOKENS) ** 0.5 / EXPERTS ** 1.5), 14.0, ((0, 4), (1, 2), (2, 4)), jnp.float32)
    out_square = jnp.clip(jnp.exp(math.log(3.4278) - 2.779509 * jax.random.uniform(key_of[21], (EXPERTS, FF, D), jnp.float32) ** steps_of(key_of[21], (EXPERTS, FF, D), ((0, 4), (1, 2), (2, 4)), -0.2, 0.2)), 0.21276, 3.4278)
    return dict(block_input=block_input, cotangent=cotangent, routes=routes, priority=priority, norm_params=norm_params, norm_moment=norm_moment, norm_square=norm_square, qkv_weight=qkv_weight, qkv_moment=qkv_moment, qkv_square=qkv_square, attn_weight=attn_weight, attn_moment=attn_moment, attn_square=attn_square, router_weight=router_weight, router_moment=router_moment, router_square=router_square, expert_in=expert_in, in_moment=in_moment, in_square=in_square, expert_out=expert_out, out_moment=out_moment, out_square=out_square)


EPS_NORM = 1e-06
BETA_ONE = 0.9
BETA_TWO = 0.999
ADAM_EPS = 1e-08
DECAY_RATE = 0.1
PRECISE = lax.Precision.HIGHEST

@jax.custom_vjp
def low(v):
    return lax.optimization_barrier(v.astype(jnp.bfloat16)).astype(jnp.float32)

@jax.custom_vjp
def low_back(v):
    return v

def low_keep(v):
    return (low(v), None)

def low_pass(kept, grad):
    return (grad,)

def back_keep(v):
    return (v, None)

def back_low(kept, grad):
    return (low(grad),)
low.defvjp(low_keep, low_pass)
low_back.defvjp(back_keep, back_low)

def high_dot(left, right):
    return jnp.dot(left, right, precision=PRECISE)

def layer_norm(values, gain_row, bias_row):
    center = lax.optimization_barrier(jnp.mean(values, axis=-1, keepdims=True))
    shifted = values - center
    spread = lax.optimization_barrier(jnp.mean(shifted * shifted, axis=-1, keepdims=True))
    return shifted * lax.rsqrt(spread + EPS_NORM) * gain_row + bias_row

def take_rows(table, row_index):
    return table[row_index]

def group_slots(pair_ids):
    expert_ids, rank_values = pair_ids
    onehot = (expert_ids[:, None] == jnp.arange(EXPERTS, dtype=jnp.int32)[None, :]).astype(jnp.float32)
    earlier = (rank_values[None, :] < rank_values[:, None]).astype(jnp.float32)
    counts = jnp.dot(earlier, onehot, precision=PRECISE)
    return lax.optimization_barrier(jnp.sum(counts * onehot, axis=1)).astype(jnp.int32)

def invert(target):
    filler = jnp.full((EXPERTS * CAP,), 2 * ROWS, jnp.int32)
    return filler.at[target].set(jnp.arange(2 * ROWS, dtype=jnp.int32), mode='drop')

def routing_tables(routes, priority):
    expert_ids = routes.reshape(SOURCES, 2 * ROWS).astype(jnp.int32)
    slot_index = lax.map(group_slots, (expert_ids, priority.astype(jnp.int32)))
    target = jnp.where(slot_index < CAP, expert_ids * CAP + slot_index, EXPERTS * CAP).astype(jnp.int32)
    owner_pair = jax.vmap(invert)(target)
    route_hot = (routes.reshape(SOURCES, ROWS, 2, 1) == jnp.arange(EXPERTS, dtype=jnp.int32)).astype(jnp.float32)
    return (target, owner_pair, route_hot)

def attend(image_block, qkv_low, attn_low):
    block_images = image_block.shape[0]
    projected = low_back(low(jnp.einsum('isd,dcn->iscn', image_block, qkv_low, precision=PRECISE)))
    queries = projected[:, :, 0].reshape(block_images, SEQ, HEADS, HEAD_DIM)
    key_rows = projected[:, :, 1].reshape(block_images, SEQ, HEADS, HEAD_DIM)
    value_rows = projected[:, :, 2].reshape(block_images, SEQ, HEADS, HEAD_DIM)
    scores = low_back(jnp.einsum('iqhe,ikhe->ihqk', queries, key_rows, precision=PRECISE) * HEAD_DIM ** (-0.5))
    weights = low(jax.nn.softmax(scores, axis=-1))
    context = low_back(low(jnp.einsum('ihqk,ikhe->iqhe', weights, value_rows, precision=PRECISE)))
    context = context.reshape(block_images, SEQ, D)
    return low_back(jnp.einsum('isn,nd->isd', context, attn_low, precision=PRECISE))

def expert(operands):
    slot_rows, first_weight, second_weight = operands
    pre_act = low_back(high_dot(slot_rows, first_weight))
    active = low(jax.nn.gelu(pre_act, approximate=True))
    return low_back(high_dot(active, second_weight))

def block_forward(tables, inputs, norm_params, qkv_weight, attn_weight, router_weight, expert_in, expert_out):
    target, owner_pair, route_hot = tables
    normed = low(layer_norm(inputs, norm_params[0], norm_params[1]))
    qkv_low = low(qkv_weight)
    attn_low = low(attn_weight)
    checked = jax.checkpoint(attend)

    def attend_block(image_block):
        return checked(image_block, qkv_low, attn_low)
    blocks = normed.reshape(IMAGES // IMG_DEV, IMG_DEV, SEQ, D)
    attended = lax.map(attend_block, blocks).reshape(IMAGES, SEQ, D)
    hidden = inputs + attended
    normed_two = low(layer_norm(hidden, norm_params[2], norm_params[3])).reshape(SOURCES, ROWS, D)
    logits = low_back(jnp.einsum('grd,de->gre', normed_two, low(router_weight), precision=PRECISE))
    route_probs = jax.nn.softmax(logits, axis=-1)
    gate_values = lax.optimization_barrier(jnp.sum(route_probs[:, :, None, :] * route_hot, axis=-1))
    padded = jnp.concatenate([normed_two, jnp.zeros((SOURCES, 1, D), jnp.float32)], axis=1)
    dispatched = jax.vmap(take_rows)(padded, owner_pair // 2)
    by_expert = dispatched.reshape(SOURCES, EXPERTS, CAP, D).transpose(1, 0, 2, 3).reshape(EXPERTS, SOURCES * CAP, D)
    produced = lax.map(jax.checkpoint(expert), (by_expert, low(expert_in), low(expert_out)))
    produced = produced.reshape(EXPERTS, SOURCES, CAP, D).transpose(1, 0, 2, 3).reshape(SOURCES, EXPERTS * CAP, D)
    padded_out = jnp.concatenate([produced, jnp.zeros((SOURCES, 1, D), jnp.float32)], axis=1)
    per_pair = jax.vmap(take_rows)(padded_out, target).reshape(SOURCES, ROWS, 2, D)
    combined = lax.optimization_barrier(jnp.sum(gate_values[:, :, :, None] * per_pair, axis=2))
    return hidden + combined.reshape(IMAGES, SEQ, D)

def adam_update(weight, gradient, moment, square, step_rate, decay_rate):
    moment_new = BETA_ONE * moment + (1.0 - BETA_ONE) * gradient
    square_new = BETA_TWO * square + (1.0 - BETA_TWO) * gradient * gradient
    first_hat = moment_new / (1.0 - BETA_ONE ** STEP)
    second_hat = square_new / (1.0 - BETA_TWO ** STEP)
    weight_new = weight - step_rate * (first_hat / (jnp.sqrt(second_hat) + ADAM_EPS) + decay_rate * weight)
    return (weight_new, moment_new, square_new)

def reference(block_input, cotangent, routes, priority, norm_params, norm_moment, norm_square, qkv_weight, qkv_moment, qkv_square, attn_weight, attn_moment, attn_square, router_weight, router_moment, router_square, expert_in, in_moment, in_square, expert_out, out_moment, out_square):
    tables = routing_tables(routes, priority)
    inputs = block_input.astype(jnp.float32)
    result, pullback = jax.vjp(partial(block_forward, tables), inputs, norm_params, qkv_weight, attn_weight, router_weight, expert_in, expert_out)
    gradients = pullback(cotangent.astype(jnp.float32))
    norm_new = adam_update(norm_params, gradients[1], norm_moment, norm_square, 0.25, 0.0)
    qkv_new = adam_update(qkv_weight, gradients[2], qkv_moment, qkv_square, 1.3 * D ** (-0.5), DECAY_RATE)
    attn_new = adam_update(attn_weight, gradients[3], attn_moment, attn_square, 3.0 * D ** (-0.5), DECAY_RATE)
    router_new = adam_update(router_weight, gradients[4], router_moment, router_square, 0.75 * D ** (-0.5), DECAY_RATE)
    in_new = adam_update(expert_in, gradients[5], in_moment, in_square, 1.0 * D ** (-0.5), DECAY_RATE)
    out_new = adam_update(expert_out, gradients[6], out_moment, out_square, 0.8 * EXPERTS * FF ** (-0.5), DECAY_RATE)
    return (result.astype(jnp.bfloat16), gradients[0], norm_new[0], norm_new[1], norm_new[2], qkv_new[0], qkv_new[1], qkv_new[2], attn_new[0], attn_new[1], attn_new[2], router_new[0], router_new[1], router_new[2], in_new[0], in_new[1], in_new[2], out_new[0], out_new[1], out_new[2])
```

```python
from functools import partial

import jax
import jax.numpy as jnp
from jax import lax
from jax.experimental import pallas as pl
from jax.experimental.pallas import tpu as pltpu
from jax.sharding import PartitionSpec as P

HEAD_DIM = 64
FF = 2048
STEP = 10


EPS_NORM = 1e-06
BETA_ONE = 0.9
BETA_TWO = 0.999
ADAM_EPS = 1e-08
DECAY_RATE = 0.1


def norm_forward(values, gain_row, bias_row):
    center = jnp.mean(values, axis=-1, keepdims=True)
    shifted = values - center
    inverse = lax.rsqrt(jnp.mean(shifted * shifted, axis=-1, keepdims=True) + EPS_NORM)
    unit_rows = shifted * inverse
    return (unit_rows * gain_row + bias_row, unit_rows, inverse)


def norm_backward(grad_rows, unit_rows, inverse, gain_row):
    scaled = grad_rows * gain_row
    inner_grad = (
        scaled
        - jnp.mean(scaled, axis=-1, keepdims=True)
        - unit_rows * jnp.mean(scaled * unit_rows, axis=-1, keepdims=True)
    )
    return (
        inner_grad * inverse,
        jnp.sum(grad_rows * unit_rows, axis=0),
        jnp.sum(grad_rows, axis=0),
    )


def gelu_grad(pre_act, upstream):
    result, pullback = jax.vjp(partial(jax.nn.gelu, approximate=True), pre_act)
    return pullback(upstream)[0]


def adam_update(weight, gradient, moment, square, step_rate, decay_rate):
    moment_new = BETA_ONE * moment + (1.0 - BETA_ONE) * gradient
    square_new = BETA_TWO * square + (1.0 - BETA_TWO) * gradient * gradient
    first_hat = moment_new / (1.0 - BETA_ONE**STEP)
    second_hat = square_new / (1.0 - BETA_TWO**STEP)
    weight_new = weight - step_rate * (
        first_hat / (jnp.sqrt(second_hat) + ADAM_EPS) + decay_rate * weight
    )
    return (weight_new, moment_new, square_new)


def send_rows(parcel):
    copies = jnp.broadcast_to(
        parcel[:, None], (parcel.shape[0], lax.axis_size("tensor")) + parcel.shape[1:]
    )
    flat_copies = copies.reshape((-1,) + parcel.shape[1:])
    arrived = lax.all_to_all(
        flat_copies, ("shard", "tensor"), split_axis=0, concat_axis=0, tiled=True
    )
    return arrived.reshape(copies.shape)


def return_rows(partial_rows):
    flat_rows = partial_rows.reshape((-1,) + partial_rows.shape[2:])
    arrived = lax.all_to_all(
        flat_rows.astype(jnp.bfloat16), ("shard", "tensor"), split_axis=0, concat_axis=0, tiled=True
    ).astype(flat_rows.dtype)
    return jnp.sum(arrived.reshape(partial_rows.shape), axis=1)


def slot_plan(
    block_input,
    cotangent,
    routes,
    priority,
    norm_params,
    norm_moment,
    norm_square,
    qkv_weight,
    qkv_moment,
    qkv_square,
    attn_weight,
    attn_moment,
    attn_square,
    router_weight,
    router_moment,
    router_square,
    expert_in,
    in_moment,
    in_square,
    expert_out,
    out_moment,
    out_square,
):
    images, length, model_width = block_input.shape
    row_count = images * length
    local_experts = expert_in.shape[0]
    shards = lax.axis_size("shard")
    experts = local_experts * shards
    capacity = 9 * row_count // (4 * experts)
    score_scale = HEAD_DIM ** (-0.5)
    full_qkv, full_attn = (
        lax.all_gather(qkv_weight.astype(jnp.bfloat16), ("shard", "tensor"), axis=0, tiled=True),
        lax.all_gather(attn_weight.astype(jnp.bfloat16), ("shard", "tensor"), axis=1, tiled=True),
    )
    inputs = block_input.astype(jnp.float32).reshape(row_count, model_width)
    normed, unit_one, inverse_one = norm_forward(inputs, norm_params[0], norm_params[1])
    normed_low = normed.astype(jnp.bfloat16).reshape(images, length, model_width)
    gathered, hidden_in, hidden_out = (
        lax.all_gather(normed_low, "head", axis=0, tiled=True),
        lax.all_gather(expert_in.astype(jnp.bfloat16), "head", axis=1, tiled=True),
        lax.all_gather(expert_out.astype(jnp.bfloat16), "head", axis=2, tiled=True),
    )
    local_heads = full_qkv.shape[2] // HEAD_DIM
    all_images = gathered.shape[0]
    head_shape = (all_images, length, local_heads, HEAD_DIM)
    projected = jnp.einsum(
        "isd,dcn->iscn", gathered, full_qkv, preferred_element_type=jnp.float32
    ).astype(jnp.bfloat16)
    queries = projected[:, :, 0].reshape(head_shape)
    key_rows = projected[:, :, 1].reshape(head_shape)
    value_rows = projected[:, :, 2].reshape(head_shape)
    scores = (
        jnp.einsum("iqhe,ikhe->ihqk", queries, key_rows, preferred_element_type=jnp.float32)
        * score_scale
    )
    score_top = jnp.max(scores, axis=-1, keepdims=True)
    log_total = score_top + jnp.log(jnp.sum(jnp.exp(scores - score_top), axis=-1, keepdims=True))
    probs_low = jnp.exp(scores - log_total).astype(jnp.bfloat16)
    context = jnp.einsum(
        "ihqk,ikhe->iqhe", probs_low, value_rows, preferred_element_type=jnp.float32
    ).astype(jnp.bfloat16)
    context = context.reshape(all_images * length, local_heads * HEAD_DIM)
    attended = lax.psum_scatter(
        jnp.dot(context, full_attn, preferred_element_type=jnp.float32).astype(jnp.bfloat16),
        "head",
        scatter_dimension=0,
        tiled=True,
    ).astype(jnp.float32)
    hidden = inputs + attended
    normed_two, unit_two, inverse_two = norm_forward(hidden, norm_params[2], norm_params[3])
    second_low = normed_two.astype(jnp.bfloat16)
    router_low = router_weight.astype(jnp.bfloat16)
    logits = jnp.dot(second_low, router_low, preferred_element_type=jnp.float32)
    route_probs = jax.nn.softmax(logits, axis=-1)
    route_hot = (
        routes.reshape(row_count, 2)[:, :, None]
        == jnp.arange(experts, dtype=jnp.int32)[None, None, :]
    ).astype(jnp.float32)
    gate_values = jnp.sum(route_probs[:, None, :] * route_hot, axis=-1)
    expert_ids = routes.reshape(2 * row_count)
    rank_values = priority[0]
    pair_hot = route_hot.reshape(2 * row_count, experts)
    earlier = (rank_values[None, :] < rank_values[:, None]).astype(jnp.bfloat16)
    counts = jnp.dot(earlier, pair_hot.astype(jnp.bfloat16), preferred_element_type=jnp.float32)
    slot_index = jnp.sum(counts * pair_hot, axis=1).astype(jnp.int32)
    target = jnp.where(
        slot_index < capacity, expert_ids * capacity + slot_index, experts * capacity
    )
    filler = jnp.full((experts * capacity,), 2 * row_count, jnp.int32)
    owner_pair = filler.at[target].set(jnp.arange(2 * row_count, dtype=jnp.int32), mode="drop")
    padded = jnp.concatenate([second_low, jnp.zeros((1, model_width), jnp.bfloat16)], axis=0)
    parcel = padded[owner_pair // 2].reshape(shards, local_experts, capacity, model_width)
    arrived = send_rows(parcel)
    pre_act = jnp.einsum("stecd,edf->stecf", arrived, hidden_in, preferred_element_type=jnp.float32)
    active = jax.nn.gelu(pre_act, approximate=True).astype(jnp.bfloat16)
    part_rows = jnp.einsum(
        "stecf,efd->stecd", active, hidden_out, preferred_element_type=jnp.float32
    )
    expert_rows = return_rows(part_rows).reshape(experts * capacity, model_width)
    padded_out = jnp.concatenate([expert_rows, jnp.zeros((1, model_width), jnp.float32)], axis=0)
    per_pair = padded_out[target].reshape(row_count, 2, model_width)
    block_sum = hidden + jnp.sum(gate_values[:, :, None] * per_pair, axis=1)
    block_output = block_sum.astype(jnp.bfloat16).reshape(images, length, model_width)
    upstream = cotangent.astype(jnp.float32).reshape(row_count, model_width)
    pair_grad = (
        (gate_values[:, :, None] * upstream[:, None, :])
        .astype(jnp.bfloat16)
        .reshape(2 * row_count, model_width)
    )
    gate_grad = jnp.sum(upstream[:, None, :] * per_pair, axis=-1)
    padded_grad = jnp.concatenate([pair_grad, jnp.zeros((1, model_width), jnp.bfloat16)], axis=0)
    grad_parcel = padded_grad[owner_pair].reshape(shards, local_experts, capacity, model_width)
    grad_arrived = send_rows(grad_parcel)
    grad_out_part = jnp.einsum(
        "stecf,stecd->efd", active, grad_arrived, preferred_element_type=jnp.float32
    )
    active_grad = jnp.einsum(
        "stecd,efd->stecf", grad_arrived, hidden_out, preferred_element_type=jnp.float32
    )
    pre_grad = gelu_grad(pre_act, active_grad).astype(jnp.bfloat16)
    grad_in_part = jnp.einsum(
        "stecd,stecf->edf", arrived, pre_grad, preferred_element_type=jnp.float32
    )
    row_grad = jnp.einsum(
        "stecf,edf->stecd", pre_grad, hidden_in, preferred_element_type=jnp.float32
    )
    slot_grad = return_rows(row_grad).reshape(experts * capacity, model_width)
    padded_slot = jnp.concatenate([slot_grad, jnp.zeros((1, model_width), jnp.float32)], axis=0)
    second_grad = jnp.sum(padded_slot[target].reshape(row_count, 2, model_width), axis=1)
    prob_sum = jnp.sum(gate_grad[:, :, None] * route_hot, axis=1)
    logit_grad = (
        route_probs * (prob_sum - jnp.sum(route_probs * prob_sum, axis=-1, keepdims=True))
    ).astype(jnp.bfloat16)
    router_grad = jnp.einsum(
        "rd,re->de", second_low, logit_grad, preferred_element_type=jnp.float32
    )
    second_grad = second_grad + jnp.einsum(
        "re,de->rd", logit_grad, router_low, preferred_element_type=jnp.float32
    )
    hidden_part, gain_two, bias_two = norm_backward(
        second_grad, unit_two, inverse_two, norm_params[2]
    )
    hidden_grad = upstream + hidden_part
    attended_grad = lax.all_gather(hidden_grad.astype(jnp.bfloat16), "head", axis=0, tiled=True)
    attn_grad = jnp.einsum("rn,rd->nd", context, attended_grad, preferred_element_type=jnp.float32)
    context_grad = jnp.einsum(
        "rd,nd->rn", attended_grad, full_attn, preferred_element_type=jnp.float32
    ).astype(jnp.bfloat16)
    context_grad = context_grad.reshape(head_shape)
    scores_again = (
        jnp.einsum("iqhe,ikhe->ihqk", queries, key_rows, preferred_element_type=jnp.float32)
        * score_scale
    )
    probs_full = jnp.exp(scores_again - log_total)
    prob_grad = jnp.einsum(
        "iqhe,ikhe->ihqk", context_grad, value_rows, preferred_element_type=jnp.float32
    )
    score_grad = (
        probs_full * (prob_grad - jnp.sum(probs_full * prob_grad, axis=-1, keepdims=True))
    ).astype(jnp.bfloat16)
    query_grad = (
        jnp.einsum("ihqk,ikhe->iqhe", score_grad, key_rows, preferred_element_type=jnp.float32)
        * score_scale
    )
    key_grad = (
        jnp.einsum("ihqk,iqhe->ikhe", score_grad, queries, preferred_element_type=jnp.float32)
        * score_scale
    )
    value_grad = jnp.einsum(
        "ihqk,iqhe->ikhe", probs_low, context_grad, preferred_element_type=jnp.float32
    )
    projected_grad = (
        jnp.stack([query_grad, key_grad, value_grad], axis=2)
        .reshape(all_images, length, 3, local_heads * HEAD_DIM)
        .astype(jnp.bfloat16)
    )
    qkv_grad = jnp.einsum(
        "isd,iscn->dcn", gathered, projected_grad, preferred_element_type=jnp.float32
    )
    normed_part = jnp.einsum(
        "iscn,dcn->isd", projected_grad, full_qkv, preferred_element_type=jnp.float32
    )
    normed_grad, in_grad, out_grad = (
        lax.psum_scatter(
            normed_part.astype(jnp.bfloat16), "head", scatter_dimension=0, tiled=True
        ).astype(jnp.float32),
        lax.psum_scatter(
            grad_in_part.astype(jnp.bfloat16), "head", scatter_dimension=1, tiled=True
        ).astype(jnp.float32),
        lax.psum_scatter(
            grad_out_part.astype(jnp.bfloat16), "head", scatter_dimension=2, tiled=True
        ).astype(jnp.float32),
    )
    input_part, gain_one, bias_one = norm_backward(
        normed_grad.reshape(row_count, model_width), unit_one, inverse_one, norm_params[0]
    )
    input_grad = (hidden_grad + input_part).reshape(images, length, model_width)
    norm_grad = jnp.stack([gain_one, bias_one, gain_two, bias_two])
    norm_grad, router_grad = lax.psum((norm_grad, router_grad), ("shard", "head", "tensor"))
    qkv_grad, attn_grad = (
        lax.psum_scatter(qkv_grad, ("shard", "tensor"), scatter_dimension=0, tiled=True),
        lax.psum_scatter(attn_grad, ("shard", "tensor"), scatter_dimension=1, tiled=True),
    )
    norm_new = adam_update(norm_params, norm_grad, norm_moment, norm_square, 0.25, 0.0)
    qkv_new = adam_update(
        qkv_weight, qkv_grad, qkv_moment, qkv_square, 1.3 * model_width ** (-0.5), DECAY_RATE
    )
    attn_new = adam_update(
        attn_weight, attn_grad, attn_moment, attn_square, 3.0 * model_width ** (-0.5), DECAY_RATE
    )
    router_new = adam_update(
        router_weight,
        router_grad,
        router_moment,
        router_square,
        0.75 * model_width ** (-0.5),
        DECAY_RATE,
    )
    in_new = adam_update(
        expert_in, in_grad, in_moment, in_square, 1.0 * model_width ** (-0.5), DECAY_RATE
    )
    out_new = adam_update(
        expert_out, out_grad, out_moment, out_square, 0.8 * experts * FF ** (-0.5), DECAY_RATE
    )
    return (
        block_output,
        input_grad,
        norm_new[0],
        norm_new[1],
        norm_new[2],
        qkv_new[0],
        qkv_new[1],
        qkv_new[2],
        attn_new[0],
        attn_new[1],
        attn_new[2],
        router_new[0],
        router_new[1],
        router_new[2],
        in_new[0],
        in_new[1],
        in_new[2],
        out_new[0],
        out_new[1],
        out_new[2],
    )


PAD = 208
SLOT_PAD = 16


def kernel_params(megabytes):
    return pltpu.CompilerParams(vmem_limit_bytes=megabytes << 20)


def cost(flops, moved):
    return pl.CostEstimate(flops=int(flops), bytes_accessed=int(moved), transcendentals=0)


def mm(left, right):
    return lax.dot_general(left, right, (((1,), (0,)), ((), ())), preferred_element_type=jnp.float32)


def mm_turned(left, right):
    return lax.dot_general(left, right, (((1,), (1,)), ((), ())), preferred_element_type=jnp.float32)


def mm_rows(left, right):
    return lax.dot_general(left, right, (((0,), (0,)), ((), ())), preferred_element_type=jnp.float32)


def unit_of(values):
    center = jnp.mean(values, axis=-1, keepdims=True)
    shifted = values - center
    inverse = lax.rsqrt(jnp.mean(shifted * shifted, axis=-1, keepdims=True) + EPS_NORM)
    return (shifted * inverse, inverse)


def unit_backward(grad_rows, unit_rows, inverse, gain_row):
    scaled = grad_rows * gain_row
    inner_grad = (
        scaled
        - jnp.mean(scaled, axis=-1, keepdims=True)
        - unit_rows * jnp.mean(scaled * unit_rows, axis=-1, keepdims=True)
    )
    return inner_grad * inverse


def slot_kernel(experts, capacity, row_ref, column_ref, slot_row_ref, slot_column_ref):
    none = 1 << 20
    tokens = row_ref.shape[1]
    lanes = lax.broadcasted_iota(jnp.int32, (PAD, 128), 1)
    rows_of = lax.broadcasted_iota(jnp.int32, (8, tokens), 0)

    def ranks(named, rank, expert):
        return jnp.where(
            named[0] == expert, rank[0], jnp.where(named[1] == expert, rank[1], none)
        )

    routes_row, ranks_row = (row_ref[0:1], row_ref[1:2]), (row_ref[2:3], row_ref[3:4])
    all_rows = jnp.full((8, tokens), -1, jnp.int32)
    row_of = [ranks(routes_row, ranks_row, e) for e in range(experts)]
    totals = [jnp.zeros((1, tokens), jnp.float32) for e in range(experts)]
    for block in range(tokens // PAD):
        part = column_ref[block * PAD : (block + 1) * PAD]
        routes_col, ranks_col = (part[:, 0:1], part[:, 1:2]), (part[:, 2:3], part[:, 3:4])
        result = jnp.full((PAD, 128), -1, jnp.int32)
        for e in range(experts):
            column = ranks(routes_col, ranks_col, e)
            totals[e] = totals[e] + jnp.sum(
                jnp.where(column < row_of[e], 1.0, 0.0), axis=0, keepdims=True
            )
            before = jnp.sum(
                jnp.where(row_of[e] < column, 1.0, 0.0), axis=1, keepdims=True
            ).astype(jnp.int32)
            slot = jnp.where((column < none) & (before < capacity), before, -1)
            result = jnp.where(lanes == e, slot, result)
        slot_column_ref[block * PAD : (block + 1) * PAD] = result
    for e in range(experts):
        before = totals[e].astype(jnp.int32)
        slot = jnp.where((row_of[e] < none) & (before < capacity), before, -1)
        all_rows = jnp.where(rows_of == e, slot, all_rows)
    slot_row_ref[...] = all_rows


def find_slots(routes, priority, experts, capacity):
    images, length, _ = routes.shape
    tokens = images * PAD
    table = jnp.concatenate([routes, priority.reshape(images, length, 2)], axis=2)
    table = jnp.pad(table, ((0, 0), (0, PAD - length), (0, 0)), constant_values=-1)
    table = table.reshape(tokens, 4)
    columns = jnp.pad(table, ((0, 0), (0, 4)))
    return pl.pallas_call(
        partial(slot_kernel, experts, capacity),
        out_shape=(
            jax.ShapeDtypeStruct((8, tokens), jnp.int32),
            jax.ShapeDtypeStruct((tokens, 128), jnp.int32),
        ),
        compiler_params=kernel_params(32),
        cost_estimate=cost(1e10, 1e6),
        name="find_slots",
    )(columns.T, columns)


def dense_kernel(place_ref, pieces_ref, full_ref, sems):
    count, kinds, rows, columns = pieces_ref.shape
    across = full_ref.shape[2] // columns
    copies = []
    for piece in range(count):
        down, over = piece // across, piece % across
        copies.append(
            pltpu.make_async_copy(
                pieces_ref.at[place_ref[piece]],
                full_ref.at[:, down * rows : (down + 1) * rows, over * columns : (over + 1) * columns],
                sems.at[piece],
            )
        )
    for copy in copies:
        copy.start()
    for copy in copies:
        copy.wait()


def join_dense(places, pieces, model_width):
    count, kinds = pieces.shape[:2]
    return pl.pallas_call(
        dense_kernel,
        out_shape=jax.ShapeDtypeStruct((kinds, model_width, model_width), pieces.dtype),
        in_specs=[pl.BlockSpec(memory_space=pltpu.SMEM), pl.BlockSpec(memory_space=pl.ANY)],
        out_specs=pl.BlockSpec(memory_space=pltpu.VMEM),
        scratch_shapes=[pltpu.SemaphoreType.DMA((count,))],
        compiler_params=kernel_params(16),
        cost_estimate=cost(1e6, 4e6),
        name="join_dense",
    )(places, pieces)


def attend_kernel(
    length, experts, input_ref, norm_ref, dense_ref, router_ref,
    normed_ref, projected_ref, probs_ref, context_ref, hidden_ref, second_ref, route_ref,
):
    low = jnp.bfloat16
    values = input_ref[0].astype(jnp.float32)
    width = values.shape[1]
    unit, _ = unit_of(values)
    normed = (unit * norm_ref[0:1] + norm_ref[1:2]).astype(low)
    normed_ref[0] = normed
    queries, key_rows, value_rows = (mm(normed, dense_ref[c]).astype(low) for c in range(3))
    projected_ref[0, 0] = queries
    projected_ref[0, 1] = key_rows
    projected_ref[0, 2] = value_rows
    first_half = lax.broadcasted_iota(jnp.int32, (PAD, 2 * HEAD_DIM), 1) < HEAD_DIM
    is_key = lax.broadcasted_iota(jnp.int32, (PAD, PAD), 1) < length
    zero = jnp.zeros((PAD, 2 * HEAD_DIM), low)
    pairs = []
    for pair in range(width // (2 * HEAD_DIM)):
        at = slice(pair * 2 * HEAD_DIM, (pair + 1) * 2 * HEAD_DIM)
        query, key, value = queries[:, at], key_rows[:, at], value_rows[:, at]
        halves = []
        for side in range(2):
            mine = jnp.where(first_half == (side == 0), query, zero)
            scores = mm_turned(mine, key) * (HEAD_DIM ** (-0.5))
            scores = jnp.where(is_key, scores, -1e30)
            top = jnp.max(scores, axis=-1, keepdims=True)
            raised = jnp.exp(scores - top)
            probs = (raised / jnp.sum(raised, axis=-1, keepdims=True)).astype(low)
            probs_ref[0, 2 * pair + side] = probs
            halves.append(mm(probs, value))
        pairs.append(jnp.where(first_half, halves[0], halves[1]).astype(low))
    context = jnp.concatenate(pairs, axis=1)
    context_ref[0] = context
    hidden = values + mm_turned(context, dense_ref[3])
    hidden_ref[0] = hidden
    unit, _ = unit_of(hidden)
    second = (unit * norm_ref[2:3] + norm_ref[3:4]).astype(low)
    second_ref[0] = second
    logits = mm(second, router_ref[...])
    is_expert = lax.broadcasted_iota(jnp.int32, logits.shape, 1) < experts
    logits = jnp.where(is_expert, logits, -1e30)
    raised = jnp.exp(logits - jnp.max(logits, axis=-1, keepdims=True))
    route_ref[0] = raised / jnp.sum(raised, axis=-1, keepdims=True)


def attend(length, experts, padded, norm_params, dense, router_wide):
    images, _, width = padded.shape
    heads = width // HEAD_DIM
    low, wide = jnp.bfloat16, jnp.float32

    def per_image(*shape):
        return pl.BlockSpec((1,) + shape, lambda i: (i,) + (0,) * len(shape))

    def whole(array):
        return pl.BlockSpec(array.shape, lambda i: (0,) * array.ndim)

    shapes = [
        ((PAD, width), low), ((3, PAD, width), low), ((heads, PAD, PAD), low), ((PAD, width), low),
        ((PAD, width), wide), ((PAD, width), low), ((PAD, 128), wide),
    ]
    return pl.pallas_call(
        partial(attend_kernel, length, experts),
        grid=(images,),
        in_specs=[per_image(PAD, width), whole(norm_params), whole(dense), whole(router_wide)],
        out_specs=[per_image(*s) for s, _ in shapes],
        out_shape=[jax.ShapeDtypeStruct((images,) + s, t) for s, t in shapes],
        compiler_params=kernel_params(48),
        cost_estimate=cost(images * 2.5e9, images * 5e6),
        name="attend",
    )(padded, norm_params, dense, router_wide)


def dispatch_kernel(slot_ref, second_ref, upstream_ref, route_ref, x_ref, g_ref, xt_ref, gt_ref):
    low = jnp.bfloat16
    expert = pl.program_id(0)
    slots, tokens = x_ref.shape[1], second_ref.shape[0]
    rows_of = lax.broadcasted_iota(jnp.int32, (8, tokens), 0)
    slot_row = jnp.max(jnp.where(rows_of == expert, slot_ref[...], -1), axis=0, keepdims=True)
    hot = lax.broadcasted_iota(jnp.int32, (slots, tokens), 0) == slot_row
    hot = jnp.where(hot, 1.0, 0.0).astype(low)
    lanes = lax.broadcasted_iota(jnp.int32, (tokens, 128), 1)
    gate = jnp.sum(jnp.where(lanes == expert, route_ref[...], 0.0), axis=1, keepdims=True)
    pair_grad = (gate * upstream_ref[...].astype(jnp.float32)).astype(low)
    rows = mm(hot, second_ref[...]).astype(low)
    x_ref[0] = rows
    xt_ref[0] = rows.T
    rows = mm(hot, pair_grad).astype(low)
    g_ref[0] = rows
    gt_ref[0] = rows.T


def dispatch(slot_row, second, upstream, route_probs, experts, slots):
    tokens, width = second.shape

    def whole(array):
        return pl.BlockSpec(array.shape, lambda e: (0,) * array.ndim)

    flat = pl.BlockSpec((1, slots, width), lambda e: (e, 0, 0))
    turned = pl.BlockSpec((1, width, slots), lambda e: (e, 0, 0))
    low = jnp.bfloat16
    return pl.pallas_call(
        dispatch_kernel,
        grid=(experts,),
        in_specs=[whole(a) for a in (slot_row, second, upstream, route_probs)],
        out_specs=[flat, flat, turned, turned],
        out_shape=[jax.ShapeDtypeStruct((experts, slots, width), low)] * 2
        + [jax.ShapeDtypeStruct((experts, width, slots), low)] * 2,
        compiler_params=kernel_params(48),
        cost_estimate=cost(4 * slots * tokens * width * experts, 1e7),
        name="dispatch",
    )(slot_row, second, upstream, route_probs)


def expert_kernel(first, last, place_ref, x_ref, g_ref, xt_ref, gt_ref, *refs):
    low = jnp.bfloat16
    if first:
        weights_ref, made_ref, back_ref, grads_ref = refs[:4]
        rest = refs[4:]
    else:
        made_in, back_in, weights_ref, made_ref, back_ref, grads_ref = refs[:6]
        rest = refs[6:]
    held, sent, made_sum, back_sum, in_sems, out_sems = rest
    expert, experts = pl.program_id(0), pl.num_programs(0)
    parts = place_ref.shape[1]
    _, kinds, rows, columns = weights_ref.shape
    down = held.shape[2] // rows

    def window(ref, slot, part):
        tensor, head = part // down, part % down
        return ref.at[
            slot, :, head * rows : (head + 1) * rows, tensor * columns : (tensor + 1) * columns
        ]

    def fetch(which, slot, part):
        return pltpu.make_async_copy(
            weights_ref.at[place_ref[which, part]], window(held, slot, part), in_sems.at[slot, part]
        )

    def put(which, slot, part):
        return pltpu.make_async_copy(
            window(sent, slot, part), grads_ref.at[place_ref[which, part]], out_sems.at[slot, part]
        )

    slot = lax.rem(expert, 2)

    @pl.when(expert == 0)
    def _():
        for part in range(parts):
            fetch(0, 0, part).start()

    @pl.when(expert + 1 < experts)
    def _():
        for part in range(parts):
            fetch(expert + 1, 1 - slot, part).start()

    for part in range(parts):
        fetch(expert, slot, part).wait()

    @pl.when(expert >= 2)
    def _():
        for part in range(parts):
            put(expert - 2, slot, part).wait()

    x, g, xt, gt = x_ref[0], g_ref[0], xt_ref[0], gt_ref[0]
    units = held.shape[3]
    tile = 256
    for unit in range(0, units, tile):
        at = slice(unit, unit + tile)
        w_in, w_out = held[slot, 0, :, at], held[slot, 1, :, at]
        v = mm(x, w_in)
        grad = mm(g, w_out)
        square = v * v
        tanh = jnp.tanh(v * (0.7978845608028654 + 0.035677408136300125 * square))
        half = 0.5 + 0.5 * tanh
        active = (v * half).astype(low)
        slope = half + v * (half * (1.0 - tanh)) * (
            0.7978845608028654 + 0.10703222440890037 * square
        )
        pre_grad = (grad * slope).astype(low)
        made = mm_turned(active, w_out)
        back = mm_turned(pre_grad, w_in)
        if unit == 0:
            made_sum[...] = made
            back_sum[...] = back
        else:
            made_sum[...] += made
            back_sum[...] += back
        sent[slot, 0, :, at] = mm(xt, pre_grad).astype(low)
        sent[slot, 1, :, at] = mm(gt, active).astype(low)
    made, back = made_sum[...], back_sum[...]
    if not first:
        made, back = made + made_in[0], back + back_in[0]
    made_ref[0] = made.astype(made_ref.dtype)
    back_ref[0] = back.astype(back_ref.dtype)
    for part in range(parts):
        put(expert, slot, part).start()

    @pl.when(expert == experts - 1)
    def _():
        for part in range(parts):
            put(expert - 1, 1 - slot, part).wait()
        for part in range(parts):
            put(expert, slot, part).wait()


def run_experts(places, x, g, xt, gt, sums, weights, last):
    experts, slots, width = x.shape
    pieces, kinds, rows, columns = weights.shape
    parts = places.shape[1]
    units = parts * rows * columns // width
    low = jnp.bfloat16
    flat = pl.BlockSpec((1, slots, width), lambda e: (e, 0, 0))
    turned = pl.BlockSpec((1, width, slots), lambda e: (e, 0, 0))
    anywhere = pl.BlockSpec(memory_space=pl.ANY)
    kept = low if last else jnp.float32
    first = sums is None
    given = () if first else tuple(sums)
    return pl.pallas_call(
        partial(expert_kernel, first, last),
        grid=(experts,),
        in_specs=[pl.BlockSpec(memory_space=pltpu.SMEM), flat, flat, turned, turned]
        + [flat] * len(given)
        + [anywhere],
        out_specs=[flat, flat, anywhere],
        out_shape=[jax.ShapeDtypeStruct((experts, slots, width), kept)] * 2
        + [jax.ShapeDtypeStruct(weights.shape, low)],
        scratch_shapes=[
            pltpu.VMEM((2, kinds, width, units), low),
            pltpu.VMEM((2, kinds, width, units), low),
            pltpu.VMEM((slots, width), jnp.float32),
            pltpu.VMEM((slots, width), jnp.float32),
            pltpu.SemaphoreType.DMA((2, parts)),
            pltpu.SemaphoreType.DMA((2, parts)),
        ],
        compiler_params=kernel_params(56),
        cost_estimate=cost(12 * experts * slots * width * units, 3e7),
        name="experts",
    )(places, x, g, xt, gt, *given, weights)


def combine_kernel(
    experts, slot_ref, made_ref, back_ref, hidden_ref, upstream_ref, second_ref, route_ref,
    norm_ref, router_ref, output_ref, grad_ref, router_grad_ref, norm_grad_ref,
):
    low = jnp.bfloat16
    image = pl.program_id(0)
    hidden = hidden_ref[0]
    upstream = upstream_ref[0].astype(jnp.float32)
    route_probs = route_ref[0]
    slots = made_ref.shape[1]
    lanes = lax.broadcasted_iota(jnp.int32, (PAD, slots), 1)
    wide_lanes = lax.broadcasted_iota(jnp.int32, (PAD, 128), 1)
    total = hidden
    second_grad = jnp.zeros_like(hidden)
    prob_sum = jnp.zeros((PAD, 128), jnp.float32)
    for e in range(experts):
        hot = jnp.where(lanes == slot_ref[0][:, e : e + 1], 1.0, 0.0).astype(low)
        made = mm(hot, made_ref[e])
        second_grad = second_grad + mm(hot, back_ref[e])
        total = total + route_probs[:, e : e + 1] * made
        gate_grad = jnp.sum(upstream * made, axis=-1, keepdims=True)
        prob_sum = jnp.where(wide_lanes == e, gate_grad, prob_sum)
    length = output_ref.shape[1]
    output_ref[0] = total.astype(low)[:length]
    inner = jnp.sum(route_probs * prob_sum, axis=-1, keepdims=True)
    logit_grad = (route_probs * (prob_sum - inner)).astype(low)
    second_grad = second_grad + mm_turned(logit_grad, router_ref[...])
    unit, inverse = unit_of(hidden)
    grad_ref[0] = upstream + unit_backward(second_grad, unit, inverse, norm_ref[2:3])
    router_grad = mm_rows(logit_grad, second_ref[0])[:8]
    gain = jnp.sum(second_grad * unit, axis=0, keepdims=True)
    bias = jnp.sum(second_grad, axis=0, keepdims=True)
    rows_of = lax.broadcasted_iota(jnp.int32, (8, hidden.shape[1]), 0)
    norm_grad = jnp.where(rows_of == 2, gain, jnp.where(rows_of == 3, bias, 0.0))

    @pl.when(image == 0)
    def _():
        router_grad_ref[...] = router_grad
        norm_grad_ref[...] = norm_grad

    @pl.when(image > 0)
    def _():
        router_grad_ref[...] += router_grad
        norm_grad_ref[...] += norm_grad


def combine(length, experts, slot_column, made, back, hidden, upstream, second, route_probs, norm_params, router_wide):
    images, _, width = hidden.shape
    low, wide = jnp.bfloat16, jnp.float32

    def per_image(*shape):
        return pl.BlockSpec((1,) + shape, lambda i: (i,) + (0,) * len(shape))

    def whole(array):
        return pl.BlockSpec(array.shape, lambda i: (0,) * array.ndim)

    small = pl.BlockSpec((8, width), lambda i: (0, 0))
    return pl.pallas_call(
        partial(combine_kernel, experts),
        grid=(images,),
        in_specs=[
            per_image(PAD, 128), whole(made), whole(back), per_image(PAD, width), per_image(PAD, width),
            per_image(PAD, width), per_image(PAD, 128), whole(norm_params), whole(router_wide),
        ],
        out_specs=[per_image(length, width), per_image(PAD, width), small, small],
        out_shape=[
            jax.ShapeDtypeStruct((images, length, width), low),
            jax.ShapeDtypeStruct((images, PAD, width), wide),
            jax.ShapeDtypeStruct((8, width), wide),
            jax.ShapeDtypeStruct((8, width), wide),
        ],
        compiler_params=kernel_params(48),
        cost_estimate=cost(4 * images * PAD * experts * made.shape[1] * width, 2e7),
        name="combine",
    )(slot_column, made, back, hidden, upstream, second, route_probs, norm_params, router_wide)


def attend_back_kernel(
    place_ref, input_ref, norm_ref, dense_ref, normed_ref, projected_ref, probs_ref, context_ref, grad_ref,
    input_grad_ref, norm_grad_ref, pieces_ref, sums, low_sums, sems,
):
    low = jnp.bfloat16
    image, images = pl.program_id(0), pl.num_programs(0)

    @pl.when(image == 0)
    def _():
        sums[...] = jnp.zeros_like(sums)
        norm_grad_ref[...] = jnp.zeros_like(norm_grad_ref)

    hidden_grad = grad_ref[0]
    width = hidden_grad.shape[1]
    attended_low = hidden_grad.astype(low)
    context_grad = mm(attended_low, dense_ref[3]).astype(low)
    sums[3] += mm_rows(attended_low, context_ref[0])
    queries, key_rows, value_rows = projected_ref[0, 0], projected_ref[0, 1], projected_ref[0, 2]
    first_half = lax.broadcasted_iota(jnp.int32, (PAD, 2 * HEAD_DIM), 1) < HEAD_DIM
    zero = jnp.zeros((PAD, 2 * HEAD_DIM), low)
    scale = HEAD_DIM ** (-0.5)
    parts = [[], [], []]
    for pair in range(width // (2 * HEAD_DIM)):
        at = slice(pair * 2 * HEAD_DIM, (pair + 1) * 2 * HEAD_DIM)
        query, key, value, grad = queries[:, at], key_rows[:, at], value_rows[:, at], context_grad[:, at]
        halves = []
        for side in range(2):
            mine = jnp.where(first_half == (side == 0), grad, zero)
            probs = probs_ref[0, 2 * pair + side]
            wide = probs.astype(jnp.float32)
            prob_grad = mm_turned(mine, value)
            weighted = wide * prob_grad
            score_grad = (
                weighted - wide * jnp.sum(weighted, axis=-1, keepdims=True)
            ).astype(low)
            halves.append(
                (mm(score_grad, key) * scale, mm_rows(score_grad, query) * scale, mm_rows(probs, grad))
            )
        for kind in range(3):
            parts[kind].append(jnp.where(first_half, halves[0][kind], halves[1][kind]).astype(low))
    normed = normed_ref[0]
    normed_grad = None
    for kind in range(3):
        projected_grad = jnp.concatenate(parts[kind], axis=1)
        sums[kind] += mm_rows(normed, projected_grad)
        part = mm_turned(projected_grad, dense_ref[kind])
        normed_grad = part if normed_grad is None else normed_grad + part
    unit, inverse = unit_of(input_ref[0].astype(jnp.float32))
    length = input_grad_ref.shape[1]
    input_grad = hidden_grad + unit_backward(normed_grad, unit, inverse, norm_ref[0:1])
    input_grad_ref[0] = input_grad[:length]
    gain = jnp.sum(normed_grad * unit, axis=0, keepdims=True)
    bias = jnp.sum(normed_grad, axis=0, keepdims=True)
    rows_of = lax.broadcasted_iota(jnp.int32, (8, width), 0)
    norm_grad_ref[...] += jnp.where(rows_of == 0, gain, jnp.where(rows_of == 1, bias, 0.0))

    @pl.when(image == images - 1)
    def _():
        count, kinds, rows, columns = pieces_ref.shape
        across = width // columns
        low_sums[...] = sums[...].astype(low)
        copies = []
        for piece in range(count):
            down, over = piece // across, piece % across
            copies.append(
                pltpu.make_async_copy(
                    low_sums.at[:, down * rows : (down + 1) * rows, over * columns : (over + 1) * columns],
                    pieces_ref.at[place_ref[piece]],
                    sems.at[piece],
                )
            )
        for copy in copies:
            copy.start()
        for copy in copies:
            copy.wait()


def attend_back(length, places, padded, norm_params, dense, normed, projected, probs, context, hidden_grad, pieces_shape):
    images, _, width = padded.shape
    heads = width // HEAD_DIM
    low, wide = jnp.bfloat16, jnp.float32

    def per_image(*shape):
        return pl.BlockSpec((1,) + shape, lambda i: (i,) + (0,) * len(shape))

    def whole(array):
        return pl.BlockSpec(array.shape, lambda i: (0,) * array.ndim)

    return pl.pallas_call(
        attend_back_kernel,
        grid=(images,),
        in_specs=[
            pl.BlockSpec(memory_space=pltpu.SMEM), per_image(PAD, width), whole(norm_params), whole(dense),
            per_image(PAD, width), per_image(3, PAD, width), per_image(heads, PAD, PAD),
            per_image(PAD, width), per_image(PAD, width),
        ],
        out_specs=[
            per_image(length, width), pl.BlockSpec((8, width), lambda i: (0, 0)),
            pl.BlockSpec(memory_space=pl.ANY),
        ],
        out_shape=[
            jax.ShapeDtypeStruct((images, length, width), wide),
            jax.ShapeDtypeStruct((8, width), wide),
            jax.ShapeDtypeStruct(pieces_shape, low),
        ],
        scratch_shapes=[
            pltpu.VMEM((4, width, width), wide),
            pltpu.VMEM((4, width, width), low),
            pltpu.SemaphoreType.DMA((pieces_shape[0],)),
        ],
        compiler_params=kernel_params(56),
        cost_estimate=cost(images * 5e9, images * 6e6),
        name="attend_back",
    )(places, padded, norm_params, dense, normed, projected, probs, context, hidden_grad)


def relay(block, axis, mask):
    size = lax.axis_size(axis)
    return lax.ppermute(block, axis, [(i, i ^ mask) for i in range(size)])


def spread(block, stages):
    pieces = block[None]
    for axis, mask in stages:
        pieces = jnp.concatenate([pieces, relay(pieces, axis, mask)], axis=0)
    return pieces


def collect(pieces, stages):
    for axis, mask in reversed(stages):
        half = pieces.shape[0] // 2
        arrived = relay(pieces[half:], axis, mask)
        total = pieces[:half].astype(jnp.float32) + arrived.astype(jnp.float32)
        pieces = total.astype(pieces.dtype)
    return pieces[0]


def sum_all(value, stages):
    for axis, mask in stages:
        value = value + relay(value, axis, mask)
    return value


def mesh_stages(order):
    def of(axis):
        return [(axis, 1 << b) for b in range((lax.axis_size(axis) - 1).bit_length())]

    by_name = {"z": of("shard"), "x": of("head")[1:], "y": of("tensor"), "core": of("head")[:1]}
    return [stage for name in order for stage in by_name[name]]


def relative_places(stages):
    axes = ("shard", "tensor", "head")
    shape = tuple(lax.axis_size(a) for a in axes)
    place = jnp.zeros(shape, jnp.int32)
    for bit, (axis, mask) in enumerate(stages):
        apart = lax.broadcasted_iota(jnp.int32, shape, axes.index(axis)) ^ lax.axis_index(axis)
        place = place + jnp.where((apart & mask) != 0, 1 << bit, 0)
    return place


def local_plan(
    block_input,
    cotangent,
    routes,
    priority,
    norm_params,
    norm_moment,
    norm_square,
    qkv_weight,
    qkv_moment,
    qkv_square,
    attn_weight,
    attn_moment,
    attn_square,
    router_weight,
    router_moment,
    router_square,
    expert_in,
    in_moment,
    in_square,
    expert_out,
    out_moment,
    out_square,
):
    images, length, model_width = block_input.shape
    experts = lax.axis_size("shard")
    capacity = 9 * images * length // (4 * experts)
    slots = -(-capacity // SLOT_PAD) * SLOT_PAD
    low = jnp.bfloat16
    orders = [("z", "x", "y", "core"), ("z", "y", "x", "core")]
    dense_stages = mesh_stages(orders[0])
    dense_places = relative_places(dense_stages).reshape(-1)
    dense_low = jnp.concatenate(
        [qkv_weight.transpose(1, 0, 2), attn_weight.T[None]], axis=0
    ).astype(low)
    dense_pieces = spread(dense_low, dense_stages)
    expert_low = jnp.stack([expert_in[0], expert_out[0].T]).astype(low)
    parts = len(orders)
    cut = expert_low.shape[2] // parts
    expert_stages = [mesh_stages(o) for o in orders]
    expert_places = [relative_places(s).reshape(experts, -1) for s in expert_stages]
    expert_pieces = [
        spread(expert_low[:, :, i * cut : (i + 1) * cut], s) for i, s in enumerate(expert_stages)
    ]
    router_wide = jnp.pad(router_weight, ((0, 0), (0, 128 - experts))).astype(low)
    slot_row, slot_column = find_slots(routes, priority, experts, capacity)
    slot_column = slot_column.reshape(images, PAD, 128)
    fill = ((0, 0), (0, PAD - length), (0, 0))
    padded, upstream = jnp.pad(block_input, fill), jnp.pad(cotangent, fill)
    dense = join_dense(dense_places, dense_pieces, model_width)
    normed, projected, probs, context, hidden, second, route_probs = attend(
        length, experts, padded, norm_params, dense, router_wide
    )
    tokens = images * PAD
    x, g, xt, gt = dispatch(
        slot_row, second.reshape(tokens, model_width), upstream.reshape(tokens, model_width),
        route_probs.reshape(tokens, 128), experts, slots,
    )
    sums = None
    expert_sums = []
    for i in range(parts):
        made, back, grads = run_experts(
            expert_places[i], x, g, xt, gt, sums, expert_pieces[i], i == parts - 1
        )
        sums = (made, back)
        expert_sums.append(collect(grads, expert_stages[i]))
    block_output, hidden_grad, router_part, norm_two = combine(
        length, experts, slot_column, made, back, hidden, upstream, second, route_probs,
        norm_params, router_wide,
    )
    input_grad, norm_one, dense_grads = attend_back(
        length, dense_places, padded, norm_params, dense, normed, projected, probs, context,
        hidden_grad, dense_pieces.shape,
    )
    dense_sum = collect(dense_grads, dense_stages).astype(jnp.float32)
    small = sum_all(
        jnp.concatenate([(norm_one + norm_two)[:4], router_part[:experts]]), dense_stages
    )
    norm_grad, router_grad = small[:4], small[4:].T
    qkv_grad, attn_grad = dense_sum[:3].transpose(1, 0, 2), dense_sum[3].T
    expert_sum = jnp.concatenate(expert_sums, axis=2).astype(jnp.float32)
    in_grad, out_grad = expert_sum[0][None], expert_sum[1].T[None]
    norm_new = adam_update(norm_params, norm_grad, norm_moment, norm_square, 0.25, 0.0)
    qkv_new = adam_update(
        qkv_weight, qkv_grad, qkv_moment, qkv_square, 1.3 * model_width ** (-0.5), DECAY_RATE
    )
    attn_new = adam_update(
        attn_weight, attn_grad, attn_moment, attn_square, 3.0 * model_width ** (-0.5), DECAY_RATE
    )
    router_new = adam_update(
        router_weight,
        router_grad,
        router_moment,
        router_square,
        0.75 * model_width ** (-0.5),
        DECAY_RATE,
    )
    in_new = adam_update(
        expert_in, in_grad, in_moment, in_square, 1.0 * model_width ** (-0.5), DECAY_RATE
    )
    out_new = adam_update(
        expert_out, out_grad, out_moment, out_square, 0.8 * experts * FF ** (-0.5), DECAY_RATE
    )
    return (
        block_output,
        input_grad,
        norm_new[0],
        norm_new[1],
        norm_new[2],
        qkv_new[0],
        qkv_new[1],
        qkv_new[2],
        attn_new[0],
        attn_new[1],
        attn_new[2],
        router_new[0],
        router_new[1],
        router_new[2],
        in_new[0],
        in_new[1],
        in_new[2],
        out_new[0],
        out_new[1],
        out_new[2],
    )


def solution(mesh):
    fits = mesh.shape["shard"] <= 4
    return jax.shard_map(
        local_plan if fits else slot_plan,
        mesh=mesh,
        in_specs=(
            P(("shard", "head", "tensor"), None, None),
            P(("shard", "head", "tensor"), None, None),
            P(("shard", "head", "tensor"), None, None),
            P(("shard", "head", "tensor"), None),
            P(),
            P(),
            P(),
            P(("shard", "tensor"), None, "head"),
            P(("shard", "tensor"), None, "head"),
            P(("shard", "tensor"), None, "head"),
            P("head", ("shard", "tensor")),
            P("head", ("shard", "tensor")),
            P("head", ("shard", "tensor")),
            P(),
            P(),
            P(),
            P("shard", "head", "tensor"),
            P("shard", "head", "tensor"),
            P("shard", "head", "tensor"),
            P("shard", "tensor", "head"),
            P("shard", "tensor", "head"),
            P("shard", "tensor", "head"),
        ),
        out_specs=(
            P(("shard", "head", "tensor"), None, None),
            P(("shard", "head", "tensor"), None, None),
            P(),
            P(),
            P(),
            P(("shard", "tensor"), None, "head"),
            P(("shard", "tensor"), None, "head"),
            P(("shard", "tensor"), None, "head"),
            P("head", ("shard", "tensor")),
            P("head", ("shard", "tensor")),
            P("head", ("shard", "tensor")),
            P(),
            P(),
            P(),
            P("shard", "head", "tensor"),
            P("shard", "head", "tensor"),
            P("shard", "head", "tensor"),
            P("shard", "tensor", "head"),
            P("shard", "tensor", "head"),
            P("shard", "tensor", "head"),
        ),
        check_vma=False,
    )
```

```python
import math
from functools import partial

import jax
import jax.numpy as jnp
from jax import lax
from jax.experimental import pallas as pl
from jax.experimental.pallas import tpu as pltpu
from jax.sharding import PartitionSpec as P

HEAD_DIM = 64
FF = 2048
STEP = 10


EPS_NORM = 1e-06
BETA_ONE = 0.9
BETA_TWO = 0.999
ADAM_EPS = 1e-08
DECAY_RATE = 0.1


def norm_forward(values, gain_row, bias_row):
    center = jnp.mean(values, axis=-1, keepdims=True)
    shifted = values - center
    inverse = lax.rsqrt(jnp.mean(shifted * shifted, axis=-1, keepdims=True) + EPS_NORM)
    unit_rows = shifted * inverse
    return (unit_rows * gain_row + bias_row, unit_rows, inverse)


def norm_backward(grad_rows, unit_rows, inverse, gain_row):
    scaled = grad_rows * gain_row
    inner_grad = (
        scaled
        - jnp.mean(scaled, axis=-1, keepdims=True)
        - unit_rows * jnp.mean(scaled * unit_rows, axis=-1, keepdims=True)
    )
    return (
        inner_grad * inverse,
        jnp.sum(grad_rows * unit_rows, axis=0),
        jnp.sum(grad_rows, axis=0),
    )


def gelu_grad(pre_act, upstream):
    result, pullback = jax.vjp(partial(jax.nn.gelu, approximate=True), pre_act)
    return pullback(upstream)[0]


def adam_update(weight, gradient, moment, square, step_rate, decay_rate):
    moment_new = BETA_ONE * moment + (1.0 - BETA_ONE) * gradient
    square_new = BETA_TWO * square + (1.0 - BETA_TWO) * gradient * gradient
    first_hat = moment_new / (1.0 - BETA_ONE**STEP)
    second_hat = square_new / (1.0 - BETA_TWO**STEP)
    weight_new = weight - step_rate * (
        first_hat / (jnp.sqrt(second_hat) + ADAM_EPS) + decay_rate * weight
    )
    return (weight_new, moment_new, square_new)


def send_rows(parcel):
    copies = jnp.broadcast_to(
        parcel[:, None], (parcel.shape[0], lax.axis_size("tensor")) + parcel.shape[1:]
    )
    flat_copies = copies.reshape((-1,) + parcel.shape[1:])
    arrived = lax.all_to_all(
        flat_copies, ("shard", "tensor"), split_axis=0, concat_axis=0, tiled=True
    )
    return arrived.reshape(copies.shape)


def return_rows(partial_rows):
    flat_rows = partial_rows.reshape((-1,) + partial_rows.shape[2:])
    arrived = lax.all_to_all(
        flat_rows.astype(jnp.bfloat16), ("shard", "tensor"), split_axis=0, concat_axis=0, tiled=True
    ).astype(flat_rows.dtype)
    return jnp.sum(arrived.reshape(partial_rows.shape), axis=1)


def slot_plan(
    block_input,
    cotangent,
    routes,
    priority,
    norm_params,
    norm_moment,
    norm_square,
    qkv_weight,
    qkv_moment,
    qkv_square,
    attn_weight,
    attn_moment,
    attn_square,
    router_weight,
    router_moment,
    router_square,
    expert_in,
    in_moment,
    in_square,
    expert_out,
    out_moment,
    out_square,
):
    images, length, model_width = block_input.shape
    row_count = images * length
    local_experts = expert_in.shape[0]
    shards = lax.axis_size("shard")
    experts = local_experts * shards
    capacity = 9 * row_count // (4 * experts)
    score_scale = HEAD_DIM ** (-0.5)
    full_qkv, full_attn = (
        lax.all_gather(qkv_weight.astype(jnp.bfloat16), ("shard", "tensor"), axis=0, tiled=True),
        lax.all_gather(attn_weight.astype(jnp.bfloat16), ("shard", "tensor"), axis=1, tiled=True),
    )
    inputs = block_input.astype(jnp.float32).reshape(row_count, model_width)
    normed, unit_one, inverse_one = norm_forward(inputs, norm_params[0], norm_params[1])
    normed_low = normed.astype(jnp.bfloat16).reshape(images, length, model_width)
    gathered, hidden_in, hidden_out = (
        lax.all_gather(normed_low, "head", axis=0, tiled=True),
        lax.all_gather(expert_in.astype(jnp.bfloat16), "head", axis=1, tiled=True),
        lax.all_gather(expert_out.astype(jnp.bfloat16), "head", axis=2, tiled=True),
    )
    local_heads = full_qkv.shape[2] // HEAD_DIM
    all_images = gathered.shape[0]
    head_shape = (all_images, length, local_heads, HEAD_DIM)
    projected = jnp.einsum(
        "isd,dcn->iscn", gathered, full_qkv, preferred_element_type=jnp.float32
    ).astype(jnp.bfloat16)
    queries = projected[:, :, 0].reshape(head_shape)
    key_rows = projected[:, :, 1].reshape(head_shape)
    value_rows = projected[:, :, 2].reshape(head_shape)
    scores = (
        jnp.einsum("iqhe,ikhe->ihqk", queries, key_rows, preferred_element_type=jnp.float32)
        * score_scale
    )
    score_top = jnp.max(scores, axis=-1, keepdims=True)
    log_total = score_top + jnp.log(jnp.sum(jnp.exp(scores - score_top), axis=-1, keepdims=True))
    probs_low = jnp.exp(scores - log_total).astype(jnp.bfloat16)
    context = jnp.einsum(
        "ihqk,ikhe->iqhe", probs_low, value_rows, preferred_element_type=jnp.float32
    ).astype(jnp.bfloat16)
    context = context.reshape(all_images * length, local_heads * HEAD_DIM)
    attended = lax.psum_scatter(
        jnp.dot(context, full_attn, preferred_element_type=jnp.float32).astype(jnp.bfloat16),
        "head",
        scatter_dimension=0,
        tiled=True,
    ).astype(jnp.float32)
    hidden = inputs + attended
    normed_two, unit_two, inverse_two = norm_forward(hidden, norm_params[2], norm_params[3])
    second_low = normed_two.astype(jnp.bfloat16)
    router_low = router_weight.astype(jnp.bfloat16)
    logits = jnp.dot(second_low, router_low, preferred_element_type=jnp.float32)
    route_probs = jax.nn.softmax(logits, axis=-1)
    route_hot = (
        routes.reshape(row_count, 2)[:, :, None]
        == jnp.arange(experts, dtype=jnp.int32)[None, None, :]
    ).astype(jnp.float32)
    gate_values = jnp.sum(route_probs[:, None, :] * route_hot, axis=-1)
    expert_ids = routes.reshape(2 * row_count)
    rank_values = priority[0]
    pair_hot = route_hot.reshape(2 * row_count, experts)
    earlier = (rank_values[None, :] < rank_values[:, None]).astype(jnp.bfloat16)
    counts = jnp.dot(earlier, pair_hot.astype(jnp.bfloat16), preferred_element_type=jnp.float32)
    slot_index = jnp.sum(counts * pair_hot, axis=1).astype(jnp.int32)
    target = jnp.where(
        slot_index < capacity, expert_ids * capacity + slot_index, experts * capacity
    )
    filler = jnp.full((experts * capacity,), 2 * row_count, jnp.int32)
    owner_pair = filler.at[target].set(jnp.arange(2 * row_count, dtype=jnp.int32), mode="drop")
    padded = jnp.concatenate([second_low, jnp.zeros((1, model_width), jnp.bfloat16)], axis=0)
    parcel = padded[owner_pair // 2].reshape(shards, local_experts, capacity, model_width)
    arrived = send_rows(parcel)
    pre_act = jnp.einsum("stecd,edf->stecf", arrived, hidden_in, preferred_element_type=jnp.float32)
    active = jax.nn.gelu(pre_act, approximate=True).astype(jnp.bfloat16)
    part_rows = jnp.einsum(
        "stecf,efd->stecd", active, hidden_out, preferred_element_type=jnp.float32
    )
    expert_rows = return_rows(part_rows).reshape(experts * capacity, model_width)
    padded_out = jnp.concatenate([expert_rows, jnp.zeros((1, model_width), jnp.float32)], axis=0)
    per_pair = padded_out[target].reshape(row_count, 2, model_width)
    block_sum = hidden + jnp.sum(gate_values[:, :, None] * per_pair, axis=1)
    block_output = block_sum.astype(jnp.bfloat16).reshape(images, length, model_width)
    upstream = cotangent.astype(jnp.float32).reshape(row_count, model_width)
    pair_grad = (
        (gate_values[:, :, None] * upstream[:, None, :])
        .astype(jnp.bfloat16)
        .reshape(2 * row_count, model_width)
    )
    gate_grad = jnp.sum(upstream[:, None, :] * per_pair, axis=-1)
    padded_grad = jnp.concatenate([pair_grad, jnp.zeros((1, model_width), jnp.bfloat16)], axis=0)
    grad_parcel = padded_grad[owner_pair].reshape(shards, local_experts, capacity, model_width)
    grad_arrived = send_rows(grad_parcel)
    grad_out_part = jnp.einsum(
        "stecf,stecd->efd", active, grad_arrived, preferred_element_type=jnp.float32
    )
    active_grad = jnp.einsum(
        "stecd,efd->stecf", grad_arrived, hidden_out, preferred_element_type=jnp.float32
    )
    pre_grad = gelu_grad(pre_act, active_grad).astype(jnp.bfloat16)
    grad_in_part = jnp.einsum(
        "stecd,stecf->edf", arrived, pre_grad, preferred_element_type=jnp.float32
    )
    row_grad = jnp.einsum(
        "stecf,edf->stecd", pre_grad, hidden_in, preferred_element_type=jnp.float32
    )
    slot_grad = return_rows(row_grad).reshape(experts * capacity, model_width)
    padded_slot = jnp.concatenate([slot_grad, jnp.zeros((1, model_width), jnp.float32)], axis=0)
    second_grad = jnp.sum(padded_slot[target].reshape(row_count, 2, model_width), axis=1)
    prob_sum = jnp.sum(gate_grad[:, :, None] * route_hot, axis=1)
    logit_grad = (
        route_probs * (prob_sum - jnp.sum(route_probs * prob_sum, axis=-1, keepdims=True))
    ).astype(jnp.bfloat16)
    router_grad = jnp.einsum(
        "rd,re->de", second_low, logit_grad, preferred_element_type=jnp.float32
    )
    second_grad = second_grad + jnp.einsum(
        "re,de->rd", logit_grad, router_low, preferred_element_type=jnp.float32
    )
    hidden_part, gain_two, bias_two = norm_backward(
        second_grad, unit_two, inverse_two, norm_params[2]
    )
    hidden_grad = upstream + hidden_part
    attended_grad = lax.all_gather(hidden_grad.astype(jnp.bfloat16), "head", axis=0, tiled=True)
    attn_grad = jnp.einsum("rn,rd->nd", context, attended_grad, preferred_element_type=jnp.float32)
    context_grad = jnp.einsum(
        "rd,nd->rn", attended_grad, full_attn, preferred_element_type=jnp.float32
    ).astype(jnp.bfloat16)
    context_grad = context_grad.reshape(head_shape)
    scores_again = (
        jnp.einsum("iqhe,ikhe->ihqk", queries, key_rows, preferred_element_type=jnp.float32)
        * score_scale
    )
    probs_full = jnp.exp(scores_again - log_total)
    prob_grad = jnp.einsum(
        "iqhe,ikhe->ihqk", context_grad, value_rows, preferred_element_type=jnp.float32
    )
    score_grad = (
        probs_full * (prob_grad - jnp.sum(probs_full * prob_grad, axis=-1, keepdims=True))
    ).astype(jnp.bfloat16)
    query_grad = (
        jnp.einsum("ihqk,ikhe->iqhe", score_grad, key_rows, preferred_element_type=jnp.float32)
        * score_scale
    )
    key_grad = (
        jnp.einsum("ihqk,iqhe->ikhe", score_grad, queries, preferred_element_type=jnp.float32)
        * score_scale
    )
    value_grad = jnp.einsum(
        "ihqk,iqhe->ikhe", probs_low, context_grad, preferred_element_type=jnp.float32
    )
    projected_grad = (
        jnp.stack([query_grad, key_grad, value_grad], axis=2)
        .reshape(all_images, length, 3, local_heads * HEAD_DIM)
        .astype(jnp.bfloat16)
    )
    qkv_grad = jnp.einsum(
        "isd,iscn->dcn", gathered, projected_grad, preferred_element_type=jnp.float32
    )
    normed_part = jnp.einsum(
        "iscn,dcn->isd", projected_grad, full_qkv, preferred_element_type=jnp.float32
    )
    normed_grad, in_grad, out_grad = (
        lax.psum_scatter(
            normed_part.astype(jnp.bfloat16), "head", scatter_dimension=0, tiled=True
        ).astype(jnp.float32),
        lax.psum_scatter(
            grad_in_part.astype(jnp.bfloat16), "head", scatter_dimension=1, tiled=True
        ).astype(jnp.float32),
        lax.psum_scatter(
            grad_out_part.astype(jnp.bfloat16), "head", scatter_dimension=2, tiled=True
        ).astype(jnp.float32),
    )
    input_part, gain_one, bias_one = norm_backward(
        normed_grad.reshape(row_count, model_width), unit_one, inverse_one, norm_params[0]
    )
    input_grad = (hidden_grad + input_part).reshape(images, length, model_width)
    norm_grad = jnp.stack([gain_one, bias_one, gain_two, bias_two])
    norm_grad, router_grad = lax.psum((norm_grad, router_grad), ("shard", "head", "tensor"))
    qkv_grad, attn_grad = (
        lax.psum_scatter(qkv_grad, ("shard", "tensor"), scatter_dimension=0, tiled=True),
        lax.psum_scatter(attn_grad, ("shard", "tensor"), scatter_dimension=1, tiled=True),
    )
    norm_new = adam_update(norm_params, norm_grad, norm_moment, norm_square, 0.25, 0.0)
    qkv_new = adam_update(
        qkv_weight, qkv_grad, qkv_moment, qkv_square, 1.3 * model_width ** (-0.5), DECAY_RATE
    )
    attn_new = adam_update(
        attn_weight, attn_grad, attn_moment, attn_square, 3.0 * model_width ** (-0.5), DECAY_RATE
    )
    router_new = adam_update(
        router_weight,
        router_grad,
        router_moment,
        router_square,
        0.75 * model_width ** (-0.5),
        DECAY_RATE,
    )
    in_new = adam_update(
        expert_in, in_grad, in_moment, in_square, 1.0 * model_width ** (-0.5), DECAY_RATE
    )
    out_new = adam_update(
        expert_out, out_grad, out_moment, out_square, 0.8 * experts * FF ** (-0.5), DECAY_RATE
    )
    return (
        block_output,
        input_grad,
        norm_new[0],
        norm_new[1],
        norm_new[2],
        qkv_new[0],
        qkv_new[1],
        qkv_new[2],
        attn_new[0],
        attn_new[1],
        attn_new[2],
        router_new[0],
        router_new[1],
        router_new[2],
        in_new[0],
        in_new[1],
        in_new[2],
        out_new[0],
        out_new[1],
        out_new[2],
    )


PAD = 208
SLOT_PAD = 16
CUTS = (0, 3, 8)


def kernel_params(megabytes):
    return pltpu.CompilerParams(vmem_limit_bytes=megabytes << 20)


def cost(flops, moved):
    return pl.CostEstimate(flops=int(flops), bytes_accessed=int(moved), transcendentals=0)


def mm(left, right):
    return lax.dot_general(left, right, (((1,), (0,)), ((), ())), preferred_element_type=jnp.float32)


def mm_turned(left, right):
    return lax.dot_general(left, right, (((1,), (1,)), ((), ())), preferred_element_type=jnp.float32)


def mm_rows(left, right):
    return lax.dot_general(left, right, (((0,), (0,)), ((), ())), preferred_element_type=jnp.float32)


def unit_of(values):
    center = jnp.mean(values, axis=-1, keepdims=True)
    shifted = values - center
    inverse = lax.rsqrt(jnp.mean(shifted * shifted, axis=-1, keepdims=True) + EPS_NORM)
    return (shifted * inverse, inverse)


def unit_backward(grad_rows, unit_rows, inverse, gain_row):
    scaled = grad_rows * gain_row
    inner_grad = (
        scaled
        - jnp.mean(scaled, axis=-1, keepdims=True)
        - unit_rows * jnp.mean(scaled * unit_rows, axis=-1, keepdims=True)
    )
    return inner_grad * inverse


def absolute(group):
    tensor = lax.axis_index("tensor") ^ (group // 2 % 2)
    head = lax.axis_index("head") ^ (2 * (group % 2) + group // 4)
    return tensor, head


GROUPS = 8


def slot_kernel(experts, capacity, row_ref, column_ref, slot_row_ref, slot_column_ref):
    none = 1 << 20
    tokens = row_ref.shape[1]
    lanes = lax.broadcasted_iota(jnp.int32, (PAD, 128), 1)
    rows_of = lax.broadcasted_iota(jnp.int32, (8, tokens), 0)

    def ranks(named, rank, expert):
        return jnp.where(
            named[0] == expert, rank[0], jnp.where(named[1] == expert, rank[1], none)
        )

    routes_row, ranks_row = (row_ref[0:1], row_ref[1:2]), (row_ref[2:3], row_ref[3:4])
    all_rows = jnp.full((8, tokens), -1, jnp.int32)
    row_of = [ranks(routes_row, ranks_row, e) for e in range(experts)]
    totals = [jnp.zeros((1, tokens), jnp.float32) for e in range(experts)]
    for block in range(tokens // PAD):
        part = column_ref[block * PAD : (block + 1) * PAD]
        routes_col, ranks_col = (part[:, 0:1], part[:, 1:2]), (part[:, 2:3], part[:, 3:4])
        result = jnp.full((PAD, 128), -1, jnp.int32)
        for e in range(experts):
            column = ranks(routes_col, ranks_col, e)
            totals[e] = totals[e] + jnp.sum(
                jnp.where(column < row_of[e], 1.0, 0.0), axis=0, keepdims=True
            )
            before = jnp.sum(
                jnp.where(row_of[e] < column, 1.0, 0.0), axis=1, keepdims=True
            ).astype(jnp.int32)
            slot = jnp.where((column < none) & (before < capacity), before, -1)
            result = jnp.where(lanes == e, slot, result)
        slot_column_ref[block * PAD : (block + 1) * PAD] = result
    for e in range(experts):
        before = totals[e].astype(jnp.int32)
        slot = jnp.where((row_of[e] < none) & (before < capacity), before, -1)
        all_rows = jnp.where(rows_of == e, slot, all_rows)
    slot_row_ref[...] = all_rows


def slot_tables(routes, priority):
    images, length, _ = routes.shape
    tokens = images * PAD
    table = jnp.concatenate([routes, priority.reshape(images, length, 2)], axis=2)
    table = jnp.pad(table, ((0, 0), (0, PAD - length), (0, 0)), constant_values=-1)
    table = table.reshape(tokens, 4)
    columns = jnp.pad(table, ((0, 0), (0, 4)))
    return (columns.T, columns)


def find_slots(tables, experts, capacity):
    tokens = tables[1].shape[0]
    return pl.pallas_call(
        partial(slot_kernel, experts, capacity),
        out_shape=(
            jax.ShapeDtypeStruct((8, tokens), jnp.int32),
            jax.ShapeDtypeStruct((tokens, 128), jnp.int32),
        ),
        compiler_params=kernel_params(32),
        cost_estimate=cost(1e10, 1e6),
        name="find_slots",
    )(*tables)


def dense_window(ref, piece, shards, rows, columns):
    tensor, head = absolute(piece // shards)
    shard = lax.axis_index("shard") ^ (piece % shards)
    down = pl.multiple_of((shard * lax.axis_size("tensor") + tensor) * rows, rows)
    over = pl.multiple_of(head * columns, columns)
    return ref.at[:, pl.ds(down, rows), pl.ds(over, columns)]


def dense_kernel(*refs):
    groups, (full_ref, sems) = refs[:GROUPS], refs[GROUPS:]
    shards, kinds, rows, columns = groups[0].shape
    copies = []
    for piece in range(GROUPS * shards):
        copies.append(
            pltpu.make_async_copy(
                groups[piece // shards].at[piece % shards],
                dense_window(full_ref, piece, shards, rows, columns),
                sems.at[piece],
            )
        )
    for copy in copies:
        copy.start()
    for copy in copies:
        copy.wait()


def join_dense(groups, model_width):
    shards, kinds = groups[0].shape[:2]
    return pl.pallas_call(
        dense_kernel,
        out_shape=jax.ShapeDtypeStruct((kinds, model_width, model_width), groups[0].dtype),
        in_specs=[pl.BlockSpec(memory_space=pl.ANY)] * GROUPS,
        out_specs=pl.BlockSpec(memory_space=pltpu.VMEM),
        scratch_shapes=[pltpu.SemaphoreType.DMA((GROUPS * shards,))],
        compiler_params=kernel_params(16),
        cost_estimate=cost(1e6, 4e6),
        name="join_dense",
    )(*groups)


def attend_kernel(
    length, experts, input_ref, cotangent_ref, norm_ref, dense_ref, router_ref,
    normed_ref, projected_ref, probs_ref, context_ref, hidden_ref, second_ref, route_ref, upstream_ref, whole,
):
    low = jnp.bfloat16
    whole[length // 8 * 8 :] = jnp.zeros_like(whole[length // 8 * 8 :])
    whole[:length] = cotangent_ref[0].astype(jnp.float32)
    upstream_ref[0] = whole[...].astype(low)
    whole[:length] = input_ref[0].astype(jnp.float32)
    values = whole[...]
    width = values.shape[1]
    unit, _ = unit_of(values)
    normed = (unit * norm_ref[0:1] + norm_ref[1:2]).astype(low)
    normed_ref[0] = normed
    queries, key_rows, value_rows = (mm(normed, dense_ref[c]).astype(low) for c in range(3))
    projected_ref[0, 0] = queries
    projected_ref[0, 1] = key_rows
    projected_ref[0, 2] = value_rows
    first_half = lax.broadcasted_iota(jnp.int32, (PAD, 2 * HEAD_DIM), 1) < HEAD_DIM
    is_key = lax.broadcasted_iota(jnp.int32, (PAD, PAD), 1) < length
    zero = jnp.zeros((PAD, 2 * HEAD_DIM), low)
    pairs = []
    for pair in range(width // (2 * HEAD_DIM)):
        at = slice(pair * 2 * HEAD_DIM, (pair + 1) * 2 * HEAD_DIM)
        query, key, value = queries[:, at], key_rows[:, at], value_rows[:, at]
        halves = []
        for side in range(2):
            mine = jnp.where(first_half == (side == 0), query, zero)
            scores = mm_turned(mine, key) * (HEAD_DIM ** (-0.5))
            scores = jnp.where(is_key, scores, -1e30)
            top = jnp.max(scores, axis=-1, keepdims=True)
            raised = jnp.exp(scores - top)
            probs = (raised / jnp.sum(raised, axis=-1, keepdims=True)).astype(low)
            probs_ref[0, 2 * pair + side] = probs
            halves.append(mm(probs, value))
        pairs.append(jnp.where(first_half, halves[0], halves[1]).astype(low))
    context = jnp.concatenate(pairs, axis=1)
    context_ref[0] = context
    hidden = values + mm_turned(context, dense_ref[3])
    hidden_ref[0] = hidden
    unit, _ = unit_of(hidden)
    second = (unit * norm_ref[2:3] + norm_ref[3:4]).astype(low)
    second_ref[0] = second
    logits = mm(second, router_ref[...])
    is_expert = lax.broadcasted_iota(jnp.int32, logits.shape, 1) < experts
    logits = jnp.where(is_expert, logits, -1e30)
    raised = jnp.exp(logits - jnp.max(logits, axis=-1, keepdims=True))
    route_ref[0] = raised / jnp.sum(raised, axis=-1, keepdims=True)


def attend(experts, block_input, cotangent, norm_params, dense, router_wide):
    images, length, width = block_input.shape
    heads = width // HEAD_DIM
    low, wide = jnp.bfloat16, jnp.float32

    def per_image(*shape):
        return pl.BlockSpec((1,) + shape, lambda i: (i,) + (0,) * len(shape))

    def whole(array):
        return pl.BlockSpec(array.shape, lambda i: (0,) * array.ndim)

    shapes = [
        ((PAD, width), low), ((3, PAD, width), low), ((heads, PAD, PAD), low), ((PAD, width), low),
        ((PAD, width), wide), ((PAD, width), low), ((PAD, 128), wide), ((PAD, width), low),
    ]
    return pl.pallas_call(
        partial(attend_kernel, length, experts),
        grid=(images,),
        in_specs=[per_image(length, width)] * 2 + [whole(norm_params), whole(dense), whole(router_wide)],
        out_specs=[per_image(*s) for s, _ in shapes],
        out_shape=[jax.ShapeDtypeStruct((images,) + s, t) for s, t in shapes],
        scratch_shapes=[pltpu.VMEM((PAD, width), wide)],
        compiler_params=kernel_params(48),
        cost_estimate=cost(images * 2.5e9, images * 5e6),
        name="attend",
    )(block_input, cotangent, norm_params, dense, router_wide)


def dispatch_kernel(waits, slot_ref, second_ref, upstream_ref, route_ref, *refs):
    x_ref, g_ref, xt_ref, gt_ref = refs[waits:]
    low = jnp.bfloat16
    expert = pl.program_id(0)
    slots, tokens = x_ref.shape[1], second_ref.shape[0]
    rows_of = lax.broadcasted_iota(jnp.int32, (8, tokens), 0)
    slot_row = jnp.max(jnp.where(rows_of == expert, slot_ref[...], -1), axis=0, keepdims=True)
    hot = lax.broadcasted_iota(jnp.int32, (slots, tokens), 0) == slot_row
    hot = jnp.where(hot, 1.0, 0.0).astype(low)
    lanes = lax.broadcasted_iota(jnp.int32, (tokens, 128), 1)
    gate = jnp.sum(jnp.where(lanes == expert, route_ref[...], 0.0), axis=1, keepdims=True)
    pair_grad = (gate * upstream_ref[...].astype(jnp.float32)).astype(low)
    rows = mm(hot, second_ref[...]).astype(low)
    x_ref[0] = rows
    xt_ref[0] = rows.T
    rows = mm(hot, pair_grad).astype(low)
    g_ref[0] = rows
    gt_ref[0] = rows.T


def dispatch(slot_row, second, upstream, route_probs, experts, slots, waits=()):
    tokens, width = second.shape

    def whole(array):
        return pl.BlockSpec(array.shape, lambda e: (0,) * array.ndim)

    flat = pl.BlockSpec((1, slots, width), lambda e: (e, 0, 0))
    turned = pl.BlockSpec((1, width, slots), lambda e: (e, 0, 0))
    low = jnp.bfloat16
    return pl.pallas_call(
        partial(dispatch_kernel, len(waits)),
        grid=(experts,),
        in_specs=[whole(a) for a in (slot_row, second, upstream, route_probs)]
        + [pl.BlockSpec(memory_space=pl.ANY)] * len(waits),
        out_specs=[flat, flat, turned, turned],
        out_shape=[jax.ShapeDtypeStruct((experts, slots, width), low)] * 2
        + [jax.ShapeDtypeStruct((experts, width, slots), low)] * 2,
        compiler_params=kernel_params(48),
        cost_estimate=cost(4 * slots * tokens * width * experts, 1e7),
        name="dispatch",
    )(slot_row, second, upstream, route_probs, *waits)


def expert_kernel(first, last, count, x_ref, g_ref, xt_ref, gt_ref, *refs):
    low = jnp.bfloat16
    if not first:
        made_in, back_in = refs[:2]
        refs = refs[2:]
    sources, refs = refs[:count], refs[count:]
    made_ref, back_ref, keep_ref, give_ref = refs[:4]
    if last:
        held, sent, in_sems, out_sems, made_sum, back_sum = refs[4:]
    else:
        held, sent, in_sems, out_sems = refs[4:]
        made_sum, back_sum = made_ref.at[0], back_ref.at[0]
    expert, experts = pl.program_id(0), pl.num_programs(0)
    _, kinds, rows, columns = sources[0].shape
    shards, heads, tensors = (lax.axis_size(a) for a in ("shard", "head", "tensor"))
    half = shards // 2

    def window(ref, slot, group):
        tensor, head = absolute(group)
        down = pl.multiple_of(head * rows, rows)
        over = pl.multiple_of(tensor * columns, columns)
        return ref.at[slot, :, pl.ds(down, rows), pl.ds(over, columns)]

    def fetch(source, slot, group):
        return pltpu.make_async_copy(source, window(held, slot, group), in_sems.at[slot, group])

    def start_fetch(which, slot, group):
        if count == 1:
            tensor, head = absolute(group)
            fetch(sources[0].at[(which * heads + head) * tensors + tensor], slot, group).start()
            return
        z = which ^ lax.axis_index("shard")
        place = group % 4 + (group // 4) * 5
        if group % 4 < 3:
            fetch(sources[place].at[z], slot, group).start()
            return

        @pl.when(z < half)
        def _():
            fetch(sources[place].at[z], slot, group).start()

        @pl.when(z >= half)
        def _():
            fetch(sources[place + 1].at[z - half], slot, group).start()

    def put(which, slot, group):
        target = keep_ref if group < GROUPS // 2 else give_ref
        place = group % (GROUPS // 2) * shards + (which ^ lax.axis_index("shard"))
        return pltpu.make_async_copy(window(sent, slot, group), target.at[place], out_sems.at[slot, group])

    slot = lax.rem(expert, 2)

    @pl.when(expert == 0)
    def _():
        for group in range(GROUPS):
            start_fetch(0, 0, group)

    @pl.when(expert + 1 < experts)
    def _():
        for group in range(GROUPS):
            start_fetch(expert + 1, 1 - slot, group)

    for group in range(GROUPS):
        fetch(sources[0].at[0], slot, group).wait()

    @pl.when(expert >= 2)
    def _():
        for group in range(GROUPS):
            put(expert - 2, slot, group).wait()

    x, g, xt, gt = x_ref[0], g_ref[0], xt_ref[0], gt_ref[0]
    units = held.shape[3]
    tile = TILE if units % TILE == 0 else 256
    for unit in range(0, units, tile):
        at = slice(unit, unit + tile)
        w_in, w_out = held[slot, 0, :, at], held[slot, 1, :, at]
        v = mm(x, w_in)
        grad = mm(g, w_out)
        square = v * v
        tanh = jnp.tanh(v * (0.7978845608028654 + 0.035677408136300125 * square))
        half = 0.5 + 0.5 * tanh
        active = (v * half).astype(low)
        slope = half + v * (half * (1.0 - tanh)) * (
            0.7978845608028654 + 0.10703222440890037 * square
        )
        pre_grad = (grad * slope).astype(low)
        made = mm_turned(active, w_out)
        back = mm_turned(pre_grad, w_in)
        if unit > 0:
            made, back = made_sum[...] + made, back_sum[...] + back
        elif not first:
            made, back = made_in[0] + made, back_in[0] + back
        if last and unit + tile == units:
            made_ref[0], back_ref[0] = made.astype(low), back.astype(low)
        else:
            made_sum[...] = made
            back_sum[...] = back
        sent[slot, 0, :, at] = mm(xt, pre_grad).astype(low)
        sent[slot, 1, :, at] = mm(gt, active).astype(low)
    for group in range(GROUPS):
        put(expert, slot, group).start()

    @pl.when(expert == experts - 1)
    def _():
        for group in range(GROUPS):
            put(expert - 1, 1 - slot, group).wait()
        for group in range(GROUPS):
            put(expert, slot, group).wait()


TILE = 256


def run_experts(x, g, xt, gt, sums, sources, last):
    experts, slots, width = x.shape
    _, kinds, rows, columns = sources[0].shape
    shards = lax.axis_size("shard")
    units = GROUPS * rows * columns // width
    low = jnp.bfloat16
    flat = pl.BlockSpec((1, slots, width), lambda e: (e, 0, 0))
    turned = pl.BlockSpec((1, width, slots), lambda e: (e, 0, 0))
    anywhere = pl.BlockSpec(memory_space=pl.ANY)
    kept = low if last else jnp.float32
    first = sums is None
    given = () if first else tuple(sums)
    scratch = [
        pltpu.VMEM((2, kinds, width, units), low),
        pltpu.VMEM((2, kinds, width, units), low),
        pltpu.SemaphoreType.DMA((2, GROUPS)),
        pltpu.SemaphoreType.DMA((2, GROUPS)),
    ]
    if last:
        scratch += [pltpu.VMEM((slots, width), jnp.float32)] * 2
    return pl.pallas_call(
        partial(expert_kernel, first, last, len(sources)),
        grid=(experts,),
        in_specs=[flat, flat, turned, turned] + [flat] * len(given) + [anywhere] * len(sources),
        out_specs=[flat, flat, anywhere, anywhere],
        out_shape=[jax.ShapeDtypeStruct((experts, slots, width), kept)] * 2
        + [jax.ShapeDtypeStruct((GROUPS // 2 * shards, kinds, rows, columns), low)] * 2,
        scratch_shapes=scratch,
        compiler_params=kernel_params(56),
        cost_estimate=cost(12 * experts * slots * width * units, 3e7),
        name="experts",
    )(x, g, xt, gt, *given, *sources)


def combine_kernel(
    experts, waits, slot_ref, made_ref, back_ref, hidden_ref, upstream_ref, second_ref, route_ref,
    norm_ref, router_ref, *refs
):
    output_ref, grad_ref, router_grad_ref, norm_grad_ref = refs[waits:]
    low = jnp.bfloat16
    image = pl.program_id(0)
    hidden = hidden_ref[0]
    upstream = upstream_ref[0].astype(jnp.float32)
    route_probs = route_ref[0]
    slots = made_ref.shape[1]
    lanes = lax.broadcasted_iota(jnp.int32, (PAD, slots), 1)
    wide_lanes = lax.broadcasted_iota(jnp.int32, (PAD, 128), 1)
    total = hidden
    second_grad = jnp.zeros_like(hidden)
    prob_sum = jnp.zeros((PAD, 128), jnp.float32)
    for e in range(experts):
        hot = jnp.where(lanes == slot_ref[0][:, e : e + 1], 1.0, 0.0).astype(low)
        made = mm(hot, made_ref[e])
        second_grad = second_grad + mm(hot, back_ref[e])
        total = total + route_probs[:, e : e + 1] * made
        gate_grad = jnp.sum(upstream * made, axis=-1, keepdims=True)
        prob_sum = jnp.where(wide_lanes == e, gate_grad, prob_sum)
    length = output_ref.shape[1]
    output_ref[0] = total.astype(low)[:length]
    inner = jnp.sum(route_probs * prob_sum, axis=-1, keepdims=True)
    logit_grad = (route_probs * (prob_sum - inner)).astype(low)
    second_grad = second_grad + mm_turned(logit_grad, router_ref[...])
    unit, inverse = unit_of(hidden)
    grad_ref[0] = upstream + unit_backward(second_grad, unit, inverse, norm_ref[2:3])
    router_grad = mm_rows(logit_grad, second_ref[0])[:8]
    gain = jnp.sum(second_grad * unit, axis=0, keepdims=True)
    bias = jnp.sum(second_grad, axis=0, keepdims=True)
    rows_of = lax.broadcasted_iota(jnp.int32, (8, hidden.shape[1]), 0)
    norm_grad = jnp.where(rows_of == 2, gain, jnp.where(rows_of == 3, bias, 0.0))

    @pl.when(image == 0)
    def _():
        router_grad_ref[...] = router_grad
        norm_grad_ref[...] = norm_grad

    @pl.when(image > 0)
    def _():
        router_grad_ref[...] += router_grad
        norm_grad_ref[...] += norm_grad


def combine(length, experts, slot_column, made, back, hidden, upstream, second, route_probs, norm_params, router_wide, waits=()):
    images, _, width = hidden.shape
    low, wide = jnp.bfloat16, jnp.float32

    def per_image(*shape):
        return pl.BlockSpec((1,) + shape, lambda i: (i,) + (0,) * len(shape))

    def whole(array):
        return pl.BlockSpec(array.shape, lambda i: (0,) * array.ndim)

    small = pl.BlockSpec((8, width), lambda i: (0, 0))
    return pl.pallas_call(
        partial(combine_kernel, experts, len(waits)),
        grid=(images,),
        in_specs=[
            per_image(PAD, 128), whole(made), whole(back), per_image(PAD, width), per_image(PAD, width),
            per_image(PAD, width), per_image(PAD, 128), whole(norm_params), whole(router_wide),
        ]
        + [pl.BlockSpec(memory_space=pl.ANY)] * len(waits),
        out_specs=[per_image(length, width), per_image(PAD, width), small, small],
        out_shape=[
            jax.ShapeDtypeStruct((images, length, width), low),
            jax.ShapeDtypeStruct((images, PAD, width), wide),
            jax.ShapeDtypeStruct((8, width), wide),
            jax.ShapeDtypeStruct((8, width), wide),
        ],
        compiler_params=kernel_params(48),
        cost_estimate=cost(4 * images * PAD * experts * made.shape[1] * width, 2e7),
        name="combine",
    )(slot_column, made, back, hidden, upstream, second, route_probs, norm_params, router_wide, *waits)


def attend_back_kernel(
    first, last, waits, input_ref, norm_ref, dense_ref, normed_ref, projected_ref, probs_ref,
    context_ref, grad_ref, *refs
):
    low = jnp.bfloat16
    image, images = pl.program_id(0), pl.num_programs(0)
    if not first:
        sums_in, norm_grad_in, _ = refs[:3]
        refs = refs[3:]
    refs = refs[waits:]
    input_grad_ref, norm_grad_ref = refs[:2]
    if last:
        keep_ref, give_ref, sums, low_sums, sems = refs[2:]
    else:
        sums = refs[2]

    @pl.when(image == 0)
    def _():
        if first:
            sums[...] = jnp.zeros_like(sums)
            norm_grad_ref[...] = jnp.zeros_like(norm_grad_ref)
        else:
            sums[...] = sums_in[...]
            norm_grad_ref[...] = norm_grad_in[...]

    hidden_grad = grad_ref[0]
    width = hidden_grad.shape[1]
    attended_low = hidden_grad.astype(low)
    context_grad = mm(attended_low, dense_ref[3]).astype(low)
    sums[3] += mm_rows(attended_low, context_ref[0])
    queries, key_rows, value_rows = projected_ref[0, 0], projected_ref[0, 1], projected_ref[0, 2]
    first_half = lax.broadcasted_iota(jnp.int32, (PAD, 2 * HEAD_DIM), 1) < HEAD_DIM
    zero = jnp.zeros((PAD, 2 * HEAD_DIM), low)
    scale = HEAD_DIM ** (-0.5)
    parts = [[], [], []]
    for pair in range(width // (2 * HEAD_DIM)):
        at = slice(pair * 2 * HEAD_DIM, (pair + 1) * 2 * HEAD_DIM)
        query, key, value, grad = queries[:, at], key_rows[:, at], value_rows[:, at], context_grad[:, at]
        halves = []
        for side in range(2):
            mine = jnp.where(first_half == (side == 0), grad, zero)
            probs = probs_ref[0, 2 * pair + side]
            wide = probs.astype(jnp.float32)
            prob_grad = mm_turned(mine, value)
            weighted = wide * prob_grad
            score_grad = (
                weighted - wide * jnp.sum(weighted, axis=-1, keepdims=True)
            ).astype(low)
            halves.append(
                (mm(score_grad, key) * scale, mm_rows(score_grad, query) * scale, mm_rows(probs, grad))
            )
        for kind in range(3):
            parts[kind].append(jnp.where(first_half, halves[0][kind], halves[1][kind]).astype(low))
    normed = normed_ref[0]
    normed_grad = None
    for kind in range(3):
        projected_grad = jnp.concatenate(parts[kind], axis=1)
        sums[kind] += mm_rows(normed, projected_grad)
        part = mm_turned(projected_grad, dense_ref[kind])
        normed_grad = part if normed_grad is None else normed_grad + part
    unit, inverse = unit_of(input_ref[0].astype(jnp.float32))
    length = input_grad_ref.shape[1]
    normed_grad = normed_grad[:length]
    input_grad_ref[0] = hidden_grad[:length] + unit_backward(normed_grad, unit, inverse, norm_ref[0:1])
    gain = jnp.sum(normed_grad * unit, axis=0, keepdims=True)
    bias = jnp.sum(normed_grad, axis=0, keepdims=True)
    rows_of = lax.broadcasted_iota(jnp.int32, (8, width), 0)
    norm_grad_ref[...] += jnp.where(rows_of == 0, gain, jnp.where(rows_of == 1, bias, 0.0))

    if not last:
        return

    @pl.when(image == images - 1)
    def _():
        near, kinds, rows, columns = keep_ref.shape
        shards = near * 2 // GROUPS
        low_sums[...] = sums[...].astype(low)
        copies = []
        for piece in range(2 * near):
            target = keep_ref if piece < near else give_ref
            copies.append(
                pltpu.make_async_copy(
                    dense_window(low_sums, piece, shards, rows, columns),
                    target.at[piece % near],
                    sems.at[piece],
                )
            )
        for copy in copies:
            copy.start()
        for copy in copies:
            copy.wait()


def attend_back(which, count, block_input, norm_params, dense, kept, hidden_grad, carried, near_shape, waits=()):
    images, length, width = block_input.shape
    heads = width // HEAD_DIM
    low, wide = jnp.bfloat16, jnp.float32
    first, last = carried is None, which + count == images

    def per_image(*shape):
        return pl.BlockSpec((1,) + shape, lambda i: (i + which,) + (0,) * len(shape))

    def whole(array):
        return pl.BlockSpec(array.shape, lambda i: (0,) * array.ndim)

    anywhere = pl.BlockSpec(memory_space=pl.ANY)
    small = pl.BlockSpec((8, width), lambda i: (0, 0))
    sum_shape = (4, width, width)
    given = () if first else tuple(carried)
    out_specs = [per_image(length, width), small]
    out_shape = [
        jax.ShapeDtypeStruct((images, length, width), wide),
        jax.ShapeDtypeStruct((8, width), wide),
    ]
    scratch = []
    if last:
        out_specs += [anywhere] * 2
        out_shape += [jax.ShapeDtypeStruct(near_shape, low)] * 2
        scratch = [
            pltpu.VMEM(sum_shape, wide),
            pltpu.VMEM(sum_shape, low),
            pltpu.SemaphoreType.DMA((2 * near_shape[0],)),
        ]
    else:
        out_specs += [pl.BlockSpec(sum_shape, lambda i: (0, 0, 0))]
        out_shape += [jax.ShapeDtypeStruct(sum_shape, wide)]
    given_specs = [] if first else [whole(carried[0]), small, anywhere]
    return pl.pallas_call(
        partial(attend_back_kernel, first, last, len(waits)),
        grid=(count,),
        in_specs=[
            per_image(length, width), whole(norm_params), whole(dense),
            per_image(PAD, width), per_image(3, PAD, width), per_image(heads, PAD, PAD),
            per_image(PAD, width), per_image(PAD, width),
        ]
        + given_specs
        + [anywhere] * len(waits),
        out_specs=out_specs,
        out_shape=out_shape,
        scratch_shapes=scratch,
        input_output_aliases={} if first else {10: 0},
        compiler_params=kernel_params(56),
        cost_estimate=cost(count * 5e9, count * 6e6),
        name="attend_back",
    )(block_input, norm_params, dense, *kept, hidden_grad, *given, *waits)


def relay(block, axis, mask):
    size = lax.axis_size(axis)
    return lax.ppermute(block, axis, [(i, i ^ mask) for i in range(size)])


def relay_core(block):
    return relay(block, "head", 1)


def relay_x(block):
    return relay(block, "head", 2)


def relay_y(block):
    return relay(block, "tensor", 1)


def relay_both(block):
    heads, tensors = lax.axis_size("head"), lax.axis_size("tensor")
    pairs = [
        (h * tensors + t, (h ^ 2) * tensors + (t ^ 1)) for h in range(heads) for t in range(tensors)
    ]
    return lax.ppermute(block, ("head", "tensor"), pairs)


def relay_line(blocks):
    return [relay(block, "shard", k + 1) for k, block in enumerate(blocks)]


def ordered(values, *others):
    return lax.optimization_barrier((values, others))[0]


def wide_sum(*parts):
    return sum(p.astype(jnp.float32) for p in parts)


def local_plan(
    block_input,
    cotangent,
    routes,
    priority,
    norm_params,
    norm_moment,
    norm_square,
    qkv_weight,
    qkv_moment,
    qkv_square,
    attn_weight,
    attn_moment,
    attn_square,
    router_weight,
    router_moment,
    router_square,
    expert_in,
    in_moment,
    in_square,
    expert_out,
    out_moment,
    out_square,
):
    images, length, model_width = block_input.shape
    shards = experts = lax.axis_size("shard")
    capacity = 9 * images * length // (4 * experts)
    slots = -(-capacity // SLOT_PAD) * SLOT_PAD
    low = jnp.bfloat16

    dense_low = jnp.concatenate(
        [qkv_weight.transpose(1, 0, 2), attn_weight.T[None]], axis=0
    ).astype(low)
    dense_column = jnp.stack([dense_low] + relay_line([dense_low] * (shards - 1)))
    expert_low = jnp.stack([expert_in[0], expert_out[0].T]).astype(low)
    edges = [expert_low.shape[2] * edge // CUTS[-1] for edge in CUTS]
    chunks = [expert_low[:, :, i:j] for i, j in zip(edges, edges[1:])]
    tables = slot_tables(routes, priority)
    router_wide = jnp.pad(router_weight, ((0, 0), (0, 128 - experts))).astype(low)

    def line_of(block):
        return jnp.stack([block] + relay_line([block] * (shards - 1)))

    def across(column):
        return (relay_x(column), relay_y(column), relay_both(column))

    dense_column, tables, chunks[0] = ordered((dense_column, tables, chunks[0]))
    dense_sides, dense_far = across(dense_column), (relay_core(dense_column),)
    column = line_of(chunks[0])
    later = lax.all_gather(chunks[1], ("shard", "head", "tensor"))
    slot_row, slot_column = find_slots(tables, experts, capacity)
    slot_column = slot_column.reshape(images, PAD, 128)
    dense_sides, dense_far, slot_row = ordered((dense_sides, dense_far, slot_row))
    dense_far += tuple(relay_core(s) for s in dense_sides)
    dense = join_dense((dense_column, *dense_sides, *dense_far), model_width)

    half = shards // 2
    column, dense = ordered((column, dense))
    over_x, over_y, far_column = relay_x(column), relay_y(column), relay_core(column)
    normed, projected, probs, context, hidden, second, route_probs, upstream = attend(
        experts, block_input, cotangent, norm_params, dense, router_wide
    )

    over_x, over_y, far_column, second = ordered((over_x, over_y, far_column, second))
    corners = (relay_y(over_x[:half]), relay_x(over_y[half:]))
    near, far = (column, over_x, over_y), (far_column, relay_core(over_x), relay_core(over_y))
    tokens = images * PAD
    slot_rows = dispatch(
        slot_row, second.reshape(tokens, model_width), upstream.reshape(tokens, model_width),
        route_probs.reshape(tokens, 128), experts, slots,
    )

    corners, far, slot_rows = ordered((corners, far, slot_rows))
    weights_a = (*near, *corners, *far, *(relay_core(c) for c in corners))
    quarter = shards

    class Returning:
        def __init__(self, keep, give):
            self.keep, self.come = keep, relay_core(give)

        def some(self, first, count):
            at = slice(first, first + count)
            return wide_sum(self.keep[at], self.come[at])

        def part(self, k):
            return self.some(k * quarter, quarter)

        def across(self):
            x, y, both = (self.part(k).astype(low) for k in (1, 2, 3))
            self.over = (relay_x(x), relay_y(y), relay_both(both))

        def corner(self):
            half = quarter // 2
            self.corners = (
                relay_x(self.some(3 * quarter, half).astype(low)),
                relay_y(self.some(3 * quarter + half, quarter - half).astype(low)),
            )

        def sides(self):
            half = quarter // 2
            over_x, over_y = self.part(1), self.part(2)
            from_x, from_y = (c.astype(jnp.float32) for c in self.corners)
            over_x = jnp.concatenate([over_x[:half], over_x[half:] + from_y])
            over_y = jnp.concatenate([over_y[:half] + from_x, over_y[half:]])
            self.over = (relay_x(over_x.astype(low)), relay_y(over_y.astype(low)))

        def line(self):
            total = self.part(0) + wide_sum(*self.over)
            self.own = total[0]
            self.others = relay_line([total[k].astype(low) for k in range(1, quarter)])

        def result(self):
            return self.own + wide_sum(*self.others)

    made, backed, keep, give = run_experts(*slot_rows, None, weights_a, False)

    made, keep, give, later = ordered((made, keep, give, later))
    sum_a = Returning(keep, give)
    sum_a.across()
    made, backed, keep, give = run_experts(*slot_rows, (made, backed), (later,), True)

    sum_a.over, made, keep, give = ordered((sum_a.over, made, keep, give))
    sum_a.line()
    sum_b = Returning(keep, give)
    block_output, hidden_grad, router_part, norm_two = combine(
        length, experts, slot_column, made, backed, hidden, upstream, second, route_probs,
        norm_params, router_wide,
    )

    sum_a.others, sum_b.keep, sum_b.come, hidden_grad = ordered(
        (sum_a.others, sum_b.keep, sum_b.come, hidden_grad)
    )
    sum_b.corner()
    kept = (normed, projected, probs, context)
    half = images // 2
    dense_shape = (4 * quarter, *dense_low.shape)
    input_grad, norm_one, dense_sums = attend_back(
        0, half, block_input, norm_params, dense, kept, hidden_grad, None, dense_shape
    )

    sum_b.corners, norm_one, dense_sums = ordered((sum_b.corners, norm_one, dense_sums))
    sum_b.sides()
    input_grad, norm_one, keep, give = attend_back(
        half, images - half, block_input, norm_params, dense, kept, hidden_grad,
        (dense_sums, norm_one, input_grad), dense_shape,
    )
    sum_b.over, norm_one, keep, give = ordered((sum_b.over, norm_one, keep, give))
    small = jnp.concatenate([(norm_one + norm_two)[:4], router_part[:experts]])

    def terms(value):
        high = value.astype(low)
        return jnp.stack([high, (value - high.astype(jnp.float32)).astype(low)])

    def value(terms):
        return terms[0].astype(jnp.float32) + terms[1].astype(jnp.float32)

    def with_small(block, two):
        flat = block.astype(low).reshape(-1, 128)
        return jnp.concatenate([flat, two.reshape(-1, 128)])

    def apart(message, shape):
        rows = math.prod(shape) // 128
        return message[:rows].reshape(shape), value(message[rows:].reshape((2,) + small.shape))

    two = terms(small)
    come, other = apart(relay_core(with_small(give, two)), give.shape)
    small = value(two) + other
    two = terms(small)

    def part(k):
        at = slice(k * quarter, (k + 1) * quarter)
        return wide_sum(keep[at], come[at])

    shape = (quarter,) + keep.shape[1:]
    messages = [with_small(part(k), two) for k in (1, 2, 3)]
    messages, sum_b.over = ordered((messages, sum_b.over))
    sum_b.line()
    arrived = [send(m) for m, send in zip(messages, (relay_x, relay_y, relay_both))]
    arrived, sum_b.own = ordered((arrived, sum_b.own))
    arrived = [apart(m, shape) for m in arrived]
    small = (value(two) + arrived[0][1]) + (arrived[1][1] + arrived[2][1])
    two = terms(small)
    total = part(0) + wide_sum(*(a for a, _ in arrived))
    others = [
        apart(m, shape[1:]) for m in relay_line([with_small(total[k], two) for k in range(1, quarter)])
    ]
    dense_sum = total[0] + wide_sum(*(a for a, _ in others))
    sums = [value(two)] + [s for _, s in others]
    while len(sums) > 1:
        sums = [a + b for a, b in zip(sums[::2], sums[1::2])]
    norm_grad, router_grad = sums[0][:4], sums[0][4:].T
    expert_sum = jnp.concatenate([r.result() for r in (sum_a, sum_b)], axis=2)
    in_grad, out_grad = expert_sum[0][None], ordered(expert_sum[1].T[None])
    qkv_grad, attn_grad = dense_sum[:3].transpose(1, 0, 2), dense_sum[3].T
    norm_new = adam_update(norm_params, norm_grad, norm_moment, norm_square, 0.25, 0.0)
    qkv_new = adam_update(
        qkv_weight, qkv_grad, qkv_moment, qkv_square, 1.3 * model_width ** (-0.5), DECAY_RATE
    )
    attn_new = adam_update(
        attn_weight, attn_grad, attn_moment, attn_square, 3.0 * model_width ** (-0.5), DECAY_RATE
    )
    router_new = adam_update(
        router_weight,
        router_grad,
        router_moment,
        router_square,
        0.75 * model_width ** (-0.5),
        DECAY_RATE,
    )
    in_new = adam_update(
        expert_in, in_grad, in_moment, in_square, 1.0 * model_width ** (-0.5), DECAY_RATE
    )
    out_new = adam_update(
        expert_out, out_grad, out_moment, out_square, 0.8 * experts * FF ** (-0.5), DECAY_RATE
    )
    return (
        block_output,
        input_grad,
        norm_new[0],
        norm_new[1],
        norm_new[2],
        qkv_new[0],
        qkv_new[1],
        qkv_new[2],
        attn_new[0],
        attn_new[1],
        attn_new[2],
        router_new[0],
        router_new[1],
        router_new[2],
        in_new[0],
        in_new[1],
        in_new[2],
        out_new[0],
        out_new[1],
        out_new[2],
    )


def solution(mesh):
    fits = mesh.shape["shard"] <= 4
    return jax.shard_map(
        local_plan if fits else slot_plan,
        mesh=mesh,
        in_specs=(
            P(("shard", "head", "tensor"), None, None),
            P(("shard", "head", "tensor"), None, None),
            P(("shard", "head", "tensor"), None, None),
            P(("shard", "head", "tensor"), None),
            P(),
            P(),
            P(),
            P(("shard", "tensor"), None, "head"),
            P(("shard", "tensor"), None, "head"),
            P(("shard", "tensor"), None, "head"),
            P("head", ("shard", "tensor")),
            P("head", ("shard", "tensor")),
            P("head", ("shard", "tensor")),
            P(),
            P(),
            P(),
            P("shard", "head", "tensor"),
            P("shard", "head", "tensor"),
            P("shard", "head", "tensor"),
            P("shard", "tensor", "head"),
            P("shard", "tensor", "head"),
            P("shard", "tensor", "head"),
        ),
        out_specs=(
            P(("shard", "head", "tensor"), None, None),
            P(("shard", "head", "tensor"), None, None),
            P(),
            P(),
            P(),
            P(("shard", "tensor"), None, "head"),
            P(("shard", "tensor"), None, "head"),
            P(("shard", "tensor"), None, "head"),
            P("head", ("shard", "tensor")),
            P("head", ("shard", "tensor")),
            P("head", ("shard", "tensor")),
            P(),
            P(),
            P(),
            P("shard", "head", "tensor"),
            P("shard", "head", "tensor"),
            P("shard", "head", "tensor"),
            P("shard", "tensor", "head"),
            P("shard", "tensor", "head"),
            P("shard", "tensor", "head"),
        ),
        check_vma=False,
    )
```

```python
import math
from functools import partial

import jax
import jax.numpy as jnp
from jax import lax
from jax.experimental import pallas as pl
from jax.experimental.pallas import tpu as pltpu
from jax.sharding import PartitionSpec as P

SHARD, HEAD, TENSOR = "shard", "head", "tensor"
HEAD_DIM = 64
FF = 2048
STEP = 10


EPS_NORM = 1e-06
BETA_ONE = 0.9
BETA_TWO = 0.999
ADAM_EPS = 1e-08
DECAY_RATE = 0.1


def norm_forward(values, gain_row, bias_row):
    center = jnp.mean(values, axis=-1, keepdims=True)
    shifted = values - center
    inverse = lax.rsqrt(jnp.mean(shifted * shifted, axis=-1, keepdims=True) + EPS_NORM)
    unit_rows = shifted * inverse
    return (unit_rows * gain_row + bias_row, unit_rows, inverse)


def norm_backward(grad_rows, unit_rows, inverse, gain_row):
    scaled = grad_rows * gain_row
    inner_grad = (
        scaled
        - jnp.mean(scaled, axis=-1, keepdims=True)
        - unit_rows * jnp.mean(scaled * unit_rows, axis=-1, keepdims=True)
    )
    return (
        inner_grad * inverse,
        jnp.sum(grad_rows * unit_rows, axis=0),
        jnp.sum(grad_rows, axis=0),
    )


def gelu_grad(pre_act, upstream):
    result, pullback = jax.vjp(partial(jax.nn.gelu, approximate=True), pre_act)
    return pullback(upstream)[0]


def adam_update(weight, gradient, moment, square, step_rate, decay_rate):
    moment_new = BETA_ONE * moment + (1.0 - BETA_ONE) * gradient
    square_new = BETA_TWO * square + (1.0 - BETA_TWO) * gradient * gradient
    first_hat = moment_new / (1.0 - BETA_ONE**STEP)
    second_hat = square_new / (1.0 - BETA_TWO**STEP)
    weight_new = weight - step_rate * (
        first_hat / (jnp.sqrt(second_hat) + ADAM_EPS) + decay_rate * weight
    )
    return (weight_new, moment_new, square_new)


def send_rows(parcel):
    copies = jnp.broadcast_to(
        parcel[:, None], (parcel.shape[0], lax.axis_size(TENSOR)) + parcel.shape[1:]
    )
    flat_copies = copies.reshape((-1,) + parcel.shape[1:])
    arrived = lax.all_to_all(
        flat_copies, (SHARD, TENSOR), split_axis=0, concat_axis=0, tiled=True
    )
    return arrived.reshape(copies.shape)


def return_rows(partial_rows):
    flat_rows = partial_rows.reshape((-1,) + partial_rows.shape[2:])
    arrived = lax.all_to_all(
        flat_rows.astype(jnp.bfloat16), (SHARD, TENSOR), split_axis=0, concat_axis=0, tiled=True
    ).astype(flat_rows.dtype)
    return jnp.sum(arrived.reshape(partial_rows.shape), axis=1)


def slot_plan(
    block_input,
    cotangent,
    routes,
    priority,
    norm_params,
    norm_moment,
    norm_square,
    qkv_weight,
    qkv_moment,
    qkv_square,
    attn_weight,
    attn_moment,
    attn_square,
    router_weight,
    router_moment,
    router_square,
    expert_in,
    in_moment,
    in_square,
    expert_out,
    out_moment,
    out_square,
):
    images, length, model_width = block_input.shape
    row_count = images * length
    local_experts = expert_in.shape[0]
    shards = lax.axis_size(SHARD)
    experts = local_experts * shards
    capacity = 9 * row_count // (4 * experts)
    score_scale = HEAD_DIM ** (-0.5)
    full_qkv, full_attn = (
        lax.all_gather(qkv_weight.astype(jnp.bfloat16), (SHARD, TENSOR), axis=0, tiled=True),
        lax.all_gather(attn_weight.astype(jnp.bfloat16), (SHARD, TENSOR), axis=1, tiled=True),
    )
    inputs = block_input.astype(jnp.float32).reshape(row_count, model_width)
    normed, unit_one, inverse_one = norm_forward(inputs, norm_params[0], norm_params[1])
    normed_low = normed.astype(jnp.bfloat16).reshape(images, length, model_width)
    gathered, hidden_in, hidden_out = (
        lax.all_gather(normed_low, HEAD, axis=0, tiled=True),
        lax.all_gather(expert_in.astype(jnp.bfloat16), HEAD, axis=1, tiled=True),
        lax.all_gather(expert_out.astype(jnp.bfloat16), HEAD, axis=2, tiled=True),
    )
    local_heads = full_qkv.shape[2] // HEAD_DIM
    all_images = gathered.shape[0]
    head_shape = (all_images, length, local_heads, HEAD_DIM)
    projected = jnp.einsum(
        "isd,dcn->iscn", gathered, full_qkv, preferred_element_type=jnp.float32
    ).astype(jnp.bfloat16)
    queries = projected[:, :, 0].reshape(head_shape)
    key_rows = projected[:, :, 1].reshape(head_shape)
    value_rows = projected[:, :, 2].reshape(head_shape)
    scores = (
        jnp.einsum("iqhe,ikhe->ihqk", queries, key_rows, preferred_element_type=jnp.float32)
        * score_scale
    )
    score_top = jnp.max(scores, axis=-1, keepdims=True)
    log_total = score_top + jnp.log(jnp.sum(jnp.exp(scores - score_top), axis=-1, keepdims=True))
    probs_low = jnp.exp(scores - log_total).astype(jnp.bfloat16)
    context = jnp.einsum(
        "ihqk,ikhe->iqhe", probs_low, value_rows, preferred_element_type=jnp.float32
    ).astype(jnp.bfloat16)
    context = context.reshape(all_images * length, local_heads * HEAD_DIM)
    attended = lax.psum_scatter(
        jnp.dot(context, full_attn, preferred_element_type=jnp.float32).astype(jnp.bfloat16),
        HEAD,
        scatter_dimension=0,
        tiled=True,
    ).astype(jnp.float32)
    hidden = inputs + attended
    normed_two, unit_two, inverse_two = norm_forward(hidden, norm_params[2], norm_params[3])
    second_low = normed_two.astype(jnp.bfloat16)
    router_low = router_weight.astype(jnp.bfloat16)
    logits = jnp.dot(second_low, router_low, preferred_element_type=jnp.float32)
    route_probs = jax.nn.softmax(logits, axis=-1)
    route_hot = (
        routes.reshape(row_count, 2)[:, :, None]
        == jnp.arange(experts, dtype=jnp.int32)[None, None, :]
    ).astype(jnp.float32)
    gate_values = jnp.sum(route_probs[:, None, :] * route_hot, axis=-1)
    expert_ids = routes.reshape(2 * row_count)
    rank_values = priority[0]
    pair_hot = route_hot.reshape(2 * row_count, experts)
    earlier = (rank_values[None, :] < rank_values[:, None]).astype(jnp.bfloat16)
    counts = jnp.dot(earlier, pair_hot.astype(jnp.bfloat16), preferred_element_type=jnp.float32)
    slot_index = jnp.sum(counts * pair_hot, axis=1).astype(jnp.int32)
    target = jnp.where(
        slot_index < capacity, expert_ids * capacity + slot_index, experts * capacity
    )
    filler = jnp.full((experts * capacity,), 2 * row_count, jnp.int32)
    owner_pair = filler.at[target].set(jnp.arange(2 * row_count, dtype=jnp.int32), mode="drop")
    padded = jnp.concatenate([second_low, jnp.zeros((1, model_width), jnp.bfloat16)], axis=0)
    parcel = padded[owner_pair // 2].reshape(shards, local_experts, capacity, model_width)
    arrived = send_rows(parcel)
    pre_act = jnp.einsum("stecd,edf->stecf", arrived, hidden_in, preferred_element_type=jnp.float32)
    active = jax.nn.gelu(pre_act, approximate=True).astype(jnp.bfloat16)
    part_rows = jnp.einsum(
        "stecf,efd->stecd", active, hidden_out, preferred_element_type=jnp.float32
    )
    expert_rows = return_rows(part_rows).reshape(experts * capacity, model_width)
    padded_out = jnp.concatenate([expert_rows, jnp.zeros((1, model_width), jnp.float32)], axis=0)
    per_pair = padded_out[target].reshape(row_count, 2, model_width)
    block_sum = hidden + jnp.sum(gate_values[:, :, None] * per_pair, axis=1)
    block_output = block_sum.astype(jnp.bfloat16).reshape(images, length, model_width)
    upstream = cotangent.astype(jnp.float32).reshape(row_count, model_width)
    pair_grad = (
        (gate_values[:, :, None] * upstream[:, None, :])
        .astype(jnp.bfloat16)
        .reshape(2 * row_count, model_width)
    )
    gate_grad = jnp.sum(upstream[:, None, :] * per_pair, axis=-1)
    padded_grad = jnp.concatenate([pair_grad, jnp.zeros((1, model_width), jnp.bfloat16)], axis=0)
    grad_parcel = padded_grad[owner_pair].reshape(shards, local_experts, capacity, model_width)
    grad_arrived = send_rows(grad_parcel)
    grad_out_part = jnp.einsum(
        "stecf,stecd->efd", active, grad_arrived, preferred_element_type=jnp.float32
    )
    active_grad = jnp.einsum(
        "stecd,efd->stecf", grad_arrived, hidden_out, preferred_element_type=jnp.float32
    )
    pre_grad = gelu_grad(pre_act, active_grad).astype(jnp.bfloat16)
    grad_in_part = jnp.einsum(
        "stecd,stecf->edf", arrived, pre_grad, preferred_element_type=jnp.float32
    )
    row_grad = jnp.einsum(
        "stecf,edf->stecd", pre_grad, hidden_in, preferred_element_type=jnp.float32
    )
    slot_grad = return_rows(row_grad).reshape(experts * capacity, model_width)
    padded_slot = jnp.concatenate([slot_grad, jnp.zeros((1, model_width), jnp.float32)], axis=0)
    second_grad = jnp.sum(padded_slot[target].reshape(row_count, 2, model_width), axis=1)
    prob_sum = jnp.sum(gate_grad[:, :, None] * route_hot, axis=1)
    logit_grad = (
        route_probs * (prob_sum - jnp.sum(route_probs * prob_sum, axis=-1, keepdims=True))
    ).astype(jnp.bfloat16)
    router_grad = jnp.einsum(
        "rd,re->de", second_low, logit_grad, preferred_element_type=jnp.float32
    )
    second_grad = second_grad + jnp.einsum(
        "re,de->rd", logit_grad, router_low, preferred_element_type=jnp.float32
    )
    hidden_part, gain_two, bias_two = norm_backward(
        second_grad, unit_two, inverse_two, norm_params[2]
    )
    hidden_grad = upstream + hidden_part
    attended_grad = lax.all_gather(hidden_grad.astype(jnp.bfloat16), HEAD, axis=0, tiled=True)
    attn_grad = jnp.einsum("rn,rd->nd", context, attended_grad, preferred_element_type=jnp.float32)
    context_grad = jnp.einsum(
        "rd,nd->rn", attended_grad, full_attn, preferred_element_type=jnp.float32
    ).astype(jnp.bfloat16)
    context_grad = context_grad.reshape(head_shape)
    scores_again = (
        jnp.einsum("iqhe,ikhe->ihqk", queries, key_rows, preferred_element_type=jnp.float32)
        * score_scale
    )
    probs_full = jnp.exp(scores_again - log_total)
    prob_grad = jnp.einsum(
        "iqhe,ikhe->ihqk", context_grad, value_rows, preferred_element_type=jnp.float32
    )
    score_grad = (
        probs_full * (prob_grad - jnp.sum(probs_full * prob_grad, axis=-1, keepdims=True))
    ).astype(jnp.bfloat16)
    query_grad = (
        jnp.einsum("ihqk,ikhe->iqhe", score_grad, key_rows, preferred_element_type=jnp.float32)
        * score_scale
    )
    key_grad = (
        jnp.einsum("ihqk,iqhe->ikhe", score_grad, queries, preferred_element_type=jnp.float32)
        * score_scale
    )
    value_grad = jnp.einsum(
        "ihqk,iqhe->ikhe", probs_low, context_grad, preferred_element_type=jnp.float32
    )
    projected_grad = (
        jnp.stack([query_grad, key_grad, value_grad], axis=2)
        .reshape(all_images, length, 3, local_heads * HEAD_DIM)
        .astype(jnp.bfloat16)
    )
    qkv_grad = jnp.einsum(
        "isd,iscn->dcn", gathered, projected_grad, preferred_element_type=jnp.float32
    )
    normed_part = jnp.einsum(
        "iscn,dcn->isd", projected_grad, full_qkv, preferred_element_type=jnp.float32
    )
    normed_grad, in_grad, out_grad = (
        lax.psum_scatter(
            normed_part.astype(jnp.bfloat16), HEAD, scatter_dimension=0, tiled=True
        ).astype(jnp.float32),
        lax.psum_scatter(
            grad_in_part.astype(jnp.bfloat16), HEAD, scatter_dimension=1, tiled=True
        ).astype(jnp.float32),
        lax.psum_scatter(
            grad_out_part.astype(jnp.bfloat16), HEAD, scatter_dimension=2, tiled=True
        ).astype(jnp.float32),
    )
    input_part, gain_one, bias_one = norm_backward(
        normed_grad.reshape(row_count, model_width), unit_one, inverse_one, norm_params[0]
    )
    input_grad = (hidden_grad + input_part).reshape(images, length, model_width)
    norm_grad = jnp.stack([gain_one, bias_one, gain_two, bias_two])
    norm_grad, router_grad = lax.psum((norm_grad, router_grad), (SHARD, HEAD, TENSOR))
    qkv_grad, attn_grad = (
        lax.psum_scatter(qkv_grad, (SHARD, TENSOR), scatter_dimension=0, tiled=True),
        lax.psum_scatter(attn_grad, (SHARD, TENSOR), scatter_dimension=1, tiled=True),
    )
    norm_new = adam_update(norm_params, norm_grad, norm_moment, norm_square, 0.25, 0.0)
    qkv_new = adam_update(
        qkv_weight, qkv_grad, qkv_moment, qkv_square, 1.3 * model_width ** (-0.5), DECAY_RATE
    )
    attn_new = adam_update(
        attn_weight, attn_grad, attn_moment, attn_square, 3.0 * model_width ** (-0.5), DECAY_RATE
    )
    router_new = adam_update(
        router_weight,
        router_grad,
        router_moment,
        router_square,
        0.75 * model_width ** (-0.5),
        DECAY_RATE,
    )
    in_new = adam_update(
        expert_in, in_grad, in_moment, in_square, 1.0 * model_width ** (-0.5), DECAY_RATE
    )
    out_new = adam_update(
        expert_out, out_grad, out_moment, out_square, 0.8 * experts * FF ** (-0.5), DECAY_RATE
    )
    return (
        block_output,
        input_grad,
        norm_new[0],
        norm_new[1],
        norm_new[2],
        qkv_new[0],
        qkv_new[1],
        qkv_new[2],
        attn_new[0],
        attn_new[1],
        attn_new[2],
        router_new[0],
        router_new[1],
        router_new[2],
        in_new[0],
        in_new[1],
        in_new[2],
        out_new[0],
        out_new[1],
        out_new[2],
    )


PAD = 208
SLOT_PAD = 16
CUTS = (0, 3, 8)


def kernel_params(megabytes):
    return pltpu.CompilerParams(vmem_limit_bytes=megabytes << 20)


def cost(flops, moved):
    return pl.CostEstimate(flops=int(flops), bytes_accessed=int(moved), transcendentals=0)


def mm(left, right):
    return lax.dot_general(left, right, (((1,), (0,)), ((), ())), preferred_element_type=jnp.float32)


def mm_turned(left, right):
    return lax.dot_general(left, right, (((1,), (1,)), ((), ())), preferred_element_type=jnp.float32)


def mm_rows(left, right):
    return lax.dot_general(left, right, (((0,), (0,)), ((), ())), preferred_element_type=jnp.float32)


def unit_of(values):
    center = jnp.mean(values, axis=-1, keepdims=True)
    shifted = values - center
    inverse = lax.rsqrt(jnp.mean(shifted * shifted, axis=-1, keepdims=True) + EPS_NORM)
    return (shifted * inverse, inverse)


def unit_backward(grad_rows, unit_rows, inverse, gain_row):
    scaled = grad_rows * gain_row
    inner_grad = (
        scaled
        - jnp.mean(scaled, axis=-1, keepdims=True)
        - unit_rows * jnp.mean(scaled * unit_rows, axis=-1, keepdims=True)
    )
    return inner_grad * inverse


def absolute(group):
    tensor = lax.axis_index(TENSOR) ^ (group // 2 % 2)
    head = lax.axis_index(HEAD) ^ (2 * (group % 2) + group // 4)
    return tensor, head


GROUPS = 8


def slot_kernel(experts, capacity, row_ref, column_ref, slot_row_ref, slot_column_ref):
    none = 1 << 20
    tokens = row_ref.shape[1]
    lanes = lax.broadcasted_iota(jnp.int32, (PAD, 128), 1)
    rows_of = lax.broadcasted_iota(jnp.int32, (8, tokens), 0)

    def ranks(named, rank, expert):
        return jnp.where(
            named[0] == expert, rank[0], jnp.where(named[1] == expert, rank[1], none)
        )

    routes_row, ranks_row = (row_ref[0:1], row_ref[1:2]), (row_ref[2:3], row_ref[3:4])
    all_rows = jnp.full((8, tokens), -1, jnp.int32)
    row_of = [ranks(routes_row, ranks_row, e) for e in range(experts)]
    totals = [jnp.zeros((1, tokens), jnp.float32) for e in range(experts)]
    for block in range(tokens // PAD):
        part = column_ref[block * PAD : (block + 1) * PAD]
        routes_col, ranks_col = (part[:, 0:1], part[:, 1:2]), (part[:, 2:3], part[:, 3:4])
        result = jnp.full((PAD, 128), -1, jnp.int32)
        for e in range(experts):
            column = ranks(routes_col, ranks_col, e)
            totals[e] = totals[e] + jnp.sum(
                jnp.where(column < row_of[e], 1.0, 0.0), axis=0, keepdims=True
            )
            before = jnp.sum(
                jnp.where(row_of[e] < column, 1.0, 0.0), axis=1, keepdims=True
            ).astype(jnp.int32)
            slot = jnp.where((column < none) & (before < capacity), before, -1)
            result = jnp.where(lanes == e, slot, result)
        slot_column_ref[block * PAD : (block + 1) * PAD] = result
    for e in range(experts):
        before = totals[e].astype(jnp.int32)
        slot = jnp.where((row_of[e] < none) & (before < capacity), before, -1)
        all_rows = jnp.where(rows_of == e, slot, all_rows)
    slot_row_ref[...] = all_rows


def slot_tables(routes, priority):
    images, length, _ = routes.shape
    tokens = images * PAD
    table = jnp.concatenate([routes, priority.reshape(images, length, 2)], axis=2)
    table = jnp.pad(table, ((0, 0), (0, PAD - length), (0, 0)), constant_values=-1)
    table = table.reshape(tokens, 4)
    columns = jnp.pad(table, ((0, 0), (0, 4)))
    return (columns.T, columns)


def find_slots(tables, experts, capacity):
    tokens = tables[1].shape[0]
    return pl.pallas_call(
        partial(slot_kernel, experts, capacity),
        out_shape=(
            jax.ShapeDtypeStruct((8, tokens), jnp.int32),
            jax.ShapeDtypeStruct((tokens, 128), jnp.int32),
        ),
        compiler_params=kernel_params(32),
        cost_estimate=cost(1e10, 1e6),
        name="find_slots",
    )(*tables)


def dense_window(ref, piece, shards, rows, columns):
    tensor, head = absolute(piece // shards)
    shard = lax.axis_index(SHARD) ^ (piece % shards)
    down = pl.multiple_of((shard * lax.axis_size(TENSOR) + tensor) * rows, rows)
    over = pl.multiple_of(head * columns, columns)
    return ref.at[:, pl.ds(down, rows), pl.ds(over, columns)]


def dense_kernel(*refs):
    groups, (full_ref, sems) = refs[:GROUPS], refs[GROUPS:]
    shards, kinds, rows, columns = groups[0].shape
    copies = []
    for piece in range(GROUPS * shards):
        copies.append(
            pltpu.make_async_copy(
                groups[piece // shards].at[piece % shards],
                dense_window(full_ref, piece, shards, rows, columns),
                sems.at[piece],
            )
        )
    for copy in copies:
        copy.start()
    for copy in copies:
        copy.wait()


def join_dense(groups, model_width):
    shards, kinds = groups[0].shape[:2]
    return pl.pallas_call(
        dense_kernel,
        out_shape=jax.ShapeDtypeStruct((kinds, model_width, model_width), groups[0].dtype),
        in_specs=[pl.BlockSpec(memory_space=pl.ANY)] * GROUPS,
        out_specs=pl.BlockSpec(memory_space=pltpu.VMEM),
        scratch_shapes=[pltpu.SemaphoreType.DMA((GROUPS * shards,))],
        compiler_params=kernel_params(16),
        cost_estimate=cost(1e6, 4e6),
        name="join_dense",
    )(*groups)


def attend_kernel(
    length, experts, input_ref, cotangent_ref, norm_ref, dense_ref, router_ref,
    normed_ref, projected_ref, probs_ref, context_ref, hidden_ref, second_ref, route_ref, upstream_ref, whole,
):
    low = jnp.bfloat16
    whole[length // 8 * 8 :] = jnp.zeros_like(whole[length // 8 * 8 :])
    whole[:length] = cotangent_ref[0].astype(jnp.float32)
    upstream_ref[0] = whole[...].astype(low)
    whole[:length] = input_ref[0].astype(jnp.float32)
    values = whole[...]
    width = values.shape[1]
    unit, _ = unit_of(values)
    normed = (unit * norm_ref[0:1] + norm_ref[1:2]).astype(low)
    normed_ref[0] = normed
    queries, key_rows, value_rows = (mm(normed, dense_ref[c]).astype(low) for c in range(3))
    projected_ref[0, 0] = queries
    projected_ref[0, 1] = key_rows
    projected_ref[0, 2] = value_rows
    first_half = lax.broadcasted_iota(jnp.int32, (PAD, 2 * HEAD_DIM), 1) < HEAD_DIM
    is_key = lax.broadcasted_iota(jnp.int32, (PAD, PAD), 1) < length
    zero = jnp.zeros((PAD, 2 * HEAD_DIM), low)
    pairs = []
    for pair in range(width // (2 * HEAD_DIM)):
        at = slice(pair * 2 * HEAD_DIM, (pair + 1) * 2 * HEAD_DIM)
        query, key, value = queries[:, at], key_rows[:, at], value_rows[:, at]
        halves = []
        for side in range(2):
            mine = jnp.where(first_half == (side == 0), query, zero)
            scores = mm_turned(mine, key) * (HEAD_DIM ** (-0.5))
            scores = jnp.where(is_key, scores, -1e30)
            top = jnp.max(scores, axis=-1, keepdims=True)
            raised = jnp.exp(scores - top)
            probs = (raised / jnp.sum(raised, axis=-1, keepdims=True)).astype(low)
            probs_ref[0, 2 * pair + side] = probs
            halves.append(mm(probs, value))
        pairs.append(jnp.where(first_half, halves[0], halves[1]).astype(low))
    context = jnp.concatenate(pairs, axis=1)
    context_ref[0] = context
    hidden = values + mm_turned(context, dense_ref[3])
    hidden_ref[0] = hidden
    unit, _ = unit_of(hidden)
    second = (unit * norm_ref[2:3] + norm_ref[3:4]).astype(low)
    second_ref[0] = second
    logits = mm(second, router_ref[...])
    is_expert = lax.broadcasted_iota(jnp.int32, logits.shape, 1) < experts
    logits = jnp.where(is_expert, logits, -1e30)
    raised = jnp.exp(logits - jnp.max(logits, axis=-1, keepdims=True))
    route_ref[0] = raised / jnp.sum(raised, axis=-1, keepdims=True)


def attend(experts, block_input, cotangent, norm_params, dense, router_wide):
    images, length, width = block_input.shape
    heads = width // HEAD_DIM
    low, wide = jnp.bfloat16, jnp.float32

    def per_image(*shape):
        return pl.BlockSpec((1,) + shape, lambda i: (i,) + (0,) * len(shape))

    def whole(array):
        return pl.BlockSpec(array.shape, lambda i: (0,) * array.ndim)

    shapes = [
        ((PAD, width), low), ((3, PAD, width), low), ((heads, PAD, PAD), low), ((PAD, width), low),
        ((PAD, width), wide), ((PAD, width), low), ((PAD, 128), wide), ((PAD, width), low),
    ]
    return pl.pallas_call(
        partial(attend_kernel, length, experts),
        grid=(images,),
        in_specs=[per_image(length, width)] * 2 + [whole(norm_params), whole(dense), whole(router_wide)],
        out_specs=[per_image(*s) for s, _ in shapes],
        out_shape=[jax.ShapeDtypeStruct((images,) + s, t) for s, t in shapes],
        scratch_shapes=[pltpu.VMEM((PAD, width), wide)],
        compiler_params=kernel_params(48),
        cost_estimate=cost(images * 2.5e9, images * 5e6),
        name="attend",
    )(block_input, cotangent, norm_params, dense, router_wide)


def dispatch_kernel(waits, slot_ref, second_ref, upstream_ref, route_ref, *refs):
    x_ref, g_ref, xt_ref, gt_ref = refs[waits:]
    low = jnp.bfloat16
    expert = pl.program_id(0)
    slots, tokens = x_ref.shape[1], second_ref.shape[0]
    rows_of = lax.broadcasted_iota(jnp.int32, (8, tokens), 0)
    slot_row = jnp.max(jnp.where(rows_of == expert, slot_ref[...], -1), axis=0, keepdims=True)
    hot = lax.broadcasted_iota(jnp.int32, (slots, tokens), 0) == slot_row
    hot = jnp.where(hot, 1.0, 0.0).astype(low)
    lanes = lax.broadcasted_iota(jnp.int32, (tokens, 128), 1)
    gate = jnp.sum(jnp.where(lanes == expert, route_ref[...], 0.0), axis=1, keepdims=True)
    pair_grad = (gate * upstream_ref[...].astype(jnp.float32)).astype(low)
    rows = mm(hot, second_ref[...]).astype(low)
    x_ref[0] = rows
    xt_ref[0] = rows.T
    rows = mm(hot, pair_grad).astype(low)
    g_ref[0] = rows
    gt_ref[0] = rows.T


def dispatch(slot_row, second, upstream, route_probs, experts, slots, waits=()):
    tokens, width = second.shape

    def whole(array):
        return pl.BlockSpec(array.shape, lambda e: (0,) * array.ndim)

    flat = pl.BlockSpec((1, slots, width), lambda e: (e, 0, 0))
    turned = pl.BlockSpec((1, width, slots), lambda e: (e, 0, 0))
    low = jnp.bfloat16
    return pl.pallas_call(
        partial(dispatch_kernel, len(waits)),
        grid=(experts,),
        in_specs=[whole(a) for a in (slot_row, second, upstream, route_probs)]
        + [pl.BlockSpec(memory_space=pl.ANY)] * len(waits),
        out_specs=[flat, flat, turned, turned],
        out_shape=[jax.ShapeDtypeStruct((experts, slots, width), low)] * 2
        + [jax.ShapeDtypeStruct((experts, width, slots), low)] * 2,
        compiler_params=kernel_params(48),
        cost_estimate=cost(4 * slots * tokens * width * experts, 1e7),
        name="dispatch",
    )(slot_row, second, upstream, route_probs, *waits)


def expert_kernel(first, last, apart, count, x_ref, g_ref, xt_ref, gt_ref, *refs):
    low = jnp.bfloat16
    if not first:
        made_in, back_in = refs[:2]
        refs = refs[2:]
    sources, refs = refs[:count], refs[count:]
    made_ref, back_ref, *targets = refs[: 4 if apart else 3]
    if last:
        held, sent, in_sems, out_sems, made_sum, back_sum = refs[4 if apart else 3 :]
    else:
        held, sent, in_sems, out_sems = refs[4 if apart else 3 :]
        made_sum, back_sum = made_ref.at[0], back_ref.at[0]
    expert, experts = pl.program_id(0), pl.num_programs(0)
    _, kinds, rows, columns = sources[0].shape
    shards, heads, tensors = (lax.axis_size(a) for a in (SHARD, HEAD, TENSOR))
    half = shards // 2

    def window(ref, slot, group):
        tensor, head = absolute(group)
        down = pl.multiple_of(head * rows, rows)
        over = pl.multiple_of(tensor * columns, columns)
        return ref.at[slot, :, pl.ds(down, rows), pl.ds(over, columns)]

    def fetch(source, slot, group):
        return pltpu.make_async_copy(source, window(held, slot, group), in_sems.at[slot, group])

    def start_fetch(which, slot, group):
        if count == 1:
            tensor, head = absolute(group)
            fetch(sources[0].at[(which * heads + head) * tensors + tensor], slot, group).start()
            return
        z = which ^ lax.axis_index(SHARD)
        place = group % 4 + (group // 4) * 5
        if group % 4 < 3:
            fetch(sources[place].at[z], slot, group).start()
            return

        @pl.when(z < half)
        def _():
            fetch(sources[place].at[z], slot, group).start()

        @pl.when(z >= half)
        def _():
            fetch(sources[place + 1].at[z - half], slot, group).start()

    def put(which, slot, group):
        z = which ^ lax.axis_index(SHARD)
        if apart:
            target, place = targets[group // (GROUPS // 2)], group % (GROUPS // 2) * shards + z
        else:
            tensor, head = absolute(group)
            target, place = targets[0], (head * tensors + tensor) * shards + z
        return pltpu.make_async_copy(window(sent, slot, group), target.at[place], out_sems.at[slot, group])

    slot = lax.rem(expert, 2)

    @pl.when(expert == 0)
    def _():
        for group in range(GROUPS):
            start_fetch(0, 0, group)

    @pl.when(expert + 1 < experts)
    def _():
        for group in range(GROUPS):
            start_fetch(expert + 1, 1 - slot, group)

    for group in range(GROUPS):
        fetch(sources[0].at[0], slot, group).wait()

    @pl.when(expert >= 2)
    def _():
        for group in range(GROUPS):
            put(expert - 2, slot, group).wait()

    x, g, xt, gt = x_ref[0], g_ref[0], xt_ref[0], gt_ref[0]
    units = held.shape[3]
    tile = TILE if units % TILE == 0 else 256
    for unit in range(0, units, tile):
        at = slice(unit, unit + tile)
        w_in, w_out = held[slot, 0, :, at], held[slot, 1, :, at]
        v = mm(x, w_in)
        grad = mm(g, w_out)
        square = v * v
        tanh = jnp.tanh(v * (0.7978845608028654 + 0.035677408136300125 * square))
        half = 0.5 + 0.5 * tanh
        active = (v * half).astype(low)
        slope = half + v * (half * (1.0 - tanh)) * (
            0.7978845608028654 + 0.10703222440890037 * square
        )
        pre_grad = (grad * slope).astype(low)
        made = mm_turned(active, w_out)
        back = mm_turned(pre_grad, w_in)
        if unit > 0:
            made, back = made_sum[...] + made, back_sum[...] + back
        elif not first:
            made, back = made_in[0] + made, back_in[0] + back
        if last and unit + tile == units:
            made_ref[0], back_ref[0] = made.astype(low), back.astype(low)
        else:
            made_sum[...] = made
            back_sum[...] = back
        sent[slot, 0, :, at] = mm(xt, pre_grad).astype(low)
        sent[slot, 1, :, at] = mm(gt, active).astype(low)
    for group in range(GROUPS):
        put(expert, slot, group).start()

    @pl.when(expert == experts - 1)
    def _():
        for group in range(GROUPS):
            put(expert - 1, 1 - slot, group).wait()
        for group in range(GROUPS):
            put(expert, slot, group).wait()


TILE = 256


def run_experts(x, g, xt, gt, sums, sources, last, apart):
    experts, slots, width = x.shape
    _, kinds, rows, columns = sources[0].shape
    shards = lax.axis_size(SHARD)
    units = GROUPS * rows * columns // width
    low = jnp.bfloat16
    flat = pl.BlockSpec((1, slots, width), lambda e: (e, 0, 0))
    turned = pl.BlockSpec((1, width, slots), lambda e: (e, 0, 0))
    anywhere = pl.BlockSpec(memory_space=pl.ANY)
    kept = low if last else jnp.float32
    first = sums is None
    given = () if first else tuple(sums)
    scratch = [
        pltpu.VMEM((2, kinds, width, units), low),
        pltpu.VMEM((2, kinds, width, units), low),
        pltpu.SemaphoreType.DMA((2, GROUPS)),
        pltpu.SemaphoreType.DMA((2, GROUPS)),
    ]
    if last:
        scratch += [pltpu.VMEM((slots, width), jnp.float32)] * 2
    return pl.pallas_call(
        partial(expert_kernel, first, last, apart, len(sources)),
        grid=(experts,),
        in_specs=[flat, flat, turned, turned] + [flat] * len(given) + [anywhere] * len(sources),
        out_specs=[flat, flat] + [anywhere] * (2 if apart else 1),
        out_shape=[jax.ShapeDtypeStruct((experts, slots, width), kept)] * 2
        + (
            [jax.ShapeDtypeStruct((GROUPS // 2 * shards, kinds, rows, columns), low)] * 2
            if apart
            else [jax.ShapeDtypeStruct((GROUPS * shards, kinds, rows, columns), low)]
        ),
        scratch_shapes=scratch,
        compiler_params=kernel_params(56),
        cost_estimate=cost(12 * experts * slots * width * units, 3e7),
        name="experts",
    )(x, g, xt, gt, *given, *sources)


def combine_kernel(
    experts, waits, slot_ref, made_ref, back_ref, hidden_ref, upstream_ref, second_ref, route_ref,
    norm_ref, router_ref, *refs
):
    output_ref, grad_ref, small_ref = refs[waits:]
    low = jnp.bfloat16
    image = pl.program_id(0)
    hidden = hidden_ref[0]
    upstream = upstream_ref[0].astype(jnp.float32)
    route_probs = route_ref[0]
    slots = made_ref.shape[1]
    lanes = lax.broadcasted_iota(jnp.int32, (PAD, slots), 1)
    wide_lanes = lax.broadcasted_iota(jnp.int32, (PAD, 128), 1)
    total = hidden
    second_grad = jnp.zeros_like(hidden)
    prob_sum = jnp.zeros((PAD, 128), jnp.float32)
    gates = route_probs
    for e in range(experts):
        hot = jnp.where(lanes == slot_ref[0][:, e : e + 1], 1.0, 0.0).astype(low)
        made = mm(hot, made_ref[e])
        second_grad = second_grad + mm(hot, back_ref[e])
        total = total + route_probs[:, e : e + 1] * made
        gate_grad = jnp.sum(upstream * made, axis=-1, keepdims=True)
        prob_sum = jnp.where(wide_lanes == e, gate_grad, prob_sum)
        gates = jnp.where(wide_lanes == experts + e, route_probs[:, e : e + 1], gates)
        prob_sum = jnp.where(wide_lanes == experts + e, gate_grad, prob_sum)
    length = output_ref.shape[1]
    output_ref[0] = total.astype(low)[:length]
    inner = jnp.sum(route_probs * prob_sum, axis=-1, keepdims=True)
    logit_grad = (gates * (prob_sum - inner)).astype(low)
    second_grad = second_grad + mm_turned(logit_grad, router_ref[...])
    unit, inverse = unit_of(hidden)
    grad_ref[0] = upstream + unit_backward(second_grad, unit, inverse, norm_ref[2:3])
    router_grad = mm_rows(logit_grad, second_ref[0])[:8]
    gain = jnp.sum(second_grad * unit, axis=0, keepdims=True)
    bias = jnp.sum(second_grad, axis=0, keepdims=True)
    rows_of = lax.broadcasted_iota(jnp.int32, (8, hidden.shape[1]), 0)
    small = jnp.where(
        rows_of == 2, gain, jnp.where(rows_of == 3, bias, jnp.where(rows_of >= experts, router_grad, 0.0))
    )

    @pl.when(image == 0)
    def _():
        small_ref[...] = small

    @pl.when(image > 0)
    def _():
        small_ref[...] += small


def combine(length, experts, slot_column, made, back, hidden, upstream, second, route_probs, norm_params, router_wide, waits=()):
    images, _, width = hidden.shape
    low, wide = jnp.bfloat16, jnp.float32

    def per_image(*shape):
        return pl.BlockSpec((1,) + shape, lambda i: (i,) + (0,) * len(shape))

    def whole(array):
        return pl.BlockSpec(array.shape, lambda i: (0,) * array.ndim)

    small = pl.BlockSpec((8, width), lambda i: (0, 0))
    return pl.pallas_call(
        partial(combine_kernel, experts, len(waits)),
        grid=(images,),
        in_specs=[
            per_image(PAD, 128), whole(made), whole(back), per_image(PAD, width), per_image(PAD, width),
            per_image(PAD, width), per_image(PAD, 128), whole(norm_params), whole(router_wide),
        ]
        + [pl.BlockSpec(memory_space=pl.ANY)] * len(waits),
        out_specs=[per_image(length, width), per_image(PAD, width), small],
        out_shape=[
            jax.ShapeDtypeStruct((images, length, width), low),
            jax.ShapeDtypeStruct((images, PAD, width), wide),
            jax.ShapeDtypeStruct((8, width), wide),
        ],
        compiler_params=kernel_params(48),
        cost_estimate=cost(4 * images * PAD * experts * made.shape[1] * width, 2e7),
        name="combine",
    )(slot_column, made, back, hidden, upstream, second, route_probs, norm_params, router_wide, *waits)


def regroup(rows):
    return jnp.concatenate([rows[:, k : k + 128] for k in range(0, rows.shape[1], 128)], axis=0)


def two_terms(value):
    high = value.astype(jnp.bfloat16).astype(jnp.float32)
    less = (value - high).astype(jnp.bfloat16).astype(jnp.float32)
    return jnp.concatenate([high, less], axis=0).astype(jnp.bfloat16), high + less


def term_sum(terms):
    terms = terms.astype(jnp.float32)
    half = terms.shape[0] // 2
    return terms[:half] + terms[half:]


def attend_back_kernel(
    first, last, input_ref, norm_ref, dense_ref, normed_ref, projected_ref, probs_ref,
    context_ref, grad_ref, norm_grad_in, *refs
):
    low = jnp.bfloat16
    image, images = pl.program_id(0), pl.num_programs(0)
    if not first:
        sums_in = refs[0]
        refs = refs[2:]
    input_grad_ref, norm_grad_ref = refs[:2]
    if last:
        keep_ref, give_ref, sums, low_sums, packed, sems = refs[2:]
    else:
        sums = refs[2]

    @pl.when(image == 0)
    def _():
        sums[...] = jnp.zeros_like(sums) if first else sums_in[...]
        norm_grad_ref[...] = norm_grad_in[...]

    hidden_grad = grad_ref[0]
    width = hidden_grad.shape[1]
    attended_low = hidden_grad.astype(low)
    context_grad = mm(attended_low, dense_ref[3]).astype(low)
    sums[3] += mm_rows(attended_low, context_ref[0])
    queries, key_rows, value_rows = projected_ref[0, 0], projected_ref[0, 1], projected_ref[0, 2]
    first_half = lax.broadcasted_iota(jnp.int32, (PAD, 2 * HEAD_DIM), 1) < HEAD_DIM
    zero = jnp.zeros((PAD, 2 * HEAD_DIM), low)
    scale = HEAD_DIM ** (-0.5)
    parts = [[], [], []]
    for pair in range(width // (2 * HEAD_DIM)):
        at = slice(pair * 2 * HEAD_DIM, (pair + 1) * 2 * HEAD_DIM)
        query, key, value, grad = queries[:, at], key_rows[:, at], value_rows[:, at], context_grad[:, at]
        halves = []
        for side in range(2):
            mine = jnp.where(first_half == (side == 0), grad, zero)
            probs = probs_ref[0, 2 * pair + side]
            wide = probs.astype(jnp.float32)
            prob_grad = mm_turned(mine, value)
            weighted = wide * prob_grad
            score_grad = (
                weighted - wide * jnp.sum(weighted, axis=-1, keepdims=True)
            ).astype(low)
            halves.append(
                (mm(score_grad, key) * scale, mm_rows(score_grad, query) * scale, mm_rows(probs, grad))
            )
        for kind in range(3):
            parts[kind].append(jnp.where(first_half, halves[0][kind], halves[1][kind]).astype(low))
    normed = normed_ref[0]
    normed_grad = None
    for kind in range(3):
        projected_grad = jnp.concatenate(parts[kind], axis=1)
        sums[kind] += mm_rows(normed, projected_grad)
        part = mm_turned(projected_grad, dense_ref[kind])
        normed_grad = part if normed_grad is None else normed_grad + part
    unit, inverse = unit_of(input_ref[0].astype(jnp.float32))
    length = input_grad_ref.shape[1]
    normed_grad = normed_grad[:length]
    input_grad_ref[0] = hidden_grad[:length] + unit_backward(normed_grad, unit, inverse, norm_ref[0:1])
    gain = jnp.sum(normed_grad * unit, axis=0, keepdims=True)
    bias = jnp.sum(normed_grad, axis=0, keepdims=True)
    rows_of = lax.broadcasted_iota(jnp.int32, (8, width), 0)
    norm_grad_ref[...] += jnp.where(rows_of == 0, gain, jnp.where(rows_of == 1, bias, 0.0))

    if not last:
        return

    @pl.when(image == images - 1)
    def _():
        kinds, rows, columns = sums.shape[0], *keep_ref.shape[1:]
        near = keep_ref.shape[0] // kinds
        shards = near * 2 // GROUPS
        low_sums[...] = sums[...].astype(low)
        packed[...] = two_terms(regroup(norm_grad_ref[...]))[0]
        copies = [pltpu.make_async_copy(packed, give_ref.at[kinds * near], sems.at[2 * near])]
        for piece in range(2 * near):
            target = keep_ref if piece < near else give_ref
            copies.append(
                pltpu.make_async_copy(
                    dense_window(low_sums, piece, shards, rows, columns),
                    target.at[pl.ds(piece % near * kinds, kinds)],
                    sems.at[piece],
                )
            )
        for copy in copies:
            copy.start()
        for copy in copies:
            copy.wait()


def attend_back(which, count, block_input, norm_params, dense, kept, hidden_grad, norm_grad, carried, near_shape):
    images, length, width = block_input.shape
    heads = width // HEAD_DIM
    low, wide = jnp.bfloat16, jnp.float32
    first, last = carried is None, which + count == images
    near, kinds, rows, columns = near_shape

    def per_image(*shape):
        return pl.BlockSpec((1,) + shape, lambda i: (i + which,) + (0,) * len(shape))

    def whole(array):
        return pl.BlockSpec(array.shape, lambda i: (0,) * array.ndim)

    anywhere = pl.BlockSpec(memory_space=pl.ANY)
    small = pl.BlockSpec((8, width), lambda i: (0, 0))
    sum_shape = (4, width, width)
    given = () if first else tuple(carried)
    out_specs = [per_image(length, width), small]
    out_shape = [
        jax.ShapeDtypeStruct((images, length, width), wide),
        jax.ShapeDtypeStruct((8, width), wide),
    ]
    scratch = []
    if last:
        out_specs += [anywhere] * 2
        out_shape += [jax.ShapeDtypeStruct((near * kinds + k, rows, columns), low) for k in (0, 1)]
        scratch = [
            pltpu.VMEM(sum_shape, wide),
            pltpu.VMEM(sum_shape, low),
            pltpu.VMEM((rows, columns), low),
            pltpu.SemaphoreType.DMA((2 * near + 1,)),
        ]
    else:
        out_specs += [pl.BlockSpec(sum_shape, lambda i: (0, 0, 0))]
        out_shape += [jax.ShapeDtypeStruct(sum_shape, wide)]
    given_specs = [] if first else [whole(carried[0]), anywhere]
    return pl.pallas_call(
        partial(attend_back_kernel, first, last),
        grid=(count,),
        in_specs=[
            per_image(length, width), whole(norm_params), whole(dense),
            per_image(PAD, width), per_image(3, PAD, width), per_image(heads, PAD, PAD),
            per_image(PAD, width), per_image(PAD, width), small,
        ]
        + given_specs,
        out_specs=out_specs,
        out_shape=out_shape,
        scratch_shapes=scratch,
        input_output_aliases={} if first else {10: 0},
        compiler_params=kernel_params(56),
        cost_estimate=cost(count * 5e9, count * 6e6),
        name="attend_back",
    )(block_input, norm_params, dense, *kept, hidden_grad, norm_grad, *given)


def fold_core_kernel(quarter, keep_ref, come_ref, small_ref, x_ref, y_ref, both_ref, own_ref, own_small_ref):
    small = two_terms(regroup(small_ref[...]))[1] + term_sum(come_ref[4 * quarter])
    packed, own_small_ref[...] = two_terms(small)
    for k, target in enumerate((own_ref, x_ref, y_ref, both_ref)):
        at = slice(k * quarter, (k + 1) * quarter)
        total = keep_ref[at].astype(jnp.float32) + come_ref[at].astype(jnp.float32)
        target[:quarter] = total.astype(target.dtype)
        if k:
            target[quarter] = packed


def fold_core(keep, come, small):
    count, rows, columns = keep.shape
    quarter = count // 4
    message = jax.ShapeDtypeStruct((quarter + 1, rows, columns), jnp.bfloat16)
    return pl.pallas_call(
        partial(fold_core_kernel, quarter),
        out_shape=[message] * 3
        + [
            jax.ShapeDtypeStruct((quarter, rows, columns), jnp.float32),
            jax.ShapeDtypeStruct((rows // 2, columns), jnp.float32),
        ],
        compiler_params=kernel_params(24),
        cost_estimate=cost(1e6, 4e6),
        name="fold_core",
    )(keep, come, small)


def fold_sides_kernel(own_ref, small_ref, x_ref, y_ref, both_ref, *refs):
    messages, (total_ref, total_small_ref) = refs[:-2], refs[-2:]
    count = own_ref.shape[0]
    each = count // (len(messages) + 1)
    small = (small_ref[...] + term_sum(x_ref[count])) + (term_sum(y_ref[count]) + term_sum(both_ref[count]))
    packed, total_small_ref[...] = two_terms(small)
    for k, target in enumerate((total_ref, *messages)):
        at = slice(k * each, (k + 1) * each)
        total = own_ref[at] + sum(r[at].astype(jnp.float32) for r in (x_ref, y_ref, both_ref))
        target[:each] = total.astype(target.dtype)
        if k:
            target[each] = packed


def fold_sides(own, small, arrived, shards):
    count, rows, columns = own.shape
    each = count // shards
    message = jax.ShapeDtypeStruct((each + 1, rows, columns), jnp.bfloat16)
    return pl.pallas_call(
        fold_sides_kernel,
        out_shape=[message] * (shards - 1)
        + [jax.ShapeDtypeStruct((each, rows, columns), jnp.float32), jax.ShapeDtypeStruct(small.shape, jnp.float32)],
        compiler_params=kernel_params(24),
        cost_estimate=cost(1e6, 2e6),
        name="fold_sides",
    )(own, small, *arrived)


def dense_update_kernel(shards, own_ref, small_ref, *refs):
    arrived, refs = refs[: shards - 1], refs[shards - 1 :]
    kept, made = refs[:12], refs[12:]
    kinds = own_ref.shape[0]
    width = kept[0].shape[1]

    def update(group, at, gradient, rate, decay):
        old = [ref[at] for ref in kept[3 * group : 3 * group + 3]]
        new = adam_update(old[0], gradient, old[1], old[2], rate, decay)
        for ref, value in zip(made[3 * group : 3 * group + 3], new):
            ref[at] = value

    sums = [small_ref[...]] + [term_sum(r[kinds]) for r in arrived]
    while len(sums) > 1:
        sums = [a + b for a, b in zip(sums[::2], sums[1::2])]
    for k in range(width // 128):
        at = (slice(None), slice(k * 128, (k + 1) * 128))
        block = sums[0][k * 8 : (k + 1) * 8]
        update(0, at, block[:4], 0.25, 0.0)
        update(3, at, block[4:], 0.75 * width ** (-0.5), DECAY_RATE)
    for kind in range(kinds):
        gradient = own_ref[kind] + sum(r[kind].astype(jnp.float32) for r in arrived)
        if kind < kinds - 1:
            update(1, kind, gradient, 1.3 * width ** (-0.5), DECAY_RATE)
        else:
            update(2, (slice(None), slice(None)), gradient, 3.0 * width ** (-0.5), DECAY_RATE)


def dense_update(own, small, arrived, kept):
    return pl.pallas_call(
        partial(dense_update_kernel, len(arrived) + 1),
        out_shape=[jax.ShapeDtypeStruct(a.shape, a.dtype) for a in kept],
        compiler_params=kernel_params(24),
        cost_estimate=cost(1e6, 4e6),
        name="dense_update",
    )(own, small, *arrived, *kept)


def expert_update_kernel(first, experts, terms, *refs):
    parts, refs = refs[:terms], refs[terms:]
    kept, made = refs[:6], refs[6 if first else 12 :]
    width = 4 * kept[0].shape[1]
    rates = (1.0 * width ** (-0.5), 0.8 * experts * FF ** (-0.5))
    for kind in range(2):
        gradient = sum(r[kind].astype(jnp.float32) for r in parts)
        gradient = gradient if kind == 0 else gradient.T
        old = [ref[0] for ref in kept[3 * kind : 3 * kind + 3]]
        new = adam_update(old[0], gradient, old[1], old[2], rates[kind], DECAY_RATE)
        for ref, value in zip(made[3 * kind : 3 * kind + 3], new):
            ref[0] = value


def expert_update(parts, start, kept, before):
    _, rows, columns = parts[0].shape
    offset = start // 128
    anywhere = pl.BlockSpec(memory_space=pl.ANY)
    part = pl.BlockSpec((2, rows, 128), lambda j: (0, 0, j))
    into = pl.BlockSpec((1, rows, 128), lambda j: (0, 0, j + offset))
    out = pl.BlockSpec((1, 128, rows), lambda j: (0, j + offset, 0))
    specs = [into] * 3 + [out] * 3
    before = () if before is None else tuple(before)
    return pl.pallas_call(
        partial(expert_update_kernel, not before, lax.axis_size(SHARD), len(parts)),
        grid=(columns // 128,),
        in_specs=[part] * len(parts) + specs + [anywhere] * len(before),
        out_specs=specs,
        out_shape=[jax.ShapeDtypeStruct(a.shape, a.dtype) for a in kept],
        input_output_aliases={len(parts) + 6 + k: k for k in range(len(before))},
        compiler_params=kernel_params(24),
        cost_estimate=cost(1e6, 12 * 4 * rows * columns),
        name="expert_update",
    )(*parts, *kept, *before)


def relay(block, axis, mask):
    size = lax.axis_size(axis)
    return lax.ppermute(block, axis, [(i, i ^ mask) for i in range(size)])


def relay_core(block):
    return relay(block, HEAD, 1)


def relay_x(block):
    return relay(block, HEAD, 2)


def relay_y(block):
    return relay(block, TENSOR, 1)


def relay_both(block):
    heads, tensors = lax.axis_size(HEAD), lax.axis_size(TENSOR)
    pairs = [
        (h * tensors + t, (h ^ 2) * tensors + (t ^ 1)) for h in range(heads) for t in range(tensors)
    ]
    return lax.ppermute(block, (HEAD, TENSOR), pairs)


def relay_line(blocks):
    return [relay(block, SHARD, k + 1) for k, block in enumerate(blocks)]


def ordered(values, *others):
    return lax.optimization_barrier((values, others))[0]


def wide_sum(*parts):
    return sum(p.astype(jnp.float32) for p in parts)


def local_plan(
    block_input,
    cotangent,
    routes,
    priority,
    norm_params,
    norm_moment,
    norm_square,
    qkv_weight,
    qkv_moment,
    qkv_square,
    attn_weight,
    attn_moment,
    attn_square,
    router_weight,
    router_moment,
    router_square,
    expert_in,
    in_moment,
    in_square,
    expert_out,
    out_moment,
    out_square,
):
    images, length, model_width = block_input.shape
    shards = experts = lax.axis_size(SHARD)
    capacity = 9 * images * length // (4 * experts)
    slots = -(-capacity // SLOT_PAD) * SLOT_PAD
    low = jnp.bfloat16

    dense_low = jnp.concatenate(
        [qkv_weight.transpose(1, 0, 2), attn_weight.T[None]], axis=0
    ).astype(low)
    dense_column = jnp.stack([dense_low] + relay_line([dense_low] * (shards - 1)))
    expert_low = jnp.stack([expert_in[0], expert_out[0].T]).astype(low)
    edges = [expert_low.shape[2] * edge // CUTS[-1] for edge in CUTS]
    chunks = [expert_low[:, :, i:j] for i, j in zip(edges, edges[1:])]
    tables = slot_tables(routes, priority)
    router_wide = jnp.pad(router_weight, ((0, 0), (0, 128 - experts))).astype(low)

    def line_of(block):
        return jnp.stack([block] + relay_line([block] * (shards - 1)))

    def across(column):
        return (relay_x(column), relay_y(column), relay_both(column))

    dense_column, tables, chunks[0] = ordered((dense_column, tables, chunks[0]))
    dense_sides, dense_far = across(dense_column), (relay_core(dense_column),)
    column = line_of(chunks[0])
    later = lax.all_gather(chunks[1], (SHARD, HEAD, TENSOR))
    slot_row, slot_column = find_slots(tables, experts, capacity)
    slot_column = slot_column.reshape(images, PAD, 128)
    dense_sides, dense_far, slot_row = ordered((dense_sides, dense_far, slot_row))
    dense_far += tuple(relay_core(s) for s in dense_sides)
    dense = join_dense((dense_column, *dense_sides, *dense_far), model_width)

    half = shards // 2
    column, dense = ordered((column, dense))
    over_x, over_y, far_column = relay_x(column), relay_y(column), relay_core(column)
    normed, projected, probs, context, hidden, second, route_probs, upstream = attend(
        experts, block_input, cotangent, norm_params, dense, router_wide
    )

    over_x, over_y, far_column, second = ordered((over_x, over_y, far_column, second))
    corners = (relay_y(over_x[:half]), relay_x(over_y[half:]))
    near, far = (column, over_x, over_y), (far_column, relay_core(over_x), relay_core(over_y))
    tokens = images * PAD
    slot_rows = dispatch(
        slot_row, second.reshape(tokens, model_width), upstream.reshape(tokens, model_width),
        route_probs.reshape(tokens, 128), experts, slots,
    )

    corners, far, slot_rows = ordered((corners, far, slot_rows))
    weights_a = (*near, *corners, *far, *(relay_core(c) for c in corners))
    quarter = shards

    class Returning:
        def __init__(self, keep, give):
            self.keep, self.come = keep, relay_core(give)

        def some(self, first, count):
            at = slice(first, first + count)
            return wide_sum(self.keep[at], self.come[at])

        def part(self, k):
            return self.some(k * quarter, quarter)

        def across(self):
            x, y, both = (self.part(k).astype(low) for k in (1, 2, 3))
            self.over = (relay_x(x), relay_y(y), relay_both(both))

        def corner(self):
            half = quarter // 2
            self.corners = (
                relay_x(self.some(3 * quarter, half).astype(low)),
                relay_y(self.some(3 * quarter + half, quarter - half).astype(low)),
            )

        def sides(self):
            half = quarter // 2
            over_x, over_y = self.part(1), self.part(2)
            from_x, from_y = (c.astype(jnp.float32) for c in self.corners)
            over_x = jnp.concatenate([over_x[:half], over_x[half:] + from_y])
            over_y = jnp.concatenate([over_y[:half] + from_x, over_y[half:]])
            self.over = (relay_x(over_x.astype(low)), relay_y(over_y.astype(low)))

        def line(self):
            total = self.part(0) + wide_sum(*self.over)
            self.own = total[0]
            self.others = relay_line([total[k].astype(low) for k in range(1, quarter)])

        def result(self):
            return self.own + wide_sum(*self.others)

    made, backed, grads = run_experts(*slot_rows, None, weights_a, False, False)

    made, grads, later = ordered((made, grads, later))
    own_a = lax.psum_scatter(grads, (HEAD, TENSOR), scatter_dimension=0, tiled=True)
    made, backed, keep, give = run_experts(*slot_rows, (made, backed), (later,), True, True)

    made, keep, give = ordered((made, keep, give))
    sum_b = Returning(keep, give)
    block_output, hidden_grad, norm_grad = combine(
        length, experts, slot_column, made, backed, hidden, upstream, second, route_probs,
        norm_params, router_wide,
    )

    sum_b.keep, sum_b.come, hidden_grad = ordered((sum_b.keep, sum_b.come, hidden_grad))
    sum_b.corner()
    kept = (normed, projected, probs, context)
    half = images // 2
    dense_shape = (4 * quarter, *dense_low.shape)
    input_grad, norm_grad, dense_sums = attend_back(
        0, half, block_input, norm_params, dense, kept, hidden_grad, norm_grad, None, (4 * quarter, *dense_low.shape)
    )

    sum_b.corners, own_a, norm_grad, dense_sums = ordered((sum_b.corners, own_a, norm_grad, dense_sums))
    others_a = relay_line([own_a[k] for k in range(1, quarter)])
    sum_b.sides()
    input_grad, norm_grad, keep, give = attend_back(
        half, images - half, block_input, norm_params, dense, kept, hidden_grad, norm_grad,
        (dense_sums, input_grad), (4 * quarter, *dense_low.shape),
    )

    sum_b.over, others_a, keep, give = ordered((sum_b.over, others_a, keep, give))
    come = relay_core(give)
    sum_b.line()
    come, sum_b.own = ordered((come, sum_b.own))
    *messages, own, own_small = fold_core(keep, come, norm_grad)
    arrived = [send(m) for m, send in zip(messages, (relay_x, relay_y, relay_both))]
    messages, own_a, others_a = ordered((messages, own_a, others_a))
    expert_kept = (expert_in, in_moment, in_square, expert_out, out_moment, out_square)
    updated = expert_update([own_a[0], *others_a], 0, expert_kept, None)
    arrived, updated = ordered((arrived, updated))
    *messages, own, own_small = fold_sides(own, own_small, arrived, shards)
    arrived = relay_line(messages)
    updated = expert_update([sum_b.own, *sum_b.others], edges[1], expert_kept, updated)
    arrived, updated = ordered((arrived, updated))
    turns = ((0, 1), (1, 0, 2), (1, 0), (1, 0))
    dense_kept = (
        (norm_params, norm_moment, norm_square),
        (qkv_weight, qkv_moment, qkv_square),
        (attn_weight, attn_moment, attn_square),
        (router_weight, router_moment, router_square),
    )
    flat = [a.transpose(t) for t, group in zip(turns, dense_kept) for a in group]
    dense_new = dense_update(own, own_small, arrived, flat)
    dense_new = [a.transpose(turns[k // 3]) for k, a in enumerate(dense_new)]
    return (block_output, input_grad, *dense_new, *updated)


def solution(mesh):
    fits = mesh.shape[SHARD] <= 4
    return jax.shard_map(
        local_plan if fits else slot_plan,
        mesh=mesh,
        in_specs=(
            P((SHARD, HEAD, TENSOR), None, None),
            P((SHARD, HEAD, TENSOR), None, None),
            P((SHARD, HEAD, TENSOR), None, None),
            P((SHARD, HEAD, TENSOR), None),
            P(),
            P(),
            P(),
            P((SHARD, TENSOR), None, HEAD),
            P((SHARD, TENSOR), None, HEAD),
            P((SHARD, TENSOR), None, HEAD),
            P(HEAD, (SHARD, TENSOR)),
            P(HEAD, (SHARD, TENSOR)),
            P(HEAD, (SHARD, TENSOR)),
            P(),
            P(),
            P(),
            P(SHARD, HEAD, TENSOR),
            P(SHARD, HEAD, TENSOR),
            P(SHARD, HEAD, TENSOR),
            P(SHARD, TENSOR, HEAD),
            P(SHARD, TENSOR, HEAD),
            P(SHARD, TENSOR, HEAD),
        ),
        out_specs=(
            P((SHARD, HEAD, TENSOR), None, None),
            P((SHARD, HEAD, TENSOR), None, None),
            P(),
            P(),
            P(),
            P((SHARD, TENSOR), None, HEAD),
            P((SHARD, TENSOR), None, HEAD),
            P((SHARD, TENSOR), None, HEAD),
            P(HEAD, (SHARD, TENSOR)),
            P(HEAD, (SHARD, TENSOR)),
            P(HEAD, (SHARD, TENSOR)),
            P(),
            P(),
            P(),
            P(SHARD, HEAD, TENSOR),
            P(SHARD, HEAD, TENSOR),
            P(SHARD, HEAD, TENSOR),
            P(SHARD, TENSOR, HEAD),
            P(SHARD, TENSOR, HEAD),
            P(SHARD, TENSOR, HEAD),
        ),
        check_vma=False,
    )
```

```python
import math
from functools import partial

import jax
import jax.numpy as jnp
from jax import lax
from jax.experimental import pallas as pl
from jax.experimental.pallas import tpu as pltpu
from jax.sharding import PartitionSpec as P

SHARD, HEAD, TENSOR = "shard", "head", "tensor"
HEAD_DIM = 64
FF = 2048
STEP = 10


EPS_NORM = 1e-06
BETA_ONE = 0.9
BETA_TWO = 0.999
ADAM_EPS = 1e-08
DECAY_RATE = 0.1


def norm_forward(values, gain_row, bias_row):
    center = jnp.mean(values, axis=-1, keepdims=True)
    shifted = values - center
    inverse = lax.rsqrt(jnp.mean(shifted * shifted, axis=-1, keepdims=True) + EPS_NORM)
    unit_rows = shifted * inverse
    return (unit_rows * gain_row + bias_row, unit_rows, inverse)


def norm_backward(grad_rows, unit_rows, inverse, gain_row):
    scaled = grad_rows * gain_row
    inner_grad = (
        scaled
        - jnp.mean(scaled, axis=-1, keepdims=True)
        - unit_rows * jnp.mean(scaled * unit_rows, axis=-1, keepdims=True)
    )
    return (
        inner_grad * inverse,
        jnp.sum(grad_rows * unit_rows, axis=0),
        jnp.sum(grad_rows, axis=0),
    )


def gelu_grad(pre_act, upstream):
    result, pullback = jax.vjp(partial(jax.nn.gelu, approximate=True), pre_act)
    return pullback(upstream)[0]


def adam_update(weight, gradient, moment, square, step_rate, decay_rate):
    moment_new = BETA_ONE * moment + (1.0 - BETA_ONE) * gradient
    square_new = BETA_TWO * square + (1.0 - BETA_TWO) * gradient * gradient
    first_hat = moment_new / (1.0 - BETA_ONE**STEP)
    second_hat = square_new / (1.0 - BETA_TWO**STEP)
    weight_new = weight - step_rate * (
        first_hat / (jnp.sqrt(second_hat) + ADAM_EPS) + decay_rate * weight
    )
    return (weight_new, moment_new, square_new)


def send_rows(parcel):
    copies = jnp.broadcast_to(
        parcel[:, None], (parcel.shape[0], lax.axis_size(TENSOR)) + parcel.shape[1:]
    )
    flat_copies = copies.reshape((-1,) + parcel.shape[1:])
    arrived = lax.all_to_all(
        flat_copies, (SHARD, TENSOR), split_axis=0, concat_axis=0, tiled=True
    )
    return arrived.reshape(copies.shape)


def return_rows(partial_rows):
    flat_rows = partial_rows.reshape((-1,) + partial_rows.shape[2:])
    arrived = lax.all_to_all(
        flat_rows.astype(jnp.bfloat16), (SHARD, TENSOR), split_axis=0, concat_axis=0, tiled=True
    ).astype(flat_rows.dtype)
    return jnp.sum(arrived.reshape(partial_rows.shape), axis=1)


def slot_plan(
    block_input,
    cotangent,
    routes,
    priority,
    norm_params,
    norm_moment,
    norm_square,
    qkv_weight,
    qkv_moment,
    qkv_square,
    attn_weight,
    attn_moment,
    attn_square,
    router_weight,
    router_moment,
    router_square,
    expert_in,
    in_moment,
    in_square,
    expert_out,
    out_moment,
    out_square,
):
    images, length, model_width = block_input.shape
    row_count = images * length
    local_experts = expert_in.shape[0]
    shards = lax.axis_size(SHARD)
    experts = local_experts * shards
    capacity = 9 * row_count // (4 * experts)
    score_scale = HEAD_DIM ** (-0.5)
    full_qkv, full_attn = (
        lax.all_gather(qkv_weight.astype(jnp.bfloat16), (SHARD, TENSOR), axis=0, tiled=True),
        lax.all_gather(attn_weight.astype(jnp.bfloat16), (SHARD, TENSOR), axis=1, tiled=True),
    )
    inputs = block_input.astype(jnp.float32).reshape(row_count, model_width)
    normed, unit_one, inverse_one = norm_forward(inputs, norm_params[0], norm_params[1])
    normed_low = normed.astype(jnp.bfloat16).reshape(images, length, model_width)
    gathered, hidden_in, hidden_out = (
        lax.all_gather(normed_low, HEAD, axis=0, tiled=True),
        lax.all_gather(expert_in.astype(jnp.bfloat16), HEAD, axis=1, tiled=True),
        lax.all_gather(expert_out.astype(jnp.bfloat16), HEAD, axis=2, tiled=True),
    )
    local_heads = full_qkv.shape[2] // HEAD_DIM
    all_images = gathered.shape[0]
    head_shape = (all_images, length, local_heads, HEAD_DIM)
    projected = jnp.einsum(
        "isd,dcn->iscn", gathered, full_qkv, preferred_element_type=jnp.float32
    ).astype(jnp.bfloat16)
    queries = projected[:, :, 0].reshape(head_shape)
    key_rows = projected[:, :, 1].reshape(head_shape)
    value_rows = projected[:, :, 2].reshape(head_shape)
    scores = (
        jnp.einsum("iqhe,ikhe->ihqk", queries, key_rows, preferred_element_type=jnp.float32)
        * score_scale
    )
    score_top = jnp.max(scores, axis=-1, keepdims=True)
    log_total = score_top + jnp.log(jnp.sum(jnp.exp(scores - score_top), axis=-1, keepdims=True))
    probs_low = jnp.exp(scores - log_total).astype(jnp.bfloat16)
    context = jnp.einsum(
        "ihqk,ikhe->iqhe", probs_low, value_rows, preferred_element_type=jnp.float32
    ).astype(jnp.bfloat16)
    context = context.reshape(all_images * length, local_heads * HEAD_DIM)
    attended = lax.psum_scatter(
        jnp.dot(context, full_attn, preferred_element_type=jnp.float32).astype(jnp.bfloat16),
        HEAD,
        scatter_dimension=0,
        tiled=True,
    ).astype(jnp.float32)
    hidden = inputs + attended
    normed_two, unit_two, inverse_two = norm_forward(hidden, norm_params[2], norm_params[3])
    second_low = normed_two.astype(jnp.bfloat16)
    router_low = router_weight.astype(jnp.bfloat16)
    logits = jnp.dot(second_low, router_low, preferred_element_type=jnp.float32)
    route_probs = jax.nn.softmax(logits, axis=-1)
    route_hot = (
        routes.reshape(row_count, 2)[:, :, None]
        == jnp.arange(experts, dtype=jnp.int32)[None, None, :]
    ).astype(jnp.float32)
    gate_values = jnp.sum(route_probs[:, None, :] * route_hot, axis=-1)
    expert_ids = routes.reshape(2 * row_count)
    rank_values = priority[0]
    pair_hot = route_hot.reshape(2 * row_count, experts)
    earlier = (rank_values[None, :] < rank_values[:, None]).astype(jnp.bfloat16)
    counts = jnp.dot(earlier, pair_hot.astype(jnp.bfloat16), preferred_element_type=jnp.float32)
    slot_index = jnp.sum(counts * pair_hot, axis=1).astype(jnp.int32)
    target = jnp.where(
        slot_index < capacity, expert_ids * capacity + slot_index, experts * capacity
    )
    filler = jnp.full((experts * capacity,), 2 * row_count, jnp.int32)
    owner_pair = filler.at[target].set(jnp.arange(2 * row_count, dtype=jnp.int32), mode="drop")
    padded = jnp.concatenate([second_low, jnp.zeros((1, model_width), jnp.bfloat16)], axis=0)
    parcel = padded[owner_pair // 2].reshape(shards, local_experts, capacity, model_width)
    arrived = send_rows(parcel)
    pre_act = jnp.einsum("stecd,edf->stecf", arrived, hidden_in, preferred_element_type=jnp.float32)
    active = jax.nn.gelu(pre_act, approximate=True).astype(jnp.bfloat16)
    part_rows = jnp.einsum(
        "stecf,efd->stecd", active, hidden_out, preferred_element_type=jnp.float32
    )
    expert_rows = return_rows(part_rows).reshape(experts * capacity, model_width)
    padded_out = jnp.concatenate([expert_rows, jnp.zeros((1, model_width), jnp.float32)], axis=0)
    per_pair = padded_out[target].reshape(row_count, 2, model_width)
    block_sum = hidden + jnp.sum(gate_values[:, :, None] * per_pair, axis=1)
    block_output = block_sum.astype(jnp.bfloat16).reshape(images, length, model_width)
    upstream = cotangent.astype(jnp.float32).reshape(row_count, model_width)
    pair_grad = (
        (gate_values[:, :, None] * upstream[:, None, :])
        .astype(jnp.bfloat16)
        .reshape(2 * row_count, model_width)
    )
    gate_grad = jnp.sum(upstream[:, None, :] * per_pair, axis=-1)
    padded_grad = jnp.concatenate([pair_grad, jnp.zeros((1, model_width), jnp.bfloat16)], axis=0)
    grad_parcel = padded_grad[owner_pair].reshape(shards, local_experts, capacity, model_width)
    grad_arrived = send_rows(grad_parcel)
    grad_out_part = jnp.einsum(
        "stecf,stecd->efd", active, grad_arrived, preferred_element_type=jnp.float32
    )
    active_grad = jnp.einsum(
        "stecd,efd->stecf", grad_arrived, hidden_out, preferred_element_type=jnp.float32
    )
    pre_grad = gelu_grad(pre_act, active_grad).astype(jnp.bfloat16)
    grad_in_part = jnp.einsum(
        "stecd,stecf->edf", arrived, pre_grad, preferred_element_type=jnp.float32
    )
    row_grad = jnp.einsum(
        "stecf,edf->stecd", pre_grad, hidden_in, preferred_element_type=jnp.float32
    )
    slot_grad = return_rows(row_grad).reshape(experts * capacity, model_width)
    padded_slot = jnp.concatenate([slot_grad, jnp.zeros((1, model_width), jnp.float32)], axis=0)
    second_grad = jnp.sum(padded_slot[target].reshape(row_count, 2, model_width), axis=1)
    prob_sum = jnp.sum(gate_grad[:, :, None] * route_hot, axis=1)
    logit_grad = (
        route_probs * (prob_sum - jnp.sum(route_probs * prob_sum, axis=-1, keepdims=True))
    ).astype(jnp.bfloat16)
    router_grad = jnp.einsum(
        "rd,re->de", second_low, logit_grad, preferred_element_type=jnp.float32
    )
    second_grad = second_grad + jnp.einsum(
        "re,de->rd", logit_grad, router_low, preferred_element_type=jnp.float32
    )
    hidden_part, gain_two, bias_two = norm_backward(
        second_grad, unit_two, inverse_two, norm_params[2]
    )
    hidden_grad = upstream + hidden_part
    attended_grad = lax.all_gather(hidden_grad.astype(jnp.bfloat16), HEAD, axis=0, tiled=True)
    attn_grad = jnp.einsum("rn,rd->nd", context, attended_grad, preferred_element_type=jnp.float32)
    context_grad = jnp.einsum(
        "rd,nd->rn", attended_grad, full_attn, preferred_element_type=jnp.float32
    ).astype(jnp.bfloat16)
    context_grad = context_grad.reshape(head_shape)
    scores_again = (
        jnp.einsum("iqhe,ikhe->ihqk", queries, key_rows, preferred_element_type=jnp.float32)
        * score_scale
    )
    probs_full = jnp.exp(scores_again - log_total)
    prob_grad = jnp.einsum(
        "iqhe,ikhe->ihqk", context_grad, value_rows, preferred_element_type=jnp.float32
    )
    score_grad = (
        probs_full * (prob_grad - jnp.sum(probs_full * prob_grad, axis=-1, keepdims=True))
    ).astype(jnp.bfloat16)
    query_grad = (
        jnp.einsum("ihqk,ikhe->iqhe", score_grad, key_rows, preferred_element_type=jnp.float32)
        * score_scale
    )
    key_grad = (
        jnp.einsum("ihqk,iqhe->ikhe", score_grad, queries, preferred_element_type=jnp.float32)
        * score_scale
    )
    value_grad = jnp.einsum(
        "ihqk,iqhe->ikhe", probs_low, context_grad, preferred_element_type=jnp.float32
    )
    projected_grad = (
        jnp.stack([query_grad, key_grad, value_grad], axis=2)
        .reshape(all_images, length, 3, local_heads * HEAD_DIM)
        .astype(jnp.bfloat16)
    )
    qkv_grad = jnp.einsum(
        "isd,iscn->dcn", gathered, projected_grad, preferred_element_type=jnp.float32
    )
    normed_part = jnp.einsum(
        "iscn,dcn->isd", projected_grad, full_qkv, preferred_element_type=jnp.float32
    )
    normed_grad, in_grad, out_grad = (
        lax.psum_scatter(
            normed_part.astype(jnp.bfloat16), HEAD, scatter_dimension=0, tiled=True
        ).astype(jnp.float32),
        lax.psum_scatter(
            grad_in_part.astype(jnp.bfloat16), HEAD, scatter_dimension=1, tiled=True
        ).astype(jnp.float32),
        lax.psum_scatter(
            grad_out_part.astype(jnp.bfloat16), HEAD, scatter_dimension=2, tiled=True
        ).astype(jnp.float32),
    )
    input_part, gain_one, bias_one = norm_backward(
        normed_grad.reshape(row_count, model_width), unit_one, inverse_one, norm_params[0]
    )
    input_grad = (hidden_grad + input_part).reshape(images, length, model_width)
    norm_grad = jnp.stack([gain_one, bias_one, gain_two, bias_two])
    norm_grad, router_grad = lax.psum((norm_grad, router_grad), (SHARD, HEAD, TENSOR))
    qkv_grad, attn_grad = (
        lax.psum_scatter(qkv_grad, (SHARD, TENSOR), scatter_dimension=0, tiled=True),
        lax.psum_scatter(attn_grad, (SHARD, TENSOR), scatter_dimension=1, tiled=True),
    )
    norm_new = adam_update(norm_params, norm_grad, norm_moment, norm_square, 0.25, 0.0)
    qkv_new = adam_update(
        qkv_weight, qkv_grad, qkv_moment, qkv_square, 1.3 * model_width ** (-0.5), DECAY_RATE
    )
    attn_new = adam_update(
        attn_weight, attn_grad, attn_moment, attn_square, 3.0 * model_width ** (-0.5), DECAY_RATE
    )
    router_new = adam_update(
        router_weight,
        router_grad,
        router_moment,
        router_square,
        0.75 * model_width ** (-0.5),
        DECAY_RATE,
    )
    in_new = adam_update(
        expert_in, in_grad, in_moment, in_square, 1.0 * model_width ** (-0.5), DECAY_RATE
    )
    out_new = adam_update(
        expert_out, out_grad, out_moment, out_square, 0.8 * experts * FF ** (-0.5), DECAY_RATE
    )
    return (
        block_output,
        input_grad,
        norm_new[0],
        norm_new[1],
        norm_new[2],
        qkv_new[0],
        qkv_new[1],
        qkv_new[2],
        attn_new[0],
        attn_new[1],
        attn_new[2],
        router_new[0],
        router_new[1],
        router_new[2],
        in_new[0],
        in_new[1],
        in_new[2],
        out_new[0],
        out_new[1],
        out_new[2],
    )


PAD = 208
SLOT_PAD = 16
CUTS = (0, 3, 8)
TOGETHER = 2


def kernel_params(megabytes):
    return pltpu.CompilerParams(vmem_limit_bytes=megabytes << 20)


def cost(flops, moved):
    return pl.CostEstimate(flops=int(flops), bytes_accessed=int(moved), transcendentals=0)


def mm(left, right):
    return lax.dot_general(left, right, (((1,), (0,)), ((), ())), preferred_element_type=jnp.float32)


def mm_turned(left, right):
    return lax.dot_general(left, right, (((1,), (1,)), ((), ())), preferred_element_type=jnp.float32)


def mm_rows(left, right):
    return lax.dot_general(left, right, (((0,), (0,)), ((), ())), preferred_element_type=jnp.float32)


def unit_of(values):
    center = jnp.mean(values, axis=-1, keepdims=True)
    shifted = values - center
    inverse = lax.rsqrt(jnp.mean(shifted * shifted, axis=-1, keepdims=True) + EPS_NORM)
    return (shifted * inverse, inverse)


def unit_backward(grad_rows, unit_rows, inverse, gain_row):
    scaled = grad_rows * gain_row
    inner_grad = (
        scaled
        - jnp.mean(scaled, axis=-1, keepdims=True)
        - unit_rows * jnp.mean(scaled * unit_rows, axis=-1, keepdims=True)
    )
    return inner_grad * inverse


def absolute(group):
    tensor = lax.axis_index(TENSOR) ^ (group // 2 % 2)
    head = lax.axis_index(HEAD) ^ (2 * (group % 2) + group // 4)
    return tensor, head


GROUPS = 8


def slot_kernel(experts, capacity, row_ref, column_ref, slot_row_ref, slot_column_ref):
    none = 1 << 20
    tokens = row_ref.shape[1]
    lanes = lax.broadcasted_iota(jnp.int32, (PAD, 128), 1)
    rows_of = lax.broadcasted_iota(jnp.int32, (8, tokens), 0)

    def ranks(named, rank, expert):
        return jnp.where(
            named[0] == expert, rank[0], jnp.where(named[1] == expert, rank[1], none)
        )

    routes_row, ranks_row = (row_ref[0:1], row_ref[1:2]), (row_ref[2:3], row_ref[3:4])
    all_rows = jnp.full((8, tokens), -1, jnp.int32)
    row_of = [ranks(routes_row, ranks_row, e) for e in range(experts)]
    totals = [jnp.zeros((1, tokens), jnp.float32) for e in range(experts)]
    for block in range(tokens // PAD):
        part = column_ref[block * PAD : (block + 1) * PAD]
        routes_col, ranks_col = (part[:, 0:1], part[:, 1:2]), (part[:, 2:3], part[:, 3:4])
        result = jnp.full((PAD, 128), -1, jnp.int32)
        for e in range(experts):
            column = ranks(routes_col, ranks_col, e)
            totals[e] = totals[e] + jnp.sum(
                jnp.where(column < row_of[e], 1.0, 0.0), axis=0, keepdims=True
            )
            before = jnp.sum(
                jnp.where(row_of[e] < column, 1.0, 0.0), axis=1, keepdims=True
            ).astype(jnp.int32)
            slot = jnp.where((column < none) & (before < capacity), before, -1)
            result = jnp.where(lanes == e, slot, result)
        slot_column_ref[block * PAD : (block + 1) * PAD] = result
    for e in range(experts):
        before = totals[e].astype(jnp.int32)
        slot = jnp.where((row_of[e] < none) & (before < capacity), before, -1)
        all_rows = jnp.where(rows_of == e, slot, all_rows)
    slot_row_ref[...] = all_rows


def slot_tables(routes, priority):
    images, length, _ = routes.shape
    tokens = images * PAD
    table = jnp.concatenate([routes, priority.reshape(images, length, 2)], axis=2)
    table = jnp.pad(table, ((0, 0), (0, PAD - length), (0, 0)), constant_values=-1)
    table = table.reshape(tokens, 4)
    columns = jnp.pad(table, ((0, 0), (0, 4)))
    return (columns.T, columns)


def find_slots(tables, experts, capacity):
    tokens = tables[1].shape[0]
    return pl.pallas_call(
        partial(slot_kernel, experts, capacity),
        out_shape=(
            jax.ShapeDtypeStruct((8, tokens), jnp.int32),
            jax.ShapeDtypeStruct((tokens, 128), jnp.int32),
        ),
        compiler_params=kernel_params(32),
        cost_estimate=cost(1e10, 1e6),
        name="find_slots",
    )(*tables)


def dense_window(ref, piece, shards, rows, columns):
    tensor, head = absolute(piece // shards)
    shard = lax.axis_index(SHARD) ^ (piece % shards)
    down = pl.multiple_of((shard * lax.axis_size(TENSOR) + tensor) * rows, rows)
    over = pl.multiple_of(head * columns, columns)
    return ref.at[:, pl.ds(down, rows), pl.ds(over, columns)]


def dense_kernel(*refs):
    groups, (full_ref, sems) = refs[:GROUPS], refs[GROUPS:]
    shards, kinds, rows, columns = groups[0].shape
    copies = []
    for piece in range(GROUPS * shards):
        copies.append(
            pltpu.make_async_copy(
                groups[piece // shards].at[piece % shards],
                dense_window(full_ref, piece, shards, rows, columns),
                sems.at[piece],
            )
        )
    for copy in copies:
        copy.start()
    for copy in copies:
        copy.wait()


def join_dense(groups, model_width):
    shards, kinds = groups[0].shape[:2]
    return pl.pallas_call(
        dense_kernel,
        out_shape=jax.ShapeDtypeStruct((kinds, model_width, model_width), groups[0].dtype),
        in_specs=[pl.BlockSpec(memory_space=pl.ANY)] * GROUPS,
        out_specs=pl.BlockSpec(memory_space=pltpu.VMEM),
        scratch_shapes=[pltpu.SemaphoreType.DMA((GROUPS * shards,))],
        compiler_params=kernel_params(16),
        cost_estimate=cost(1e6, 4e6),
        name="join_dense",
    )(*groups)


def attend_kernel(
    length, experts, input_ref, cotangent_ref, norm_ref, dense_ref, router_ref,
    normed_ref, projected_ref, probs_ref, context_ref, hidden_ref, second_ref, route_ref, upstream_ref, whole,
):
    low = jnp.bfloat16
    count, width = input_ref.shape[0], input_ref.shape[2]
    whole[...] = jnp.zeros_like(whole)
    for i in range(count):
        whole[i * PAD : i * PAD + length] = cotangent_ref[i].astype(jnp.float32)
    upstream_ref[...] = whole[...].astype(low).reshape(upstream_ref.shape)
    for i in range(count):
        whole[i * PAD : i * PAD + length] = input_ref[i].astype(jnp.float32)
    values = whole[...]
    unit, _ = unit_of(values)
    normed = (unit * norm_ref[0:1] + norm_ref[1:2]).astype(low)
    normed_ref[...] = normed.reshape(normed_ref.shape)
    queries, key_rows, value_rows = (mm(normed, dense_ref[c]).astype(low) for c in range(3))
    first_half = lax.broadcasted_iota(jnp.int32, (PAD, 2 * HEAD_DIM), 1) < HEAD_DIM
    is_key = lax.broadcasted_iota(jnp.int32, (PAD, PAD), 0) < length
    zero = jnp.zeros((PAD, 2 * HEAD_DIM), low)
    contexts = []
    for i in range(count):
        rows = slice(i * PAD, (i + 1) * PAD)
        for c, part in enumerate((queries, key_rows, value_rows)):
            projected_ref[i, c] = part[rows]
        pairs = []
        for pair in range(width // (2 * HEAD_DIM)):
            at = slice(pair * 2 * HEAD_DIM, (pair + 1) * 2 * HEAD_DIM)
            query, key, value = queries[rows, at], key_rows[rows, at], value_rows[rows, at]
            halves = []
            for side in range(2):
                mine = jnp.where(first_half == (side == 0), query, zero)
                scores = mm_turned(key, mine) * (HEAD_DIM ** (-0.5))
                scores = jnp.where(is_key, scores, -1e30)
                top = jnp.max(scores, axis=0, keepdims=True)
                raised = jnp.exp(scores - top)
                probs = (raised / jnp.sum(raised, axis=0, keepdims=True)).astype(low)
                probs_ref[i, 2 * pair + side] = probs
                halves.append(mm_rows(value, probs)[side * HEAD_DIM : (side + 1) * HEAD_DIM])
            pairs.append(jnp.concatenate(halves, axis=0).T.astype(low))
        contexts.append(jnp.concatenate(pairs, axis=1))
    context = jnp.concatenate(contexts, axis=0)
    context_ref[...] = context.reshape(context_ref.shape)
    hidden = values + mm_turned(context, dense_ref[3])
    hidden_ref[...] = hidden.reshape(hidden_ref.shape)
    unit, _ = unit_of(hidden)
    second = (unit * norm_ref[2:3] + norm_ref[3:4]).astype(low)
    second_ref[...] = second.reshape(second_ref.shape)
    logits = mm(second, router_ref[...])
    is_expert = lax.broadcasted_iota(jnp.int32, logits.shape, 1) < experts
    logits = jnp.where(is_expert, logits, -1e30)
    raised = jnp.exp(logits - jnp.max(logits, axis=-1, keepdims=True))
    route_probs = raised / jnp.sum(raised, axis=-1, keepdims=True)
    route_ref[...] = route_probs.reshape(route_ref.shape)


def attend(experts, block_input, cotangent, norm_params, dense, router_wide):
    images, length, width = block_input.shape
    heads = width // HEAD_DIM
    low, wide = jnp.bfloat16, jnp.float32

    def per_image(*shape):
        return pl.BlockSpec((TOGETHER,) + shape, lambda i: (i,) + (0,) * len(shape))

    def whole(array):
        return pl.BlockSpec(array.shape, lambda i: (0,) * array.ndim)

    shapes = [
        ((PAD, width), low), ((3, PAD, width), low), ((heads, PAD, PAD), low), ((PAD, width), low),
        ((PAD, width), wide), ((PAD, width), low), ((PAD, 128), wide), ((PAD, width), low),
    ]
    return pl.pallas_call(
        partial(attend_kernel, length, experts),
        grid=(images // TOGETHER,),
        in_specs=[per_image(length, width)] * 2 + [whole(norm_params), whole(dense), whole(router_wide)],
        out_specs=[per_image(*s) for s, _ in shapes],
        out_shape=[jax.ShapeDtypeStruct((images,) + s, t) for s, t in shapes],
        scratch_shapes=[pltpu.VMEM((TOGETHER * PAD, width), wide)],
        compiler_params=kernel_params(56),
        cost_estimate=cost(images * 2.5e9, images * 5e6),
        name="attend",
    )(block_input, cotangent, norm_params, dense, router_wide)


def dispatch_kernel(waits, slot_ref, second_ref, upstream_ref, route_ref, *refs):
    x_ref, g_ref, xt_ref, gt_ref = refs[waits:]
    low = jnp.bfloat16
    expert = pl.program_id(0)
    slots, tokens = x_ref.shape[1], second_ref.shape[0]
    rows_of = lax.broadcasted_iota(jnp.int32, (8, tokens), 0)
    slot_row = jnp.max(jnp.where(rows_of == expert, slot_ref[...], -1), axis=0, keepdims=True)
    hot = lax.broadcasted_iota(jnp.int32, (slots, tokens), 0) == slot_row
    hot = jnp.where(hot, 1.0, 0.0).astype(low)
    lanes = lax.broadcasted_iota(jnp.int32, (tokens, 128), 1)
    gate = jnp.sum(jnp.where(lanes == expert, route_ref[...], 0.0), axis=1, keepdims=True)
    pair_grad = (gate * upstream_ref[...].astype(jnp.float32)).astype(low)
    rows = mm(hot, second_ref[...]).astype(low)
    x_ref[0] = rows
    xt_ref[0] = rows.T
    rows = mm(hot, pair_grad).astype(low)
    g_ref[0] = rows
    gt_ref[0] = rows.T


def dispatch(slot_row, second, upstream, route_probs, experts, slots, waits=()):
    tokens, width = second.shape

    def whole(array):
        return pl.BlockSpec(array.shape, lambda e: (0,) * array.ndim)

    flat = pl.BlockSpec((1, slots, width), lambda e: (e, 0, 0))
    turned = pl.BlockSpec((1, width, slots), lambda e: (e, 0, 0))
    low = jnp.bfloat16
    return pl.pallas_call(
        partial(dispatch_kernel, len(waits)),
        grid=(experts,),
        in_specs=[whole(a) for a in (slot_row, second, upstream, route_probs)]
        + [pl.BlockSpec(memory_space=pl.ANY)] * len(waits),
        out_specs=[flat, flat, turned, turned],
        out_shape=[jax.ShapeDtypeStruct((experts, slots, width), low)] * 2
        + [jax.ShapeDtypeStruct((experts, width, slots), low)] * 2,
        compiler_params=kernel_params(60),
        cost_estimate=cost(4 * slots * tokens * width * experts, 1e7),
        name="dispatch",
    )(slot_row, second, upstream, route_probs, *waits)


def expert_kernel(first, last, split, count, x_ref, g_ref, xt_ref, gt_ref, *refs):
    low = jnp.bfloat16
    if not first:
        made_in, back_in = refs[:2]
        refs = refs[2:]
    sources, refs = refs[:count], refs[count:]
    _, _, rows, columns = sources[0].shape
    made_ref, back_ref, *targets, held, sent, in_sems, out_sems = refs
    expert, experts = pl.program_id(0), pl.num_programs(0)
    shards, heads, tensors = (lax.axis_size(a) for a in (SHARD, HEAD, TENSOR))
    middle = shards // 2

    def window(ref, slot, group, start=0, width=None):
        tensor, head = absolute(group)
        down = pl.multiple_of(head * rows, rows)
        over = pl.multiple_of(tensor * columns + start, 128)
        return ref.at[slot, :, pl.ds(down, rows), pl.ds(over, columns if width is None else width)]

    def fetch(source, slot, group):
        return pltpu.make_async_copy(source, window(held, slot, group), in_sems.at[slot, group])

    def start_fetch(which, slot, group):
        if count == 1:
            tensor, head = absolute(group)
            fetch(sources[0].at[(which * heads + head) * tensors + tensor], slot, group).start()
            return
        z = which ^ lax.axis_index(SHARD)
        place = group % 4 + (group // 4) * 5
        if group % 4 < 3:
            fetch(sources[place].at[z], slot, group).start()
            return

        @pl.when(z < middle)
        def _():
            fetch(sources[place].at[z], slot, group).start()

        @pl.when(z >= middle)
        def _():
            fetch(sources[place + 1].at[z - middle], slot, group).start()

    def puts(which, slot, group):
        z = which ^ lax.axis_index(SHARD)
        tensor, head = absolute(group)
        copies = []
        if split > 0:
            source, target = window(sent, slot, group, 0, split), targets[0].at[(head * tensors + tensor) * shards + z]
            copies.append(pltpu.make_async_copy(source, target, out_sems.at[slot, group, 0]))
        if split < columns:
            source = window(sent, slot, group, split, columns - split)
            target = targets[-2 + group // (GROUPS // 2)].at[group % (GROUPS // 2) * shards + z]
            copies.append(pltpu.make_async_copy(source, target, out_sems.at[slot, group, 1]))
        return copies

    slot = lax.rem(expert, 2)

    @pl.when(expert == 0)
    def _():
        for group in range(GROUPS):
            start_fetch(0, 0, group)

    @pl.when(expert + 1 < experts)
    def _():
        for group in range(GROUPS):
            start_fetch(expert + 1, 1 - slot, group)

    for group in range(GROUPS):
        fetch(sources[0].at[0], slot, group).wait()

    @pl.when(expert >= 2)
    def _():
        for group in range(GROUPS):
            for copy in puts(expert - 2, slot, group):
                copy.wait()

    x, g, xt, gt = x_ref[0], g_ref[0], xt_ref[0], gt_ref[0]
    w_in, w_out = held[slot, 0], held[slot, 1]
    v = mm(x, w_in)
    grad = mm(g, w_out)
    square = v * v
    tanh = jnp.tanh(v * (0.7978845608028654 + 0.035677408136300125 * square))
    half = 0.5 + 0.5 * tanh
    active = (v * half).astype(low)
    slope = half + v * (half * (1.0 - tanh)) * (0.7978845608028654 + 0.10703222440890037 * square)
    pre_grad = (grad * slope).astype(low)
    made = mm_turned(active, w_out)
    back = mm_turned(pre_grad, w_in)
    if not first:
        made, back = made_in[0] + made, back_in[0] + back
    made_ref[0], back_ref[0] = made.astype(made_ref.dtype), back.astype(back_ref.dtype)
    sent[slot, 0] = mm(xt, pre_grad).astype(low)
    sent[slot, 1] = mm(gt, active).astype(low)
    for group in range(GROUPS):
        for copy in puts(expert, slot, group):
            copy.start()

    @pl.when(expert == experts - 1)
    def _():
        for group in range(GROUPS):
            for copy in puts(expert - 1, 1 - slot, group):
                copy.wait()
        for group in range(GROUPS):
            for copy in puts(expert, slot, group):
                copy.wait()


def run_experts(x, g, xt, gt, sums, sources, last, split):
    experts, slots, width = x.shape
    _, kinds, rows, columns = sources[0].shape
    shards = lax.axis_size(SHARD)
    units = GROUPS * rows * columns // width
    low = jnp.bfloat16
    flat = pl.BlockSpec((1, slots, width), lambda e: (e, 0, 0))
    turned = pl.BlockSpec((1, width, slots), lambda e: (e, 0, 0))
    anywhere = pl.BlockSpec(memory_space=pl.ANY)
    kept = low if last else jnp.float32
    first = sums is None
    given = () if first else tuple(sums)
    pieces = []
    if split > 0:
        pieces += [(GROUPS * shards, kinds, rows, split)]
    if split < columns:
        pieces += [(GROUPS // 2 * shards, kinds, rows, columns - split)] * 2
    return pl.pallas_call(
        partial(expert_kernel, first, last, split, len(sources)),
        grid=(experts,),
        in_specs=[flat, flat, turned, turned] + [flat] * len(given) + [anywhere] * len(sources),
        out_specs=[flat, flat] + [anywhere] * len(pieces),
        out_shape=[jax.ShapeDtypeStruct((experts, slots, width), kept)] * 2
        + [jax.ShapeDtypeStruct(piece, low) for piece in pieces],
        scratch_shapes=[
            pltpu.VMEM((2, kinds, width, units), low),
            pltpu.VMEM((2, kinds, width, units), low),
            pltpu.SemaphoreType.DMA((2, GROUPS)),
            pltpu.SemaphoreType.DMA((2, GROUPS, 2)),
        ],
        compiler_params=kernel_params(60),
        cost_estimate=cost(12 * experts * slots * width * units, 3e7),
        name="experts",
    )(x, g, xt, gt, *given, *sources)


def combine_kernel(
    experts, waits, slot_ref, made_ref, back_ref, hidden_ref, upstream_ref, second_ref, route_ref,
    norm_ref, router_ref, *refs
):
    output_ref, grad_ref, small_ref = refs[waits:]
    low = jnp.bfloat16
    image = pl.program_id(0)
    count, _, width = hidden_ref.shape
    tokens = count * PAD
    hidden = hidden_ref[...].reshape(tokens, width)
    upstream = upstream_ref[...].reshape(tokens, width).astype(jnp.float32)
    route_probs = route_ref[...].reshape(tokens, 128)
    slot_of = slot_ref[...].reshape(tokens, 128)
    slots = made_ref.shape[1]
    lanes = lax.broadcasted_iota(jnp.int32, (tokens, slots), 1)
    wide_lanes = lax.broadcasted_iota(jnp.int32, (tokens, 128), 1)
    total = hidden
    second_grad = jnp.zeros_like(hidden)
    prob_sum = jnp.zeros((tokens, 128), jnp.float32)
    gates = route_probs
    for e in range(experts):
        hot = jnp.where(lanes == slot_of[:, e : e + 1], 1.0, 0.0).astype(low)
        made = mm(hot, made_ref[e])
        second_grad = second_grad + mm(hot, back_ref[e])
        total = total + route_probs[:, e : e + 1] * made
        gate_grad = jnp.sum(upstream * made, axis=-1, keepdims=True)
        prob_sum = jnp.where(wide_lanes == e, gate_grad, prob_sum)
        gates = jnp.where(wide_lanes == experts + e, route_probs[:, e : e + 1], gates)
        prob_sum = jnp.where(wide_lanes == experts + e, gate_grad, prob_sum)
    length = output_ref.shape[1]
    for i in range(count):
        output_ref[i] = total[i * PAD : (i + 1) * PAD].astype(low)[:length]
    inner = jnp.sum(route_probs * prob_sum, axis=-1, keepdims=True)
    logit_grad = (gates * (prob_sum - inner)).astype(low)
    second_grad = second_grad + mm_turned(logit_grad, router_ref[...])
    unit, inverse = unit_of(hidden)
    grad = upstream + unit_backward(second_grad, unit, inverse, norm_ref[2:3])
    grad_ref[...] = grad.reshape(grad_ref.shape)
    router_grad = mm_rows(logit_grad, second_ref[...].reshape(tokens, width))[:8]
    gain = jnp.sum(second_grad * unit, axis=0, keepdims=True)
    bias = jnp.sum(second_grad, axis=0, keepdims=True)
    rows_of = lax.broadcasted_iota(jnp.int32, (8, hidden.shape[1]), 0)
    small = jnp.where(
        rows_of == 2, gain, jnp.where(rows_of == 3, bias, jnp.where(rows_of >= experts, router_grad, 0.0))
    )

    @pl.when(image == 0)
    def _():
        small_ref[...] = small

    @pl.when(image > 0)
    def _():
        small_ref[...] += small


def combine(length, experts, slot_column, made, back, hidden, upstream, second, route_probs, norm_params, router_wide, waits=()):
    images, _, width = hidden.shape
    low, wide = jnp.bfloat16, jnp.float32

    def per_image(*shape):
        return pl.BlockSpec((TOGETHER,) + shape, lambda i: (i,) + (0,) * len(shape))

    def whole(array):
        return pl.BlockSpec(array.shape, lambda i: (0,) * array.ndim)

    small = pl.BlockSpec((8, width), lambda i: (0, 0))
    return pl.pallas_call(
        partial(combine_kernel, experts, len(waits)),
        grid=(images // TOGETHER,),
        in_specs=[
            per_image(PAD, 128), whole(made), whole(back), per_image(PAD, width), per_image(PAD, width),
            per_image(PAD, width), per_image(PAD, 128), whole(norm_params), whole(router_wide),
        ]
        + [pl.BlockSpec(memory_space=pl.ANY)] * len(waits),
        out_specs=[per_image(length, width), per_image(PAD, width), small],
        out_shape=[
            jax.ShapeDtypeStruct((images, length, width), low),
            jax.ShapeDtypeStruct((images, PAD, width), wide),
            jax.ShapeDtypeStruct((8, width), wide),
        ],
        compiler_params=kernel_params(60),
        cost_estimate=cost(4 * images * PAD * experts * made.shape[1] * width, 2e7),
        name="combine",
    )(slot_column, made, back, hidden, upstream, second, route_probs, norm_params, router_wide, *waits)


def regroup(rows):
    return jnp.concatenate([rows[:, k : k + 128] for k in range(0, rows.shape[1], 128)], axis=0)


def two_terms(value):
    high = value.astype(jnp.bfloat16).astype(jnp.float32)
    less = (value - high).astype(jnp.bfloat16).astype(jnp.float32)
    return jnp.concatenate([high, less], axis=0).astype(jnp.bfloat16), high + less


def term_sum(terms):
    terms = terms.astype(jnp.float32)
    half = terms.shape[0] // 2
    return terms[:half] + terms[half:]


def attend_back_kernel(
    first, last, input_ref, norm_ref, dense_ref, normed_ref, projected_ref, probs_ref,
    context_ref, grad_ref, norm_grad_in, *refs
):
    low = jnp.bfloat16
    image, images = pl.program_id(0), pl.num_programs(0)
    if not first:
        sums_in = refs[0]
        refs = refs[2:]
    input_grad_ref, norm_grad_ref = refs[:2]
    if last:
        keep_ref, give_ref, sums, low_sums, packed, sems = refs[2:]
    else:
        sums = refs[2]

    @pl.when(image == 0)
    def _():
        sums[...] = jnp.zeros_like(sums) if first else sums_in[...]
        norm_grad_ref[...] = norm_grad_in[...]

    count, _, width = grad_ref.shape
    tokens = count * PAD
    hidden_grad = grad_ref[...].reshape(tokens, width)
    attended_low = hidden_grad.astype(low)
    context_grad = mm(attended_low, dense_ref[3]).astype(low)
    sums[3] += mm_rows(attended_low, context_ref[...].reshape(tokens, width))
    first_half = lax.broadcasted_iota(jnp.int32, (PAD, 2 * HEAD_DIM), 1) < HEAD_DIM
    zero = jnp.zeros((PAD, 2 * HEAD_DIM), low)
    scale = HEAD_DIM ** (-0.5)
    whole = [[], [], []]
    for i in range(count):
        parts = [[], [], []]
        for pair in range(width // (2 * HEAD_DIM)):
            at = slice(pair * 2 * HEAD_DIM, (pair + 1) * 2 * HEAD_DIM)
            query, key, value = (projected_ref[i, c, :, at] for c in range(3))
            grad = context_grad[i * PAD : (i + 1) * PAD, at]
            halves = []
            for side in range(2):
                mine = jnp.where(first_half == (side == 0), grad, zero)
                probs = probs_ref[i, 2 * pair + side]
                wide = probs.astype(jnp.float32)
                prob_grad = mm_turned(value, mine)
                weighted = wide * prob_grad
                score_grad = (
                    weighted - wide * jnp.sum(weighted, axis=0, keepdims=True)
                ).astype(low)
                query_grad = mm_rows(key, score_grad)[side * HEAD_DIM : (side + 1) * HEAD_DIM]
                halves.append((query_grad, mm(score_grad, query), mm(probs, grad)))
            parts[0].append((jnp.concatenate([halves[0][0], halves[1][0]], axis=0) * scale).T.astype(low))
            parts[1].append((jnp.where(first_half, halves[0][1], halves[1][1]) * scale).astype(low))
            parts[2].append(jnp.where(first_half, halves[0][2], halves[1][2]).astype(low))
        for kind in range(3):
            whole[kind].append(jnp.concatenate(parts[kind], axis=1))
    normed = normed_ref[...].reshape(tokens, width)
    normed_grad = None
    for kind in range(3):
        projected_grad = jnp.concatenate(whole[kind], axis=0)
        sums[kind] += mm_rows(normed, projected_grad)
        part = mm_turned(projected_grad, dense_ref[kind])
        normed_grad = part if normed_grad is None else normed_grad + part
    length = input_grad_ref.shape[1]
    gain, bias = 0.0, 0.0
    for i in range(count):
        unit, inverse = unit_of(input_ref[i].astype(jnp.float32))
        part = normed_grad[i * PAD : (i + 1) * PAD][:length]
        input_grad_ref[i] = hidden_grad[i * PAD : (i + 1) * PAD][:length] + unit_backward(
            part, unit, inverse, norm_ref[0:1]
        )
        gain = gain + jnp.sum(part * unit, axis=0, keepdims=True)
        bias = bias + jnp.sum(part, axis=0, keepdims=True)
    rows_of = lax.broadcasted_iota(jnp.int32, (8, width), 0)
    norm_grad_ref[...] += jnp.where(rows_of == 0, gain, jnp.where(rows_of == 1, bias, 0.0))

    if not last:
        return

    @pl.when(image == images - 1)
    def _():
        kinds, rows, columns = sums.shape[0], *keep_ref.shape[1:]
        near = keep_ref.shape[0] // kinds
        shards = near * 2 // GROUPS
        low_sums[...] = sums[...].astype(low)
        packed[...] = two_terms(regroup(norm_grad_ref[...]))[0]
        copies = [pltpu.make_async_copy(packed, give_ref.at[kinds * near], sems.at[2 * near])]
        for piece in range(2 * near):
            target = keep_ref if piece < near else give_ref
            copies.append(
                pltpu.make_async_copy(
                    dense_window(low_sums, piece, shards, rows, columns),
                    target.at[pl.ds(piece % near * kinds, kinds)],
                    sems.at[piece],
                )
            )
        for copy in copies:
            copy.start()
        for copy in copies:
            copy.wait()


def attend_back(which, count, block_input, norm_params, dense, kept, hidden_grad, norm_grad, carried, near_shape):
    images, length, width = block_input.shape
    heads = width // HEAD_DIM
    low, wide = jnp.bfloat16, jnp.float32
    first, last = carried is None, which + count == images
    near, kinds, rows, columns = near_shape

    def per_image(*shape):
        return pl.BlockSpec((1,) + shape, lambda i: (i + which,) + (0,) * len(shape))

    def whole(array):
        return pl.BlockSpec(array.shape, lambda i: (0,) * array.ndim)

    anywhere = pl.BlockSpec(memory_space=pl.ANY)
    small = pl.BlockSpec((8, width), lambda i: (0, 0))
    sum_shape = (4, width, width)
    given = () if first else tuple(carried)
    out_specs = [per_image(length, width), small]
    out_shape = [
        jax.ShapeDtypeStruct((images, length, width), wide),
        jax.ShapeDtypeStruct((8, width), wide),
    ]
    scratch = []
    if last:
        out_specs += [anywhere] * 2
        out_shape += [jax.ShapeDtypeStruct((near * kinds + k, rows, columns), low) for k in (0, 1)]
        scratch = [
            pltpu.VMEM(sum_shape, wide),
            pltpu.VMEM(sum_shape, low),
            pltpu.VMEM((rows, columns), low),
            pltpu.SemaphoreType.DMA((2 * near + 1,)),
        ]
    else:
        out_specs += [pl.BlockSpec(sum_shape, lambda i: (0, 0, 0))]
        out_shape += [jax.ShapeDtypeStruct(sum_shape, wide)]
    given_specs = [] if first else [whole(carried[0]), anywhere]
    return pl.pallas_call(
        partial(attend_back_kernel, first, last),
        grid=(count,),
        in_specs=[
            per_image(length, width), whole(norm_params), whole(dense),
            per_image(PAD, width), per_image(3, PAD, width), per_image(heads, PAD, PAD),
            per_image(PAD, width), per_image(PAD, width), small,
        ]
        + given_specs,
        out_specs=out_specs,
        out_shape=out_shape,
        scratch_shapes=scratch,
        input_output_aliases={} if first else {10: 0},
        compiler_params=kernel_params(60),
        cost_estimate=cost(count * 5e9, count * 6e6),
        name="attend_back",
    )(block_input, norm_params, dense, *kept, hidden_grad, norm_grad, *given)


def fold_core_kernel(quarter, keep_ref, come_ref, small_ref, x_ref, y_ref, both_ref, own_ref, own_small_ref):
    small = two_terms(regroup(small_ref[...]))[1] + term_sum(come_ref[4 * quarter])
    packed, own_small_ref[...] = two_terms(small)
    for k, target in enumerate((own_ref, x_ref, y_ref, both_ref)):
        at = slice(k * quarter, (k + 1) * quarter)
        total = keep_ref[at].astype(jnp.float32) + come_ref[at].astype(jnp.float32)
        target[:quarter] = total.astype(target.dtype)
        if k:
            target[quarter] = packed


def fold_core(keep, come, small):
    count, rows, columns = keep.shape
    quarter = count // 4
    message = jax.ShapeDtypeStruct((quarter + 1, rows, columns), jnp.bfloat16)
    return pl.pallas_call(
        partial(fold_core_kernel, quarter),
        out_shape=[message] * 3
        + [
            jax.ShapeDtypeStruct((quarter, rows, columns), jnp.float32),
            jax.ShapeDtypeStruct((rows // 2, columns), jnp.float32),
        ],
        compiler_params=kernel_params(24),
        cost_estimate=cost(1e6, 4e6),
        name="fold_core",
    )(keep, come, small)


def fold_sides_kernel(own_ref, small_ref, x_ref, y_ref, both_ref, *refs):
    messages, (total_ref, total_small_ref) = refs[:-2], refs[-2:]
    count = own_ref.shape[0]
    each = count // (len(messages) + 1)
    small = (small_ref[...] + term_sum(x_ref[count])) + (term_sum(y_ref[count]) + term_sum(both_ref[count]))
    packed, total_small_ref[...] = two_terms(small)
    for k, target in enumerate((total_ref, *messages)):
        at = slice(k * each, (k + 1) * each)
        total = own_ref[at] + sum(r[at].astype(jnp.float32) for r in (x_ref, y_ref, both_ref))
        target[:each] = total.astype(target.dtype)
        if k:
            target[each] = packed


def fold_sides(own, small, arrived, shards):
    count, rows, columns = own.shape
    each = count // shards
    message = jax.ShapeDtypeStruct((each + 1, rows, columns), jnp.bfloat16)
    return pl.pallas_call(
        fold_sides_kernel,
        out_shape=[message] * (shards - 1)
        + [jax.ShapeDtypeStruct((each, rows, columns), jnp.float32), jax.ShapeDtypeStruct(small.shape, jnp.float32)],
        compiler_params=kernel_params(24),
        cost_estimate=cost(1e6, 2e6),
        name="fold_sides",
    )(own, small, *arrived)


def dense_update_kernel(shards, own_ref, small_ref, *refs):
    arrived, refs = refs[: shards - 1], refs[shards - 1 :]
    kept, made = refs[:12], refs[12:]
    kinds = own_ref.shape[0]
    width = kept[0].shape[1]

    def update(group, at, gradient, rate, decay):
        old = [ref[at] for ref in kept[3 * group : 3 * group + 3]]
        new = adam_update(old[0], gradient, old[1], old[2], rate, decay)
        for ref, value in zip(made[3 * group : 3 * group + 3], new):
            ref[at] = value

    sums = [small_ref[...]] + [term_sum(r[kinds]) for r in arrived]
    while len(sums) > 1:
        sums = [a + b for a, b in zip(sums[::2], sums[1::2])]
    for k in range(width // 128):
        at = (slice(None), slice(k * 128, (k + 1) * 128))
        block = sums[0][k * 8 : (k + 1) * 8]
        update(0, at, block[:4], 0.25, 0.0)
        update(3, at, block[4:], 0.75 * width ** (-0.5), DECAY_RATE)
    for kind in range(kinds):
        gradient = own_ref[kind] + sum(r[kind].astype(jnp.float32) for r in arrived)
        if kind < kinds - 1:
            update(1, kind, gradient, 1.3 * width ** (-0.5), DECAY_RATE)
        else:
            update(2, (slice(None), slice(None)), gradient, 3.0 * width ** (-0.5), DECAY_RATE)


def dense_update(own, small, arrived, kept):
    return pl.pallas_call(
        partial(dense_update_kernel, len(arrived) + 1),
        out_shape=[jax.ShapeDtypeStruct(a.shape, a.dtype) for a in kept],
        compiler_params=kernel_params(24),
        cost_estimate=cost(1e6, 4e6),
        name="dense_update",
    )(own, small, *arrived, *kept)


def expert_update_kernel(first, experts, terms, *refs):
    parts, refs = refs[:terms], refs[terms:]
    kept, made = refs[:6], refs[6 if first else 12 :]
    width = 4 * kept[0].shape[1]
    rates = (1.0 * width ** (-0.5), 0.8 * experts * FF ** (-0.5))
    for kind in range(2):
        gradient = sum(r[kind].astype(jnp.float32) for r in parts)
        gradient = gradient if kind == 0 else gradient.T
        old = [ref[0] for ref in kept[3 * kind : 3 * kind + 3]]
        new = adam_update(old[0], gradient, old[1], old[2], rates[kind], DECAY_RATE)
        for ref, value in zip(made[3 * kind : 3 * kind + 3], new):
            ref[0] = value


def expert_update(parts, start, kept, before):
    _, rows, columns = parts[0].shape
    offset = start // 128
    anywhere = pl.BlockSpec(memory_space=pl.ANY)
    part = pl.BlockSpec((2, rows, 128), lambda j: (0, 0, j))
    into = pl.BlockSpec((1, rows, 128), lambda j: (0, 0, j + offset))
    out = pl.BlockSpec((1, 128, rows), lambda j: (0, j + offset, 0))
    specs = [into] * 3 + [out] * 3
    before = () if before is None else tuple(before)
    return pl.pallas_call(
        partial(expert_update_kernel, not before, lax.axis_size(SHARD), len(parts)),
        grid=(columns // 128,),
        in_specs=[part] * len(parts) + specs + [anywhere] * len(before),
        out_specs=specs,
        out_shape=[jax.ShapeDtypeStruct(a.shape, a.dtype) for a in kept],
        input_output_aliases={len(parts) + 6 + k: k for k in range(len(before))},
        compiler_params=kernel_params(24),
        cost_estimate=cost(1e6, 12 * 4 * rows * columns),
        name="expert_update",
    )(*parts, *kept, *before)


def join_sides_kernel(quarter, keep_x, keep_y, come_x, come_y, from_x, from_y, over_x, over_y):
    late = pl.program_id(0) >= quarter // 2
    x = keep_x[...].astype(jnp.float32) + come_x[...].astype(jnp.float32)
    y = keep_y[...].astype(jnp.float32) + come_y[...].astype(jnp.float32)
    over_x[...] = (x + jnp.where(late, from_y[...].astype(jnp.float32), 0.0)).astype(over_x.dtype)
    over_y[...] = (y + jnp.where(late, 0.0, from_x[...].astype(jnp.float32))).astype(over_y.dtype)


def join_sides(keep, come, from_x, from_y):
    count, *rest = keep.shape
    quarter = count // 4
    half = quarter // 2
    block = (1, *rest)

    def group(k):
        return pl.BlockSpec(block, lambda j: (k * quarter + j, 0, 0, 0))

    first = pl.BlockSpec(block, lambda j: (jnp.minimum(j, half - 1), 0, 0, 0))
    second = pl.BlockSpec(block, lambda j: (jnp.maximum(j - half, 0), 0, 0, 0))
    return pl.pallas_call(
        partial(join_sides_kernel, quarter),
        grid=(quarter,),
        in_specs=[group(1), group(2), group(1), group(2), first, second],
        out_specs=[pl.BlockSpec(block, lambda j: (j, 0, 0, 0))] * 2,
        out_shape=[jax.ShapeDtypeStruct((quarter, *rest), keep.dtype)] * 2,
        compiler_params=kernel_params(60),
        cost_estimate=cost(1e6, 8e6),
        name="join_sides",
    )(keep, keep, come, come, from_x, from_y)


def relay(block, axis, mask):
    size = lax.axis_size(axis)
    return lax.ppermute(block, axis, [(i, i ^ mask) for i in range(size)])


def relay_core(block):
    return relay(block, HEAD, 1)


def relay_x(block):
    return relay(block, HEAD, 2)


def relay_y(block):
    return relay(block, TENSOR, 1)


def relay_both(block):
    heads, tensors = lax.axis_size(HEAD), lax.axis_size(TENSOR)
    pairs = [
        (h * tensors + t, (h ^ 2) * tensors + (t ^ 1)) for h in range(heads) for t in range(tensors)
    ]
    return lax.ppermute(block, (HEAD, TENSOR), pairs)


def relay_line(blocks):
    return [relay(block, SHARD, k + 1) for k, block in enumerate(blocks)]


def ordered(values, *others):
    return lax.optimization_barrier((values, others))[0]


def wide_sum(*parts):
    return sum(p.astype(jnp.float32) for p in parts)


def local_plan(
    block_input,
    cotangent,
    routes,
    priority,
    norm_params,
    norm_moment,
    norm_square,
    qkv_weight,
    qkv_moment,
    qkv_square,
    attn_weight,
    attn_moment,
    attn_square,
    router_weight,
    router_moment,
    router_square,
    expert_in,
    in_moment,
    in_square,
    expert_out,
    out_moment,
    out_square,
):
    images, length, model_width = block_input.shape
    shards = experts = lax.axis_size(SHARD)
    capacity = 9 * images * length // (4 * experts)
    slots = -(-capacity // SLOT_PAD) * SLOT_PAD
    low = jnp.bfloat16

    dense_low = jnp.concatenate(
        [qkv_weight.transpose(1, 0, 2), attn_weight.T[None]], axis=0
    ).astype(low)
    dense_column = jnp.stack([dense_low] + relay_line([dense_low] * (shards - 1)))
    expert_low = jnp.stack([expert_in[0], expert_out[0].T]).astype(low)
    edges = [expert_low.shape[2] * edge // CUTS[-1] for edge in CUTS]
    chunks = [expert_low[:, :, i:j] for i, j in zip(edges, edges[1:])]
    tables = slot_tables(routes, priority)
    router_wide = jnp.pad(router_weight, ((0, 0), (0, 128 - experts))).astype(low)

    def line_of(block):
        return jnp.stack([block] + relay_line([block] * (shards - 1)))

    def across(column):
        return (relay_x(column), relay_y(column), relay_both(column))

    dense_column, tables, chunks[0] = ordered((dense_column, tables, chunks[0]))
    dense_sides, dense_far = across(dense_column), (relay_core(dense_column),)
    column = line_of(chunks[0])
    later = lax.all_gather(chunks[1], (SHARD, HEAD, TENSOR))
    slot_row, slot_column = find_slots(tables, experts, capacity)
    slot_column = slot_column.reshape(images, PAD, 128)
    dense_sides, dense_far, slot_row = ordered((dense_sides, dense_far, slot_row))
    dense_far += tuple(relay_core(s) for s in dense_sides)
    dense = join_dense((dense_column, *dense_sides, *dense_far), model_width)

    half = shards // 2
    column, dense = ordered((column, dense))
    over_x, over_y, far_column = relay_x(column), relay_y(column), relay_core(column)
    normed, projected, probs, context, hidden, second, route_probs, upstream = attend(
        experts, block_input, cotangent, norm_params, dense, router_wide
    )

    over_x, over_y, far_column, second = ordered((over_x, over_y, far_column, second))
    corners = (relay_y(over_x[:half]), relay_x(over_y[half:]))
    near, far = (column, over_x, over_y), (far_column, relay_core(over_x), relay_core(over_y))
    tokens = images * PAD
    slot_rows = dispatch(
        slot_row, second.reshape(tokens, model_width), upstream.reshape(tokens, model_width),
        route_probs.reshape(tokens, 128), experts, slots,
    )

    corners, far, slot_rows = ordered((corners, far, slot_rows))
    weights_a = (*near, *corners, *far, *(relay_core(c) for c in corners))
    quarter = shards

    class Returning:
        def __init__(self, keep, give):
            self.keep, self.come = keep, relay_core(give)

        def some(self, first, count):
            at = slice(first, first + count)
            return wide_sum(self.keep[at], self.come[at])

        def part(self, k):
            return self.some(k * quarter, quarter)

        def corner(self):
            half = quarter // 2
            self.corners = (
                relay_x(self.some(3 * quarter, half).astype(low)),
                relay_y(self.some(3 * quarter + half, quarter - half).astype(low)),
            )

        def sides(self):
            over_x, over_y = join_sides(self.keep, self.come, *self.corners)
            self.over = (relay_x(over_x), relay_y(over_y))

        def line(self):
            total = self.part(0) + wide_sum(*self.over)
            self.own = total[0]
            self.others = relay_line([total[k].astype(low) for k in range(1, quarter)])

        def result(self):
            return self.own + wide_sum(*self.others)

    made, backed, grads = run_experts(*slot_rows, None, weights_a, False, edges[1])

    made, grads, later = ordered((made, grads, later))
    own_a = lax.psum_scatter(grads, (HEAD, TENSOR), scatter_dimension=0, tiled=True)
    made, backed, keep, give = run_experts(*slot_rows, (made, backed), (later,), True, 0)

    made, keep, give = ordered((made, keep, give))
    sum_b = Returning(keep, give)
    block_output, hidden_grad, norm_grad = combine(
        length, experts, slot_column, made, backed, hidden, upstream, second, route_probs,
        norm_params, router_wide,
    )

    sum_b.keep, sum_b.come, hidden_grad = ordered((sum_b.keep, sum_b.come, hidden_grad))
    sum_b.corner()
    kept = (normed, projected, probs, context)
    half = images // 2
    dense_shape = (4 * quarter, *dense_low.shape)
    input_grad, norm_grad, dense_sums = attend_back(
        0, half, block_input, norm_params, dense, kept, hidden_grad, norm_grad, None, (4 * quarter, *dense_low.shape)
    )

    sum_b.corners, own_a, norm_grad, dense_sums = ordered((sum_b.corners, own_a, norm_grad, dense_sums))
    others_a = relay_line([own_a[k] for k in range(1, quarter)])
    sum_b.sides()
    input_grad, norm_grad, keep, give = attend_back(
        half, images - half, block_input, norm_params, dense, kept, hidden_grad, norm_grad,
        (dense_sums, input_grad), (4 * quarter, *dense_low.shape),
    )

    sum_b.over, others_a, keep, give = ordered((sum_b.over, others_a, keep, give))
    come = relay_core(give)
    sum_b.line()
    come, sum_b.own = ordered((come, sum_b.own))
    *messages, own, own_small = fold_core(keep, come, norm_grad)
    arrived = [send(m) for m, send in zip(messages, (relay_x, relay_y, relay_both))]
    messages, own_a, others_a = ordered((messages, own_a, others_a))
    expert_kept = (expert_in, in_moment, in_square, expert_out, out_moment, out_square)
    updated = expert_update([own_a[0], *others_a], 0, expert_kept, None)
    arrived, updated = ordered((arrived, updated))
    *messages, own, own_small = fold_sides(own, own_small, arrived, shards)
    arrived = relay_line(messages)
    updated = expert_update([sum_b.own, *sum_b.others], edges[1], expert_kept, updated)
    arrived, updated = ordered((arrived, updated))
    turns = ((0, 1), (1, 0, 2), (1, 0), (1, 0))
    dense_kept = (
        (norm_params, norm_moment, norm_square),
        (qkv_weight, qkv_moment, qkv_square),
        (attn_weight, attn_moment, attn_square),
        (router_weight, router_moment, router_square),
    )
    flat = [a.transpose(t) for t, group in zip(turns, dense_kept) for a in group]
    dense_new = dense_update(own, own_small, arrived, flat)
    dense_new = [a.transpose(turns[k // 3]) for k, a in enumerate(dense_new)]
    return (block_output, input_grad, *dense_new, *updated)


def solution(mesh):
    fits = mesh.shape[SHARD] <= 4
    return jax.shard_map(
        local_plan if fits else slot_plan,
        mesh=mesh,
        in_specs=(
            P((SHARD, HEAD, TENSOR), None, None),
            P((SHARD, HEAD, TENSOR), None, None),
            P((SHARD, HEAD, TENSOR), None, None),
            P((SHARD, HEAD, TENSOR), None),
            P(),
            P(),
            P(),
            P((SHARD, TENSOR), None, HEAD),
            P((SHARD, TENSOR), None, HEAD),
            P((SHARD, TENSOR), None, HEAD),
            P(HEAD, (SHARD, TENSOR)),
            P(HEAD, (SHARD, TENSOR)),
            P(HEAD, (SHARD, TENSOR)),
            P(),
            P(),
            P(),
            P(SHARD, HEAD, TENSOR),
            P(SHARD, HEAD, TENSOR),
            P(SHARD, HEAD, TENSOR),
            P(SHARD, TENSOR, HEAD),
            P(SHARD, TENSOR, HEAD),
            P(SHARD, TENSOR, HEAD),
        ),
        out_specs=(
            P((SHARD, HEAD, TENSOR), None, None),
            P((SHARD, HEAD, TENSOR), None, None),
            P(),
            P(),
            P(),
            P((SHARD, TENSOR), None, HEAD),
            P((SHARD, TENSOR), None, HEAD),
            P((SHARD, TENSOR), None, HEAD),
            P(HEAD, (SHARD, TENSOR)),
            P(HEAD, (SHARD, TENSOR)),
            P(HEAD, (SHARD, TENSOR)),
            P(),
            P(),
            P(),
            P(SHARD, HEAD, TENSOR),
            P(SHARD, HEAD, TENSOR),
            P(SHARD, HEAD, TENSOR),
            P(SHARD, TENSOR, HEAD),
            P(SHARD, TENSOR, HEAD),
            P(SHARD, TENSOR, HEAD),
        ),
        check_vma=False,
    )
```

```python
import math
from functools import partial

import jax
import jax.numpy as jnp
from jax import lax
from jax.experimental import pallas as pl
from jax.experimental.pallas import tpu as pltpu
from jax.sharding import PartitionSpec as P

SHARD, HEAD, TENSOR = "shard", "head", "tensor"
HEAD_DIM = 64
FF = 2048
STEP = 10


EPS_NORM = 1e-06
BETA_ONE = 0.9
BETA_TWO = 0.999
ADAM_EPS = 1e-08
DECAY_RATE = 0.1


def norm_forward(values, gain_row, bias_row):
    center = jnp.mean(values, axis=-1, keepdims=True)
    shifted = values - center
    inverse = lax.rsqrt(jnp.mean(shifted * shifted, axis=-1, keepdims=True) + EPS_NORM)
    unit_rows = shifted * inverse
    return (unit_rows * gain_row + bias_row, unit_rows, inverse)


def norm_backward(grad_rows, unit_rows, inverse, gain_row):
    scaled = grad_rows * gain_row
    inner_grad = (
        scaled
        - jnp.mean(scaled, axis=-1, keepdims=True)
        - unit_rows * jnp.mean(scaled * unit_rows, axis=-1, keepdims=True)
    )
    return (
        inner_grad * inverse,
        jnp.sum(grad_rows * unit_rows, axis=0),
        jnp.sum(grad_rows, axis=0),
    )


def gelu_grad(pre_act, upstream):
    result, pullback = jax.vjp(partial(jax.nn.gelu, approximate=True), pre_act)
    return pullback(upstream)[0]


def adam_update(weight, gradient, moment, square, step_rate, decay_rate):
    moment_new = BETA_ONE * moment + (1.0 - BETA_ONE) * gradient
    square_new = BETA_TWO * square + (1.0 - BETA_TWO) * gradient * gradient
    first_hat = moment_new / (1.0 - BETA_ONE**STEP)
    second_hat = square_new / (1.0 - BETA_TWO**STEP)
    weight_new = weight - step_rate * (
        first_hat / (jnp.sqrt(second_hat) + ADAM_EPS) + decay_rate * weight
    )
    return (weight_new, moment_new, square_new)


def send_rows(parcel):
    copies = jnp.broadcast_to(
        parcel[:, None], (parcel.shape[0], lax.axis_size(TENSOR)) + parcel.shape[1:]
    )
    flat_copies = copies.reshape((-1,) + parcel.shape[1:])
    arrived = lax.all_to_all(
        flat_copies, (SHARD, TENSOR), split_axis=0, concat_axis=0, tiled=True
    )
    return arrived.reshape(copies.shape)


def return_rows(partial_rows):
    flat_rows = partial_rows.reshape((-1,) + partial_rows.shape[2:])
    arrived = lax.all_to_all(
        flat_rows.astype(jnp.bfloat16), (SHARD, TENSOR), split_axis=0, concat_axis=0, tiled=True
    ).astype(flat_rows.dtype)
    return jnp.sum(arrived.reshape(partial_rows.shape), axis=1)


def slot_plan(
    block_input,
    cotangent,
    routes,
    priority,
    norm_params,
    norm_moment,
    norm_square,
    qkv_weight,
    qkv_moment,
    qkv_square,
    attn_weight,
    attn_moment,
    attn_square,
    router_weight,
    router_moment,
    router_square,
    expert_in,
    in_moment,
    in_square,
    expert_out,
    out_moment,
    out_square,
):
    images, length, model_width = block_input.shape
    row_count = images * length
    local_experts = expert_in.shape[0]
    shards = lax.axis_size(SHARD)
    experts = local_experts * shards
    capacity = 9 * row_count // (4 * experts)
    score_scale = HEAD_DIM ** (-0.5)
    full_qkv, full_attn = (
        lax.all_gather(qkv_weight.astype(jnp.bfloat16), (SHARD, TENSOR), axis=0, tiled=True),
        lax.all_gather(attn_weight.astype(jnp.bfloat16), (SHARD, TENSOR), axis=1, tiled=True),
    )
    inputs = block_input.astype(jnp.float32).reshape(row_count, model_width)
    normed, unit_one, inverse_one = norm_forward(inputs, norm_params[0], norm_params[1])
    normed_low = normed.astype(jnp.bfloat16).reshape(images, length, model_width)
    gathered, hidden_in, hidden_out = (
        lax.all_gather(normed_low, HEAD, axis=0, tiled=True),
        lax.all_gather(expert_in.astype(jnp.bfloat16), HEAD, axis=1, tiled=True),
        lax.all_gather(expert_out.astype(jnp.bfloat16), HEAD, axis=2, tiled=True),
    )
    local_heads = full_qkv.shape[2] // HEAD_DIM
    all_images = gathered.shape[0]
    head_shape = (all_images, length, local_heads, HEAD_DIM)
    projected = jnp.einsum(
        "isd,dcn->iscn", gathered, full_qkv, preferred_element_type=jnp.float32
    ).astype(jnp.bfloat16)
    queries = projected[:, :, 0].reshape(head_shape)
    key_rows = projected[:, :, 1].reshape(head_shape)
    value_rows = projected[:, :, 2].reshape(head_shape)
    scores = (
        jnp.einsum("iqhe,ikhe->ihqk", queries, key_rows, preferred_element_type=jnp.float32)
        * score_scale
    )
    score_top = jnp.max(scores, axis=-1, keepdims=True)
    log_total = score_top + jnp.log(jnp.sum(jnp.exp(scores - score_top), axis=-1, keepdims=True))
    probs_low = jnp.exp(scores - log_total).astype(jnp.bfloat16)
    context = jnp.einsum(
        "ihqk,ikhe->iqhe", probs_low, value_rows, preferred_element_type=jnp.float32
    ).astype(jnp.bfloat16)
    context = context.reshape(all_images * length, local_heads * HEAD_DIM)
    attended = lax.psum_scatter(
        jnp.dot(context, full_attn, preferred_element_type=jnp.float32).astype(jnp.bfloat16),
        HEAD,
        scatter_dimension=0,
        tiled=True,
    ).astype(jnp.float32)
    hidden = inputs + attended
    normed_two, unit_two, inverse_two = norm_forward(hidden, norm_params[2], norm_params[3])
    second_low = normed_two.astype(jnp.bfloat16)
    router_low = router_weight.astype(jnp.bfloat16)
    logits = jnp.dot(second_low, router_low, preferred_element_type=jnp.float32)
    route_probs = jax.nn.softmax(logits, axis=-1)
    route_hot = (
        routes.reshape(row_count, 2)[:, :, None]
        == jnp.arange(experts, dtype=jnp.int32)[None, None, :]
    ).astype(jnp.float32)
    gate_values = jnp.sum(route_probs[:, None, :] * route_hot, axis=-1)
    expert_ids = routes.reshape(2 * row_count)
    rank_values = priority[0]
    pair_hot = route_hot.reshape(2 * row_count, experts)
    earlier = (rank_values[None, :] < rank_values[:, None]).astype(jnp.bfloat16)
    counts = jnp.dot(earlier, pair_hot.astype(jnp.bfloat16), preferred_element_type=jnp.float32)
    slot_index = jnp.sum(counts * pair_hot, axis=1).astype(jnp.int32)
    target = jnp.where(
        slot_index < capacity, expert_ids * capacity + slot_index, experts * capacity
    )
    filler = jnp.full((experts * capacity,), 2 * row_count, jnp.int32)
    owner_pair = filler.at[target].set(jnp.arange(2 * row_count, dtype=jnp.int32), mode="drop")
    padded = jnp.concatenate([second_low, jnp.zeros((1, model_width), jnp.bfloat16)], axis=0)
    parcel = padded[owner_pair // 2].reshape(shards, local_experts, capacity, model_width)
    arrived = send_rows(parcel)
    pre_act = jnp.einsum("stecd,edf->stecf", arrived, hidden_in, preferred_element_type=jnp.float32)
    active = jax.nn.gelu(pre_act, approximate=True).astype(jnp.bfloat16)
    part_rows = jnp.einsum(
        "stecf,efd->stecd", active, hidden_out, preferred_element_type=jnp.float32
    )
    expert_rows = return_rows(part_rows).reshape(experts * capacity, model_width)
    padded_out = jnp.concatenate([expert_rows, jnp.zeros((1, model_width), jnp.float32)], axis=0)
    per_pair = padded_out[target].reshape(row_count, 2, model_width)
    block_sum = hidden + jnp.sum(gate_values[:, :, None] * per_pair, axis=1)
    block_output = block_sum.astype(jnp.bfloat16).reshape(images, length, model_width)
    upstream = cotangent.astype(jnp.float32).reshape(row_count, model_width)
    pair_grad = (
        (gate_values[:, :, None] * upstream[:, None, :])
        .astype(jnp.bfloat16)
        .reshape(2 * row_count, model_width)
    )
    gate_grad = jnp.sum(upstream[:, None, :] * per_pair, axis=-1)
    padded_grad = jnp.concatenate([pair_grad, jnp.zeros((1, model_width), jnp.bfloat16)], axis=0)
    grad_parcel = padded_grad[owner_pair].reshape(shards, local_experts, capacity, model_width)
    grad_arrived = send_rows(grad_parcel)
    grad_out_part = jnp.einsum(
        "stecf,stecd->efd", active, grad_arrived, preferred_element_type=jnp.float32
    )
    active_grad = jnp.einsum(
        "stecd,efd->stecf", grad_arrived, hidden_out, preferred_element_type=jnp.float32
    )
    pre_grad = gelu_grad(pre_act, active_grad).astype(jnp.bfloat16)
    grad_in_part = jnp.einsum(
        "stecd,stecf->edf", arrived, pre_grad, preferred_element_type=jnp.float32
    )
    row_grad = jnp.einsum(
        "stecf,edf->stecd", pre_grad, hidden_in, preferred_element_type=jnp.float32
    )
    slot_grad = return_rows(row_grad).reshape(experts * capacity, model_width)
    padded_slot = jnp.concatenate([slot_grad, jnp.zeros((1, model_width), jnp.float32)], axis=0)
    second_grad = jnp.sum(padded_slot[target].reshape(row_count, 2, model_width), axis=1)
    prob_sum = jnp.sum(gate_grad[:, :, None] * route_hot, axis=1)
    logit_grad = (
        route_probs * (prob_sum - jnp.sum(route_probs * prob_sum, axis=-1, keepdims=True))
    ).astype(jnp.bfloat16)
    router_grad = jnp.einsum(
        "rd,re->de", second_low, logit_grad, preferred_element_type=jnp.float32
    )
    second_grad = second_grad + jnp.einsum(
        "re,de->rd", logit_grad, router_low, preferred_element_type=jnp.float32
    )
    hidden_part, gain_two, bias_two = norm_backward(
        second_grad, unit_two, inverse_two, norm_params[2]
    )
    hidden_grad = upstream + hidden_part
    attended_grad = lax.all_gather(hidden_grad.astype(jnp.bfloat16), HEAD, axis=0, tiled=True)
    attn_grad = jnp.einsum("rn,rd->nd", context, attended_grad, preferred_element_type=jnp.float32)
    context_grad = jnp.einsum(
        "rd,nd->rn", attended_grad, full_attn, preferred_element_type=jnp.float32
    ).astype(jnp.bfloat16)
    context_grad = context_grad.reshape(head_shape)
    scores_again = (
        jnp.einsum("iqhe,ikhe->ihqk", queries, key_rows, preferred_element_type=jnp.float32)
        * score_scale
    )
    probs_full = jnp.exp(scores_again - log_total)
    prob_grad = jnp.einsum(
        "iqhe,ikhe->ihqk", context_grad, value_rows, preferred_element_type=jnp.float32
    )
    score_grad = (
        probs_full * (prob_grad - jnp.sum(probs_full * prob_grad, axis=-1, keepdims=True))
    ).astype(jnp.bfloat16)
    query_grad = (
        jnp.einsum("ihqk,ikhe->iqhe", score_grad, key_rows, preferred_element_type=jnp.float32)
        * score_scale
    )
    key_grad = (
        jnp.einsum("ihqk,iqhe->ikhe", score_grad, queries, preferred_element_type=jnp.float32)
        * score_scale
    )
    value_grad = jnp.einsum(
        "ihqk,iqhe->ikhe", probs_low, context_grad, preferred_element_type=jnp.float32
    )
    projected_grad = (
        jnp.stack([query_grad, key_grad, value_grad], axis=2)
        .reshape(all_images, length, 3, local_heads * HEAD_DIM)
        .astype(jnp.bfloat16)
    )
    qkv_grad = jnp.einsum(
        "isd,iscn->dcn", gathered, projected_grad, preferred_element_type=jnp.float32
    )
    normed_part = jnp.einsum(
        "iscn,dcn->isd", projected_grad, full_qkv, preferred_element_type=jnp.float32
    )
    normed_grad, in_grad, out_grad = (
        lax.psum_scatter(
            normed_part.astype(jnp.bfloat16), HEAD, scatter_dimension=0, tiled=True
        ).astype(jnp.float32),
        lax.psum_scatter(
            grad_in_part.astype(jnp.bfloat16), HEAD, scatter_dimension=1, tiled=True
        ).astype(jnp.float32),
        lax.psum_scatter(
            grad_out_part.astype(jnp.bfloat16), HEAD, scatter_dimension=2, tiled=True
        ).astype(jnp.float32),
    )
    input_part, gain_one, bias_one = norm_backward(
        normed_grad.reshape(row_count, model_width), unit_one, inverse_one, norm_params[0]
    )
    input_grad = (hidden_grad + input_part).reshape(images, length, model_width)
    norm_grad = jnp.stack([gain_one, bias_one, gain_two, bias_two])
    norm_grad, router_grad = lax.psum((norm_grad, router_grad), (SHARD, HEAD, TENSOR))
    qkv_grad, attn_grad = (
        lax.psum_scatter(qkv_grad, (SHARD, TENSOR), scatter_dimension=0, tiled=True),
        lax.psum_scatter(attn_grad, (SHARD, TENSOR), scatter_dimension=1, tiled=True),
    )
    norm_new = adam_update(norm_params, norm_grad, norm_moment, norm_square, 0.25, 0.0)
    qkv_new = adam_update(
        qkv_weight, qkv_grad, qkv_moment, qkv_square, 1.3 * model_width ** (-0.5), DECAY_RATE
    )
    attn_new = adam_update(
        attn_weight, attn_grad, attn_moment, attn_square, 3.0 * model_width ** (-0.5), DECAY_RATE
    )
    router_new = adam_update(
        router_weight,
        router_grad,
        router_moment,
        router_square,
        0.75 * model_width ** (-0.5),
        DECAY_RATE,
    )
    in_new = adam_update(
        expert_in, in_grad, in_moment, in_square, 1.0 * model_width ** (-0.5), DECAY_RATE
    )
    out_new = adam_update(
        expert_out, out_grad, out_moment, out_square, 0.8 * experts * FF ** (-0.5), DECAY_RATE
    )
    return (
        block_output,
        input_grad,
        norm_new[0],
        norm_new[1],
        norm_new[2],
        qkv_new[0],
        qkv_new[1],
        qkv_new[2],
        attn_new[0],
        attn_new[1],
        attn_new[2],
        router_new[0],
        router_new[1],
        router_new[2],
        in_new[0],
        in_new[1],
        in_new[2],
        out_new[0],
        out_new[1],
        out_new[2],
    )


PAD = 208
SLOT_PAD = 16
CUTS = (0, 3, 8)
TOGETHER = 2


def kernel_params(megabytes):
    return pltpu.CompilerParams(vmem_limit_bytes=megabytes << 20)


def cost(flops, moved):
    return pl.CostEstimate(flops=int(flops), bytes_accessed=int(moved), transcendentals=0)


def mm(left, right):
    return lax.dot_general(left, right, (((1,), (0,)), ((), ())), preferred_element_type=jnp.float32)


def mm_turned(left, right):
    return lax.dot_general(left, right, (((1,), (1,)), ((), ())), preferred_element_type=jnp.float32)


def mm_rows(left, right):
    return lax.dot_general(left, right, (((0,), (0,)), ((), ())), preferred_element_type=jnp.float32)


def unit_of(values):
    center = jnp.mean(values, axis=-1, keepdims=True)
    shifted = values - center
    inverse = lax.rsqrt(jnp.mean(shifted * shifted, axis=-1, keepdims=True) + EPS_NORM)
    return (shifted * inverse, inverse)


def unit_backward(grad_rows, unit_rows, inverse, gain_row):
    scaled = grad_rows * gain_row
    inner_grad = (
        scaled
        - jnp.mean(scaled, axis=-1, keepdims=True)
        - unit_rows * jnp.mean(scaled * unit_rows, axis=-1, keepdims=True)
    )
    return inner_grad * inverse


def absolute(group):
    tensor = lax.axis_index(TENSOR) ^ (group // 2 % 2)
    head = lax.axis_index(HEAD) ^ (2 * (group % 2) + group // 4)
    return tensor, head


GROUPS = 8


def slot_kernel(experts, capacity, row_ref, column_ref, slot_row_ref, slot_column_ref):
    none = 1 << 20
    tokens = row_ref.shape[1]
    lanes = lax.broadcasted_iota(jnp.int32, (PAD, 128), 1)
    rows_of = lax.broadcasted_iota(jnp.int32, (8, tokens), 0)

    def ranks(named, rank, expert):
        return jnp.where(
            named[0] == expert, rank[0], jnp.where(named[1] == expert, rank[1], none)
        )

    routes_row, ranks_row = (row_ref[0:1], row_ref[1:2]), (row_ref[2:3], row_ref[3:4])
    all_rows = jnp.full((8, tokens), -1, jnp.int32)
    row_of = [ranks(routes_row, ranks_row, e) for e in range(experts)]
    totals = [jnp.zeros((1, tokens), jnp.float32) for e in range(experts)]
    for block in range(tokens // PAD):
        part = column_ref[block * PAD : (block + 1) * PAD]
        routes_col, ranks_col = (part[:, 0:1], part[:, 1:2]), (part[:, 2:3], part[:, 3:4])
        result = jnp.full((PAD, 128), -1, jnp.int32)
        for e in range(experts):
            column = ranks(routes_col, ranks_col, e)
            totals[e] = totals[e] + jnp.sum(
                jnp.where(column < row_of[e], 1.0, 0.0), axis=0, keepdims=True
            )
            before = jnp.sum(
                jnp.where(row_of[e] < column, 1.0, 0.0), axis=1, keepdims=True
            ).astype(jnp.int32)
            slot = jnp.where((column < none) & (before < capacity), before, -1)
            result = jnp.where(lanes == e, slot, result)
        slot_column_ref[block * PAD : (block + 1) * PAD] = result
    for e in range(experts):
        before = totals[e].astype(jnp.int32)
        slot = jnp.where((row_of[e] < none) & (before < capacity), before, -1)
        all_rows = jnp.where(rows_of == e, slot, all_rows)
    slot_row_ref[...] = all_rows


def slot_tables(routes, priority):
    images, length, _ = routes.shape
    tokens = images * PAD
    table = jnp.concatenate([routes, priority.reshape(images, length, 2)], axis=2)
    table = jnp.pad(table, ((0, 0), (0, PAD - length), (0, 0)), constant_values=-1)
    table = table.reshape(tokens, 4)
    columns = jnp.pad(table, ((0, 0), (0, 4)))
    return (columns.T, columns)


def find_slots(tables, experts, capacity):
    tokens = tables[1].shape[0]
    return pl.pallas_call(
        partial(slot_kernel, experts, capacity),
        out_shape=(
            jax.ShapeDtypeStruct((8, tokens), jnp.int32),
            jax.ShapeDtypeStruct((tokens, 128), jnp.int32),
        ),
        compiler_params=kernel_params(32),
        cost_estimate=cost(1e10, 1e6),
        name="find_slots",
    )(*tables)


def dense_window(ref, piece, shards, rows, columns):
    tensor, head = absolute(piece // shards)
    shard = lax.axis_index(SHARD) ^ (piece % shards)
    down = pl.multiple_of((shard * lax.axis_size(TENSOR) + tensor) * rows, rows)
    over = pl.multiple_of(head * columns, columns)
    return ref.at[:, pl.ds(down, rows), pl.ds(over, columns)]


def dense_kernel(*refs):
    groups, (full_ref, sems) = refs[:GROUPS], refs[GROUPS:]
    shards, kinds, rows, columns = groups[0].shape
    copies = []
    for piece in range(GROUPS * shards):
        copies.append(
            pltpu.make_async_copy(
                groups[piece // shards].at[piece % shards],
                dense_window(full_ref, piece, shards, rows, columns),
                sems.at[piece],
            )
        )
    for copy in copies:
        copy.start()
    for copy in copies:
        copy.wait()


def join_dense(groups, model_width):
    shards, kinds = groups[0].shape[:2]
    return pl.pallas_call(
        dense_kernel,
        out_shape=jax.ShapeDtypeStruct((kinds, model_width, model_width), groups[0].dtype),
        in_specs=[pl.BlockSpec(memory_space=pl.ANY)] * GROUPS,
        out_specs=pl.BlockSpec(memory_space=pltpu.VMEM),
        scratch_shapes=[pltpu.SemaphoreType.DMA((GROUPS * shards,))],
        compiler_params=kernel_params(16),
        cost_estimate=cost(1e6, 4e6),
        name="join_dense",
    )(*groups)


def attend_kernel(
    length, experts, input_ref, cotangent_ref, norm_ref, dense_ref, router_ref,
    normed_ref, projected_ref, probs_ref, context_ref, hidden_ref, second_ref, route_ref, upstream_ref, whole,
):
    low = jnp.bfloat16
    count, width = input_ref.shape[0], input_ref.shape[2]
    whole[...] = jnp.zeros_like(whole)
    for i in range(count):
        whole[i * PAD : i * PAD + length] = cotangent_ref[i].astype(jnp.float32)
    upstream_ref[...] = whole[...].astype(low).reshape(upstream_ref.shape)
    for i in range(count):
        whole[i * PAD : i * PAD + length] = input_ref[i].astype(jnp.float32)
    values = whole[...]
    unit, _ = unit_of(values)
    normed = (unit * norm_ref[0:1] + norm_ref[1:2]).astype(low)
    normed_ref[...] = normed.reshape(normed_ref.shape)
    queries, key_rows, value_rows = (mm(normed, dense_ref[c]).astype(low) for c in range(3))
    first_half = lax.broadcasted_iota(jnp.int32, (PAD, 2 * HEAD_DIM), 1) < HEAD_DIM
    is_key = lax.broadcasted_iota(jnp.int32, (PAD, PAD), 0) < length
    zero = jnp.zeros((PAD, 2 * HEAD_DIM), low)
    contexts = []
    for i in range(count):
        rows = slice(i * PAD, (i + 1) * PAD)
        for c, part in enumerate((queries, key_rows, value_rows)):
            projected_ref[i, c] = part[rows]
        pairs = []
        for pair in range(width // (2 * HEAD_DIM)):
            at = slice(pair * 2 * HEAD_DIM, (pair + 1) * 2 * HEAD_DIM)
            query, key, value = queries[rows, at], key_rows[rows, at], value_rows[rows, at]
            halves = []
            for side in range(2):
                mine = jnp.where(first_half == (side == 0), query, zero)
                scores = mm_turned(key, mine) * (HEAD_DIM ** (-0.5))
                scores = jnp.where(is_key, scores, -1e30)
                top = jnp.max(scores, axis=0, keepdims=True)
                raised = jnp.exp(scores - top)
                probs = (raised / jnp.sum(raised, axis=0, keepdims=True)).astype(low)
                probs_ref[i, 2 * pair + side] = probs
                halves.append(mm_rows(value, probs)[side * HEAD_DIM : (side + 1) * HEAD_DIM])
            pairs.append(jnp.concatenate(halves, axis=0).T.astype(low))
        contexts.append(jnp.concatenate(pairs, axis=1))
    context = jnp.concatenate(contexts, axis=0)
    context_ref[...] = context.reshape(context_ref.shape)
    hidden = values + mm_turned(context, dense_ref[3])
    hidden_ref[...] = hidden.reshape(hidden_ref.shape)
    unit, _ = unit_of(hidden)
    second = (unit * norm_ref[2:3] + norm_ref[3:4]).astype(low)
    second_ref[...] = second.reshape(second_ref.shape)
    logits = mm(second, router_ref[...])
    is_expert = lax.broadcasted_iota(jnp.int32, logits.shape, 1) < experts
    logits = jnp.where(is_expert, logits, -1e30)
    raised = jnp.exp(logits - jnp.max(logits, axis=-1, keepdims=True))
    route_probs = raised / jnp.sum(raised, axis=-1, keepdims=True)
    route_ref[...] = route_probs.reshape(route_ref.shape)


def attend(experts, block_input, cotangent, norm_params, dense, router_wide):
    images, length, width = block_input.shape
    heads = width // HEAD_DIM
    low, wide = jnp.bfloat16, jnp.float32

    def per_image(*shape):
        return pl.BlockSpec((TOGETHER,) + shape, lambda i: (i,) + (0,) * len(shape))

    def whole(array):
        return pl.BlockSpec(array.shape, lambda i: (0,) * array.ndim)

    shapes = [
        ((PAD, width), low), ((3, PAD, width), low), ((heads, PAD, PAD), low), ((PAD, width), low),
        ((PAD, width), wide), ((PAD, width), low), ((PAD, 128), wide), ((PAD, width), low),
    ]
    return pl.pallas_call(
        partial(attend_kernel, length, experts),
        grid=(images // TOGETHER,),
        in_specs=[per_image(length, width)] * 2 + [whole(norm_params), whole(dense), whole(router_wide)],
        out_specs=[per_image(*s) for s, _ in shapes],
        out_shape=[jax.ShapeDtypeStruct((images,) + s, t) for s, t in shapes],
        scratch_shapes=[pltpu.VMEM((TOGETHER * PAD, width), wide)],
        compiler_params=kernel_params(56),
        cost_estimate=cost(images * 2.5e9, images * 5e6),
        name="attend",
    )(block_input, cotangent, norm_params, dense, router_wide)


def dispatch_kernel(waits, slot_ref, second_ref, upstream_ref, route_ref, *refs):
    x_ref, g_ref, xt_ref, gt_ref = refs[waits:]
    low = jnp.bfloat16
    expert = pl.program_id(0)
    slots, tokens = x_ref.shape[1], second_ref.shape[0]
    rows_of = lax.broadcasted_iota(jnp.int32, (8, tokens), 0)
    slot_row = jnp.max(jnp.where(rows_of == expert, slot_ref[...], -1), axis=0, keepdims=True)
    hot = lax.broadcasted_iota(jnp.int32, (slots, tokens), 0) == slot_row
    hot = jnp.where(hot, 1.0, 0.0).astype(low)
    lanes = lax.broadcasted_iota(jnp.int32, (tokens, 128), 1)
    gate = jnp.sum(jnp.where(lanes == expert, route_ref[...], 0.0), axis=1, keepdims=True)
    pair_grad = (gate * upstream_ref[...].astype(jnp.float32)).astype(low)
    rows = mm(hot, second_ref[...]).astype(low)
    x_ref[0] = rows
    xt_ref[0] = rows.T
    rows = mm(hot, pair_grad).astype(low)
    g_ref[0] = rows
    gt_ref[0] = rows.T


def dispatch(slot_row, second, upstream, route_probs, experts, slots, waits=()):
    tokens, width = second.shape

    def whole(array):
        return pl.BlockSpec(array.shape, lambda e: (0,) * array.ndim)

    flat = pl.BlockSpec((1, slots, width), lambda e: (e, 0, 0))
    turned = pl.BlockSpec((1, width, slots), lambda e: (e, 0, 0))
    low = jnp.bfloat16
    return pl.pallas_call(
        partial(dispatch_kernel, len(waits)),
        grid=(experts,),
        in_specs=[whole(a) for a in (slot_row, second, upstream, route_probs)]
        + [pl.BlockSpec(memory_space=pl.ANY)] * len(waits),
        out_specs=[flat, flat, turned, turned],
        out_shape=[jax.ShapeDtypeStruct((experts, slots, width), low)] * 2
        + [jax.ShapeDtypeStruct((experts, width, slots), low)] * 2,
        compiler_params=kernel_params(60),
        cost_estimate=cost(4 * slots * tokens * width * experts, 1e7),
        name="dispatch",
    )(slot_row, second, upstream, route_probs, *waits)


def expert_kernel(first, last, split, count, x_ref, g_ref, xt_ref, gt_ref, *refs):
    low = jnp.bfloat16
    if not first:
        made_in, back_in = refs[:2]
        refs = refs[2:]
    sources, refs = refs[:count], refs[count:]
    _, _, rows, columns = sources[0].shape
    made_ref, back_ref, *targets, held, sent, in_sems, out_sems = refs
    expert, experts = pl.program_id(0), pl.num_programs(0)
    shards, heads, tensors = (lax.axis_size(a) for a in (SHARD, HEAD, TENSOR))
    middle = shards // 2

    def window(ref, slot, group, start=0, width=None):
        tensor, head = absolute(group)
        down = pl.multiple_of(head * rows, rows)
        over = pl.multiple_of(tensor * columns + start, 128)
        return ref.at[slot, :, pl.ds(down, rows), pl.ds(over, columns if width is None else width)]

    def fetch(source, slot, group):
        return pltpu.make_async_copy(source, window(held, slot, group), in_sems.at[slot, group])

    def start_fetch(which, slot, group):
        if count == 1:
            tensor, head = absolute(group)
            fetch(sources[0].at[(which * heads + head) * tensors + tensor], slot, group).start()
            return
        z = which ^ lax.axis_index(SHARD)
        place = group % 4 + (group // 4) * 5
        if group % 4 < 3:
            fetch(sources[place].at[z], slot, group).start()
            return

        @pl.when(z < middle)
        def _():
            fetch(sources[place].at[z], slot, group).start()

        @pl.when(z >= middle)
        def _():
            fetch(sources[place + 1].at[z - middle], slot, group).start()

    def puts(which, slot, group):
        z = which ^ lax.axis_index(SHARD)
        tensor, head = absolute(group)
        copies = []
        if split > 0:
            source, target = window(sent, slot, group, 0, split), targets[0].at[(head * tensors + tensor) * shards + z]
            copies.append(pltpu.make_async_copy(source, target, out_sems.at[slot, group, 0]))
        if split < columns:
            source = window(sent, slot, group, split, columns - split)
            target = targets[-2 + group // (GROUPS // 2)].at[group % (GROUPS // 2) * shards + z]
            copies.append(pltpu.make_async_copy(source, target, out_sems.at[slot, group, 1]))
        return copies

    slot = lax.rem(expert, 2)

    @pl.when(expert == 0)
    def _():
        for group in range(GROUPS):
            start_fetch(0, 0, group)

    @pl.when(expert + 1 < experts)
    def _():
        for group in range(GROUPS):
            start_fetch(expert + 1, 1 - slot, group)

    for group in range(GROUPS):
        fetch(sources[0].at[0], slot, group).wait()

    @pl.when(expert >= 2)
    def _():
        for group in range(GROUPS):
            for copy in puts(expert - 2, slot, group):
                copy.wait()

    x, g, xt, gt = x_ref[0], g_ref[0], xt_ref[0], gt_ref[0]
    w_in, w_out = held[slot, 0], held[slot, 1]
    v = mm(x, w_in)
    grad = mm(g, w_out)
    square = v * v
    tanh = jnp.tanh(v * (0.7978845608028654 + 0.035677408136300125 * square))
    half = 0.5 + 0.5 * tanh
    active = (v * half).astype(low)
    slope = half + v * (half * (1.0 - tanh)) * (0.7978845608028654 + 0.10703222440890037 * square)
    pre_grad = (grad * slope).astype(low)
    made = mm_turned(active, w_out)
    back = mm_turned(pre_grad, w_in)
    if not first:
        made, back = made_in[0] + made, back_in[0] + back
    made_ref[0], back_ref[0] = made.astype(made_ref.dtype), back.astype(back_ref.dtype)
    sent[slot, 0] = mm(xt, pre_grad).astype(low)
    sent[slot, 1] = mm(gt, active).astype(low)
    for group in range(GROUPS):
        for copy in puts(expert, slot, group):
            copy.start()

    @pl.when(expert == experts - 1)
    def _():
        for group in range(GROUPS):
            for copy in puts(expert - 1, 1 - slot, group):
                copy.wait()
        for group in range(GROUPS):
            for copy in puts(expert, slot, group):
                copy.wait()


def run_experts(x, g, xt, gt, sums, sources, last, split):
    experts, slots, width = x.shape
    _, kinds, rows, columns = sources[0].shape
    shards = lax.axis_size(SHARD)
    units = GROUPS * rows * columns // width
    low = jnp.bfloat16
    flat = pl.BlockSpec((1, slots, width), lambda e: (e, 0, 0))
    turned = pl.BlockSpec((1, width, slots), lambda e: (e, 0, 0))
    anywhere = pl.BlockSpec(memory_space=pl.ANY)
    kept = low if last else jnp.float32
    first = sums is None
    given = () if first else tuple(sums)
    pieces = []
    if split > 0:
        pieces += [(GROUPS * shards, kinds, rows, split)]
    if split < columns:
        pieces += [(GROUPS // 2 * shards, kinds, rows, columns - split)] * 2
    return pl.pallas_call(
        partial(expert_kernel, first, last, split, len(sources)),
        grid=(experts,),
        in_specs=[flat, flat, turned, turned] + [flat] * len(given) + [anywhere] * len(sources),
        out_specs=[flat, flat] + [anywhere] * len(pieces),
        out_shape=[jax.ShapeDtypeStruct((experts, slots, width), kept)] * 2
        + [jax.ShapeDtypeStruct(piece, low) for piece in pieces],
        scratch_shapes=[
            pltpu.VMEM((2, kinds, width, units), low),
            pltpu.VMEM((2, kinds, width, units), low),
            pltpu.SemaphoreType.DMA((2, GROUPS)),
            pltpu.SemaphoreType.DMA((2, GROUPS, 2)),
        ],
        compiler_params=kernel_params(60),
        cost_estimate=cost(12 * experts * slots * width * units, 3e7),
        name="experts",
    )(x, g, xt, gt, *given, *sources)


def combine_kernel(
    first, experts, slot_ref, made_ref, back_ref, hidden_ref, upstream_ref, second_ref, route_ref,
    norm_ref, router_ref, *refs
):
    output_ref, grad_ref, small_ref = refs if first else refs[3:]
    low = jnp.bfloat16
    image = pl.program_id(0)
    count, _, width = hidden_ref.shape
    tokens = count * PAD
    hidden = hidden_ref[...].reshape(tokens, width)
    upstream = upstream_ref[...].reshape(tokens, width).astype(jnp.float32)
    route_probs = route_ref[...].reshape(tokens, 128)
    slot_of = slot_ref[...].reshape(tokens, 128)
    slots = made_ref.shape[1]
    lanes = lax.broadcasted_iota(jnp.int32, (tokens, slots), 1)
    wide_lanes = lax.broadcasted_iota(jnp.int32, (tokens, 128), 1)
    total = hidden
    second_grad = jnp.zeros_like(hidden)
    prob_sum = jnp.zeros((tokens, 128), jnp.float32)
    gates = route_probs
    for e in range(experts):
        hot = jnp.where(lanes == slot_of[:, e : e + 1], 1.0, 0.0).astype(low)
        made = mm(hot, made_ref[e])
        second_grad = second_grad + mm(hot, back_ref[e])
        total = total + route_probs[:, e : e + 1] * made
        gate_grad = jnp.sum(upstream * made, axis=-1, keepdims=True)
        prob_sum = jnp.where(wide_lanes == e, gate_grad, prob_sum)
        gates = jnp.where(wide_lanes == experts + e, route_probs[:, e : e + 1], gates)
        prob_sum = jnp.where(wide_lanes == experts + e, gate_grad, prob_sum)
    length = output_ref.shape[1]
    for i in range(count):
        output_ref[i] = total[i * PAD : (i + 1) * PAD].astype(low)[:length]
    inner = jnp.sum(route_probs * prob_sum, axis=-1, keepdims=True)
    logit_grad = (gates * (prob_sum - inner)).astype(low)
    second_grad = second_grad + mm_turned(logit_grad, router_ref[...])
    unit, inverse = unit_of(hidden)
    grad = upstream + unit_backward(second_grad, unit, inverse, norm_ref[2:3])
    grad_ref[...] = grad.reshape(grad_ref.shape)
    router_grad = mm_rows(logit_grad, second_ref[...].reshape(tokens, width))[:8]
    gain = jnp.sum(second_grad * unit, axis=0, keepdims=True)
    bias = jnp.sum(second_grad, axis=0, keepdims=True)
    rows_of = lax.broadcasted_iota(jnp.int32, (8, hidden.shape[1]), 0)
    small = jnp.where(
        rows_of == 2, gain, jnp.where(rows_of == 3, bias, jnp.where(rows_of >= experts, router_grad, 0.0))
    )

    @pl.when(image == 0)
    def _():
        small_ref[...] = small if first else small + refs[0][...]

    @pl.when(image > 0)
    def _():
        small_ref[...] += small


def combine(which, count, length, experts, slot_column, made, back, hidden, upstream, second, route_probs, norm_params, router_wide, before):
    images, _, width = hidden.shape
    low, wide = jnp.bfloat16, jnp.float32
    first = before is None
    given = () if first else tuple(before)

    def per_image(*shape):
        return pl.BlockSpec((TOGETHER,) + shape, lambda i: (i + which // TOGETHER,) + (0,) * len(shape))

    def whole(array):
        return pl.BlockSpec(array.shape, lambda i: (0,) * array.ndim)

    small = pl.BlockSpec((8, width), lambda i: (0, 0))
    return pl.pallas_call(
        partial(combine_kernel, first, experts),
        grid=(count // TOGETHER,),
        in_specs=[
            per_image(PAD, 128), whole(made), whole(back), per_image(PAD, width), per_image(PAD, width),
            per_image(PAD, width), per_image(PAD, 128), whole(norm_params), whole(router_wide),
        ]
        + ([] if first else [small] + [pl.BlockSpec(memory_space=pl.ANY)] * 2),
        input_output_aliases={} if first else {10: 0, 11: 1},
        out_specs=[per_image(length, width), per_image(PAD, width), small],
        out_shape=[
            jax.ShapeDtypeStruct((images, length, width), low),
            jax.ShapeDtypeStruct((images, PAD, width), wide),
            jax.ShapeDtypeStruct((8, width), wide),
        ],
        compiler_params=kernel_params(60),
        cost_estimate=cost(4 * count * PAD * experts * made.shape[1] * width, 2e7),
        name="combine",
    )(slot_column, made, back, hidden, upstream, second, route_probs, norm_params, router_wide, *given)


def regroup(rows):
    return jnp.concatenate([rows[:, k : k + 128] for k in range(0, rows.shape[1], 128)], axis=0)


def two_terms(value):
    high = value.astype(jnp.bfloat16).astype(jnp.float32)
    less = (value - high).astype(jnp.bfloat16).astype(jnp.float32)
    return jnp.concatenate([high, less], axis=0).astype(jnp.bfloat16), high + less


def term_sum(terms):
    terms = terms.astype(jnp.float32)
    half = terms.shape[0] // 2
    return terms[:half] + terms[half:]


def attend_back_kernel(
    first, last, input_ref, norm_ref, dense_ref, normed_ref, projected_ref, probs_ref,
    context_ref, grad_ref, norm_grad_in, *refs
):
    low = jnp.bfloat16
    image, images = pl.program_id(0), pl.num_programs(0)
    if not first:
        sums_in = refs[0]
        refs = refs[2:]
    input_grad_ref, norm_grad_ref = refs[:2]
    if last:
        keep_ref, give_ref, sums, low_sums, packed, sems = refs[2:]
    else:
        sums = refs[2]

    @pl.when(image == 0)
    def _():
        sums[...] = jnp.zeros_like(sums) if first else sums_in[...]
        norm_grad_ref[...] = norm_grad_in[...]

    count, _, width = grad_ref.shape
    tokens = count * PAD
    hidden_grad = grad_ref[...].reshape(tokens, width)
    attended_low = hidden_grad.astype(low)
    context_grad = mm(attended_low, dense_ref[3]).astype(low)
    sums[3] += mm_rows(attended_low, context_ref[...].reshape(tokens, width))
    first_half = lax.broadcasted_iota(jnp.int32, (PAD, 2 * HEAD_DIM), 1) < HEAD_DIM
    zero = jnp.zeros((PAD, 2 * HEAD_DIM), low)
    scale = HEAD_DIM ** (-0.5)
    whole = [[], [], []]
    for i in range(count):
        parts = [[], [], []]
        for pair in range(width // (2 * HEAD_DIM)):
            at = slice(pair * 2 * HEAD_DIM, (pair + 1) * 2 * HEAD_DIM)
            query, key, value = (projected_ref[i, c, :, at] for c in range(3))
            grad = context_grad[i * PAD : (i + 1) * PAD, at]
            halves = []
            for side in range(2):
                mine = jnp.where(first_half == (side == 0), grad, zero)
                probs = probs_ref[i, 2 * pair + side]
                wide = probs.astype(jnp.float32)
                prob_grad = mm_turned(value, mine)
                weighted = wide * prob_grad
                score_grad = (
                    weighted - wide * jnp.sum(weighted, axis=0, keepdims=True)
                ).astype(low)
                query_grad = mm_rows(key, score_grad)[side * HEAD_DIM : (side + 1) * HEAD_DIM]
                halves.append((query_grad, mm(score_grad, query), mm(probs, grad)))
            parts[0].append((jnp.concatenate([halves[0][0], halves[1][0]], axis=0) * scale).T.astype(low))
            parts[1].append((jnp.where(first_half, halves[0][1], halves[1][1]) * scale).astype(low))
            parts[2].append(jnp.where(first_half, halves[0][2], halves[1][2]).astype(low))
        for kind in range(3):
            whole[kind].append(jnp.concatenate(parts[kind], axis=1))
    normed = normed_ref[...].reshape(tokens, width)
    normed_grad = None
    for kind in range(3):
        projected_grad = jnp.concatenate(whole[kind], axis=0)
        sums[kind] += mm_rows(normed, projected_grad)
        part = mm_turned(projected_grad, dense_ref[kind])
        normed_grad = part if normed_grad is None else normed_grad + part
    length = input_grad_ref.shape[1]
    gain, bias = 0.0, 0.0
    for i in range(count):
        unit, inverse = unit_of(input_ref[i].astype(jnp.float32))
        part = normed_grad[i * PAD : (i + 1) * PAD][:length]
        input_grad_ref[i] = hidden_grad[i * PAD : (i + 1) * PAD][:length] + unit_backward(
            part, unit, inverse, norm_ref[0:1]
        )
        gain = gain + jnp.sum(part * unit, axis=0, keepdims=True)
        bias = bias + jnp.sum(part, axis=0, keepdims=True)
    rows_of = lax.broadcasted_iota(jnp.int32, (8, width), 0)
    norm_grad_ref[...] += jnp.where(rows_of == 0, gain, jnp.where(rows_of == 1, bias, 0.0))

    if not last:
        return

    @pl.when(image == images - 1)
    def _():
        kinds, rows, columns = sums.shape[0], *keep_ref.shape[1:]
        near = keep_ref.shape[0] // kinds
        shards = near * 2 // GROUPS
        low_sums[...] = sums[...].astype(low)
        packed[...] = two_terms(regroup(norm_grad_ref[...]))[0]
        copies = [pltpu.make_async_copy(packed, give_ref.at[kinds * near], sems.at[2 * near])]
        for piece in range(2 * near):
            target = keep_ref if piece < near else give_ref
            copies.append(
                pltpu.make_async_copy(
                    dense_window(low_sums, piece, shards, rows, columns),
                    target.at[pl.ds(piece % near * kinds, kinds)],
                    sems.at[piece],
                )
            )
        for copy in copies:
            copy.start()
        for copy in copies:
            copy.wait()


def attend_back(which, count, block_input, norm_params, dense, kept, hidden_grad, norm_grad, carried, near_shape):
    images, length, width = block_input.shape
    heads = width // HEAD_DIM
    low, wide = jnp.bfloat16, jnp.float32
    first, last = carried is None, which + count == images
    near, kinds, rows, columns = near_shape

    def per_image(*shape):
        return pl.BlockSpec((1,) + shape, lambda i: (i + which,) + (0,) * len(shape))

    def whole(array):
        return pl.BlockSpec(array.shape, lambda i: (0,) * array.ndim)

    anywhere = pl.BlockSpec(memory_space=pl.ANY)
    small = pl.BlockSpec((8, width), lambda i: (0, 0))
    sum_shape = (4, width, width)
    given = () if first else tuple(carried)
    out_specs = [per_image(length, width), small]
    out_shape = [
        jax.ShapeDtypeStruct((images, length, width), wide),
        jax.ShapeDtypeStruct((8, width), wide),
    ]
    scratch = []
    if last:
        out_specs += [anywhere] * 2
        out_shape += [jax.ShapeDtypeStruct((near * kinds + k, rows, columns), low) for k in (0, 1)]
        scratch = [
            pltpu.VMEM(sum_shape, wide),
            pltpu.VMEM(sum_shape, low),
            pltpu.VMEM((rows, columns), low),
            pltpu.SemaphoreType.DMA((2 * near + 1,)),
        ]
    else:
        out_specs += [pl.BlockSpec(sum_shape, lambda i: (0, 0, 0))]
        out_shape += [jax.ShapeDtypeStruct(sum_shape, wide)]
    given_specs = [] if first else [whole(carried[0]), anywhere]
    return pl.pallas_call(
        partial(attend_back_kernel, first, last),
        grid=(count,),
        in_specs=[
            per_image(length, width), whole(norm_params), whole(dense),
            per_image(PAD, width), per_image(3, PAD, width), per_image(heads, PAD, PAD),
            per_image(PAD, width), per_image(PAD, width), small,
        ]
        + given_specs,
        out_specs=out_specs,
        out_shape=out_shape,
        scratch_shapes=scratch,
        input_output_aliases={} if first else {10: 0},
        compiler_params=kernel_params(60),
        cost_estimate=cost(count * 5e9, count * 6e6),
        name="attend_back",
    )(block_input, norm_params, dense, *kept, hidden_grad, norm_grad, *given)


def fold_core_kernel(quarter, keep_ref, come_ref, small_ref, x_ref, y_ref, both_ref, own_ref, own_small_ref):
    small = two_terms(regroup(small_ref[...]))[1] + term_sum(come_ref[4 * quarter])
    packed, own_small_ref[...] = two_terms(small)
    for k, target in enumerate((own_ref, x_ref, y_ref, both_ref)):
        at = slice(k * quarter, (k + 1) * quarter)
        total = keep_ref[at].astype(jnp.float32) + come_ref[at].astype(jnp.float32)
        target[:quarter] = total.astype(target.dtype)
        if k:
            target[quarter] = packed


def fold_core(keep, come, small):
    count, rows, columns = keep.shape
    quarter = count // 4
    message = jax.ShapeDtypeStruct((quarter + 1, rows, columns), jnp.bfloat16)
    return pl.pallas_call(
        partial(fold_core_kernel, quarter),
        out_shape=[message] * 3
        + [
            jax.ShapeDtypeStruct((quarter, rows, columns), jnp.float32),
            jax.ShapeDtypeStruct((rows // 2, columns), jnp.float32),
        ],
        compiler_params=kernel_params(24),
        cost_estimate=cost(1e6, 4e6),
        name="fold_core",
    )(keep, come, small)


def fold_sides_kernel(own_ref, small_ref, x_ref, y_ref, both_ref, *refs):
    messages, (total_ref, total_small_ref) = refs[:-2], refs[-2:]
    count = own_ref.shape[0]
    each = count // (len(messages) + 1)
    small = (small_ref[...] + term_sum(x_ref[count])) + (term_sum(y_ref[count]) + term_sum(both_ref[count]))
    packed, total_small_ref[...] = two_terms(small)
    for k, target in enumerate((total_ref, *messages)):
        at = slice(k * each, (k + 1) * each)
        total = own_ref[at] + sum(r[at].astype(jnp.float32) for r in (x_ref, y_ref, both_ref))
        target[:each] = total.astype(target.dtype)
        if k:
            target[each] = packed


def fold_sides(own, small, arrived, shards):
    count, rows, columns = own.shape
    each = count // shards
    message = jax.ShapeDtypeStruct((each + 1, rows, columns), jnp.bfloat16)
    return pl.pallas_call(
        fold_sides_kernel,
        out_shape=[message] * (shards - 1)
        + [jax.ShapeDtypeStruct((each, rows, columns), jnp.float32), jax.ShapeDtypeStruct(small.shape, jnp.float32)],
        compiler_params=kernel_params(24),
        cost_estimate=cost(1e6, 2e6),
        name="fold_sides",
    )(own, small, *arrived)


def dense_update_kernel(shards, own_ref, small_ref, *refs):
    arrived, refs = refs[: shards - 1], refs[shards - 1 :]
    kept, made = refs[:12], refs[12:]
    kinds = own_ref.shape[0]
    width = kept[0].shape[1]

    def update(group, at, gradient, rate, decay):
        old = [ref[at] for ref in kept[3 * group : 3 * group + 3]]
        new = adam_update(old[0], gradient, old[1], old[2], rate, decay)
        for ref, value in zip(made[3 * group : 3 * group + 3], new):
            ref[at] = value

    sums = [small_ref[...]] + [term_sum(r[kinds]) for r in arrived]
    while len(sums) > 1:
        sums = [a + b for a, b in zip(sums[::2], sums[1::2])]
    for k in range(width // 128):
        at = (slice(None), slice(k * 128, (k + 1) * 128))
        block = sums[0][k * 8 : (k + 1) * 8]
        update(0, at, block[:4], 0.25, 0.0)
        update(3, at, block[4:], 0.75 * width ** (-0.5), DECAY_RATE)
    for kind in range(kinds):
        gradient = own_ref[kind] + sum(r[kind].astype(jnp.float32) for r in arrived)
        if kind < kinds - 1:
            update(1, kind, gradient, 1.3 * width ** (-0.5), DECAY_RATE)
        else:
            update(2, (slice(None), slice(None)), gradient, 3.0 * width ** (-0.5), DECAY_RATE)


def dense_update(own, small, arrived, kept):
    return pl.pallas_call(
        partial(dense_update_kernel, len(arrived) + 1),
        out_shape=[jax.ShapeDtypeStruct(a.shape, a.dtype) for a in kept],
        compiler_params=kernel_params(24),
        cost_estimate=cost(1e6, 4e6),
        name="dense_update",
    )(own, small, *arrived, *kept)


def expert_update_kernel(first, experts, terms, *refs):
    parts, refs = refs[:terms], refs[terms:]
    kept, made = refs[:6], refs[6 if first else 12 :]
    width = 4 * kept[0].shape[1]
    rates = (1.0 * width ** (-0.5), 0.8 * experts * FF ** (-0.5))
    for kind in range(2):
        gradient = sum(r[kind].astype(jnp.float32) for r in parts)
        gradient = gradient if kind == 0 else gradient.T
        old = [ref[0] for ref in kept[3 * kind : 3 * kind + 3]]
        new = adam_update(old[0], gradient, old[1], old[2], rates[kind], DECAY_RATE)
        for ref, value in zip(made[3 * kind : 3 * kind + 3], new):
            ref[0] = value


def expert_update(parts, start, kept, before):
    _, rows, columns = parts[0].shape
    offset = start // 128
    anywhere = pl.BlockSpec(memory_space=pl.ANY)
    part = pl.BlockSpec((2, rows, 128), lambda j: (0, 0, j))
    into = pl.BlockSpec((1, rows, 128), lambda j: (0, 0, j + offset))
    out = pl.BlockSpec((1, 128, rows), lambda j: (0, j + offset, 0))
    specs = [into] * 3 + [out] * 3
    before = () if before is None else tuple(before)
    return pl.pallas_call(
        partial(expert_update_kernel, not before, lax.axis_size(SHARD), len(parts)),
        grid=(columns // 128,),
        in_specs=[part] * len(parts) + specs + [anywhere] * len(before),
        out_specs=specs,
        out_shape=[jax.ShapeDtypeStruct(a.shape, a.dtype) for a in kept],
        input_output_aliases={len(parts) + 6 + k: k for k in range(len(before))},
        compiler_params=kernel_params(24),
        cost_estimate=cost(1e6, 12 * 4 * rows * columns),
        name="expert_update",
    )(*parts, *kept, *before)


def join_sides_kernel(quarter, keep_x, keep_y, come_x, come_y, from_x, from_y, over_x, over_y):
    late = pl.program_id(0) >= quarter // 2
    x = keep_x[...].astype(jnp.float32) + come_x[...].astype(jnp.float32)
    y = keep_y[...].astype(jnp.float32) + come_y[...].astype(jnp.float32)
    over_x[...] = (x + jnp.where(late, from_y[...].astype(jnp.float32), 0.0)).astype(over_x.dtype)
    over_y[...] = (y + jnp.where(late, 0.0, from_x[...].astype(jnp.float32))).astype(over_y.dtype)


def join_sides(keep, come, from_x, from_y):
    count, *rest = keep.shape
    quarter = count // 4
    half = quarter // 2
    block = (1, *rest)

    def group(k):
        return pl.BlockSpec(block, lambda j: (k * quarter + j, 0, 0, 0))

    first = pl.BlockSpec(block, lambda j: (jnp.minimum(j, half - 1), 0, 0, 0))
    second = pl.BlockSpec(block, lambda j: (jnp.maximum(j - half, 0), 0, 0, 0))
    return pl.pallas_call(
        partial(join_sides_kernel, quarter),
        grid=(quarter,),
        in_specs=[group(1), group(2), group(1), group(2), first, second],
        out_specs=[pl.BlockSpec(block, lambda j: (j, 0, 0, 0))] * 2,
        out_shape=[jax.ShapeDtypeStruct((quarter, *rest), keep.dtype)] * 2,
        compiler_params=kernel_params(60),
        cost_estimate=cost(1e6, 8e6),
        name="join_sides",
    )(keep, keep, come, come, from_x, from_y)


def relay(block, axis, mask):
    size = lax.axis_size(axis)
    return lax.ppermute(block, axis, [(i, i ^ mask) for i in range(size)])


def relay_core(block):
    return relay(block, HEAD, 1)


def relay_x(block):
    return relay(block, HEAD, 2)


def relay_y(block):
    return relay(block, TENSOR, 1)


def relay_both(block):
    heads, tensors = lax.axis_size(HEAD), lax.axis_size(TENSOR)
    pairs = [
        (h * tensors + t, (h ^ 2) * tensors + (t ^ 1)) for h in range(heads) for t in range(tensors)
    ]
    return lax.ppermute(block, (HEAD, TENSOR), pairs)


def relay_line(blocks):
    return [relay(block, SHARD, k + 1) for k, block in enumerate(blocks)]


def ordered(values, *others):
    return lax.optimization_barrier((values, others))[0]


def wide_sum(*parts):
    return sum(p.astype(jnp.float32) for p in parts)


def local_plan(
    block_input,
    cotangent,
    routes,
    priority,
    norm_params,
    norm_moment,
    norm_square,
    qkv_weight,
    qkv_moment,
    qkv_square,
    attn_weight,
    attn_moment,
    attn_square,
    router_weight,
    router_moment,
    router_square,
    expert_in,
    in_moment,
    in_square,
    expert_out,
    out_moment,
    out_square,
):
    images, length, model_width = block_input.shape
    shards = experts = lax.axis_size(SHARD)
    capacity = 9 * images * length // (4 * experts)
    slots = -(-capacity // SLOT_PAD) * SLOT_PAD
    low = jnp.bfloat16

    dense_low = jnp.concatenate(
        [qkv_weight.transpose(1, 0, 2), attn_weight.T[None]], axis=0
    ).astype(low)
    dense_column = jnp.stack([dense_low] + relay_line([dense_low] * (shards - 1)))
    expert_low = jnp.stack([expert_in[0], expert_out[0].T]).astype(low)
    edges = [expert_low.shape[2] * edge // CUTS[-1] for edge in CUTS]
    chunks = [expert_low[:, :, i:j] for i, j in zip(edges, edges[1:])]
    tables = slot_tables(routes, priority)
    router_wide = jnp.pad(router_weight, ((0, 0), (0, 128 - experts))).astype(low)

    def line_of(block):
        return jnp.stack([block] + relay_line([block] * (shards - 1)))

    def across(column):
        return (relay_x(column), relay_y(column), relay_both(column))

    dense_column, tables, chunks[0] = ordered((dense_column, tables, chunks[0]))
    dense_sides, dense_far = across(dense_column), (relay_core(dense_column),)
    column = line_of(chunks[0])
    later = lax.all_gather(chunks[1], (SHARD, HEAD, TENSOR))
    slot_row, slot_column = find_slots(tables, experts, capacity)
    slot_column = slot_column.reshape(images, PAD, 128)
    dense_sides, dense_far, slot_row = ordered((dense_sides, dense_far, slot_row))
    dense_far += tuple(relay_core(s) for s in dense_sides)
    dense = join_dense((dense_column, *dense_sides, *dense_far), model_width)

    half = shards // 2
    column, dense = ordered((column, dense))
    over_x, over_y, far_column = relay_x(column), relay_y(column), relay_core(column)
    normed, projected, probs, context, hidden, second, route_probs, upstream = attend(
        experts, block_input, cotangent, norm_params, dense, router_wide
    )

    over_x, over_y, far_column, second = ordered((over_x, over_y, far_column, second))
    corners = (relay_y(over_x[:half]), relay_x(over_y[half:]))
    near, far = (column, over_x, over_y), (far_column, relay_core(over_x), relay_core(over_y))
    tokens = images * PAD
    slot_rows = dispatch(
        slot_row, second.reshape(tokens, model_width), upstream.reshape(tokens, model_width),
        route_probs.reshape(tokens, 128), experts, slots,
    )

    corners, far, slot_rows = ordered((corners, far, slot_rows))
    weights_a = (*near, *corners, *far, *(relay_core(c) for c in corners))
    quarter = shards

    class Returning:
        def __init__(self, keep, give):
            self.keep, self.come = keep, relay_core(give)

        def some(self, first, count):
            at = slice(first, first + count)
            return wide_sum(self.keep[at], self.come[at])

        def part(self, k):
            return self.some(k * quarter, quarter)

        def corner(self):
            half = quarter // 2
            self.corners = (
                relay_x(self.some(3 * quarter, half).astype(low)),
                relay_y(self.some(3 * quarter + half, quarter - half).astype(low)),
            )

        def sides(self):
            self.joined = join_sides(self.keep, self.come, *self.corners)
            self.over = (relay_x(self.joined[0]), relay_y(self.joined[1]))

        def line(self):
            total = self.part(0) + wide_sum(*self.over)
            self.own = total[0]
            self.others = relay_line([total[k].astype(low) for k in range(1, quarter)])

        def result(self):
            return self.own + wide_sum(*self.others)

    made, backed, grads = run_experts(*slot_rows, None, weights_a, False, edges[1])

    made, grads, later = ordered((made, grads, later))
    own_a = lax.psum_scatter(grads, (HEAD, TENSOR), scatter_dimension=0, tiled=True)
    made, backed, keep, give = run_experts(*slot_rows, (made, backed), (later,), True, 0)

    made, keep, give = ordered((made, keep, give))
    sum_b = Returning(keep, give)
    rest = (slot_column, made, backed, hidden, upstream, second, route_probs, norm_params, router_wide)
    early = images - TOGETHER
    block_output, hidden_grad, norm_grad = combine(0, early, length, experts, *rest, None)

    sum_b.keep, sum_b.come, norm_grad = ordered((sum_b.keep, sum_b.come, norm_grad))
    sum_b.corner()
    block_output, hidden_grad, norm_grad = combine(
        early, TOGETHER, length, experts, *rest, (norm_grad, block_output, hidden_grad)
    )
    kept = (normed, projected, probs, context)
    half = images // 3
    dense_shape = (4 * quarter, *dense_low.shape)
    input_grad, norm_grad, dense_sums = attend_back(
        0, half, block_input, norm_params, dense, kept, hidden_grad, norm_grad, None, (4 * quarter, *dense_low.shape)
    )

    sum_b.corners, own_a, norm_grad, dense_sums = ordered((sum_b.corners, own_a, norm_grad, dense_sums))
    sum_b.sides()
    own_a = ordered(own_a, sum_b.joined)
    others_a = relay_line([own_a[k] for k in range(1, quarter)])
    input_grad, norm_grad, keep, give = attend_back(
        half, images - half, block_input, norm_params, dense, kept, hidden_grad, norm_grad,
        (dense_sums, input_grad), (4 * quarter, *dense_low.shape),
    )

    sum_b.over, others_a, keep, give = ordered((sum_b.over, others_a, keep, give))
    come = relay_core(give)
    sum_b.line()
    come, sum_b.own = ordered((come, sum_b.own))
    *messages, own, own_small = fold_core(keep, come, norm_grad)
    arrived = [send(m) for m, send in zip(messages, (relay_x, relay_y, relay_both))]
    messages, own_a, others_a = ordered((messages, own_a, others_a))
    expert_kept = (expert_in, in_moment, in_square, expert_out, out_moment, out_square)
    updated = expert_update([own_a[0], *others_a], 0, expert_kept, None)
    arrived, updated = ordered((arrived, updated))
    *messages, own, own_small = fold_sides(own, own_small, arrived, shards)
    arrived = relay_line(messages)
    updated = expert_update([sum_b.own, *sum_b.others], edges[1], expert_kept, updated)
    arrived, updated = ordered((arrived, updated))
    turns = ((0, 1), (1, 0, 2), (1, 0), (1, 0))
    dense_kept = (
        (norm_params, norm_moment, norm_square),
        (qkv_weight, qkv_moment, qkv_square),
        (attn_weight, attn_moment, attn_square),
        (router_weight, router_moment, router_square),
    )
    flat = [a.transpose(t) for t, group in zip(turns, dense_kept) for a in group]
    dense_new = dense_update(own, own_small, arrived, flat)
    dense_new = [a.transpose(turns[k // 3]) for k, a in enumerate(dense_new)]
    return (block_output, input_grad, *dense_new, *updated)


def solution(mesh):
    fits = mesh.shape[SHARD] <= 4
    return jax.shard_map(
        local_plan if fits else slot_plan,
        mesh=mesh,
        in_specs=(
            P((SHARD, HEAD, TENSOR), None, None),
            P((SHARD, HEAD, TENSOR), None, None),
            P((SHARD, HEAD, TENSOR), None, None),
            P((SHARD, HEAD, TENSOR), None),
            P(),
            P(),
            P(),
            P((SHARD, TENSOR), None, HEAD),
            P((SHARD, TENSOR), None, HEAD),
            P((SHARD, TENSOR), None, HEAD),
            P(HEAD, (SHARD, TENSOR)),
            P(HEAD, (SHARD, TENSOR)),
            P(HEAD, (SHARD, TENSOR)),
            P(),
            P(),
            P(),
            P(SHARD, HEAD, TENSOR),
            P(SHARD, HEAD, TENSOR),
            P(SHARD, HEAD, TENSOR),
            P(SHARD, TENSOR, HEAD),
            P(SHARD, TENSOR, HEAD),
            P(SHARD, TENSOR, HEAD),
        ),
        out_specs=(
            P((SHARD, HEAD, TENSOR), None, None),
            P((SHARD, HEAD, TENSOR), None, None),
            P(),
            P(),
            P(),
            P((SHARD, TENSOR), None, HEAD),
            P((SHARD, TENSOR), None, HEAD),
            P((SHARD, TENSOR), None, HEAD),
            P(HEAD, (SHARD, TENSOR)),
            P(HEAD, (SHARD, TENSOR)),
            P(HEAD, (SHARD, TENSOR)),
            P(),
            P(),
            P(),
            P(SHARD, HEAD, TENSOR),
            P(SHARD, HEAD, TENSOR),
            P(SHARD, HEAD, TENSOR),
            P(SHARD, TENSOR, HEAD),
            P(SHARD, TENSOR, HEAD),
            P(SHARD, TENSOR, HEAD),
        ),
        check_vma=False,
    )
```

```python
import math
from functools import partial

import jax
import jax.numpy as jnp
from jax import lax
from jax.experimental import pallas as pl
from jax.experimental.pallas import tpu as pltpu
from jax.sharding import PartitionSpec as P

SHARD, HEAD, TENSOR = "shard", "head", "tensor"
HEAD_DIM = 64
FF = 2048
STEP = 10


EPS_NORM = 1e-06
BETA_ONE = 0.9
BETA_TWO = 0.999
ADAM_EPS = 1e-08
DECAY_RATE = 0.1


def norm_forward(values, gain_row, bias_row):
    center = jnp.mean(values, axis=-1, keepdims=True)
    shifted = values - center
    inverse = lax.rsqrt(jnp.mean(shifted * shifted, axis=-1, keepdims=True) + EPS_NORM)
    unit_rows = shifted * inverse
    return (unit_rows * gain_row + bias_row, unit_rows, inverse)


def norm_backward(grad_rows, unit_rows, inverse, gain_row):
    scaled = grad_rows * gain_row
    inner_grad = (
        scaled
        - jnp.mean(scaled, axis=-1, keepdims=True)
        - unit_rows * jnp.mean(scaled * unit_rows, axis=-1, keepdims=True)
    )
    return (
        inner_grad * inverse,
        jnp.sum(grad_rows * unit_rows, axis=0),
        jnp.sum(grad_rows, axis=0),
    )


def gelu_grad(pre_act, upstream):
    result, pullback = jax.vjp(partial(jax.nn.gelu, approximate=True), pre_act)
    return pullback(upstream)[0]


def adam_update(weight, gradient, moment, square, step_rate, decay_rate):
    moment_new = BETA_ONE * moment + (1.0 - BETA_ONE) * gradient
    square_new = BETA_TWO * square + (1.0 - BETA_TWO) * gradient * gradient
    first_hat = moment_new / (1.0 - BETA_ONE**STEP)
    second_hat = square_new / (1.0 - BETA_TWO**STEP)
    weight_new = weight - step_rate * (
        first_hat / (jnp.sqrt(second_hat) + ADAM_EPS) + decay_rate * weight
    )
    return (weight_new, moment_new, square_new)


def send_rows(parcel):
    copies = jnp.broadcast_to(
        parcel[:, None], (parcel.shape[0], lax.axis_size(TENSOR)) + parcel.shape[1:]
    )
    flat_copies = copies.reshape((-1,) + parcel.shape[1:])
    arrived = lax.all_to_all(
        flat_copies, (SHARD, TENSOR), split_axis=0, concat_axis=0, tiled=True
    )
    return arrived.reshape(copies.shape)


def return_rows(partial_rows):
    flat_rows = partial_rows.reshape((-1,) + partial_rows.shape[2:])
    arrived = lax.all_to_all(
        flat_rows.astype(jnp.bfloat16), (SHARD, TENSOR), split_axis=0, concat_axis=0, tiled=True
    ).astype(flat_rows.dtype)
    return jnp.sum(arrived.reshape(partial_rows.shape), axis=1)


def slot_plan(
    block_input,
    cotangent,
    routes,
    priority,
    norm_params,
    norm_moment,
    norm_square,
    qkv_weight,
    qkv_moment,
    qkv_square,
    attn_weight,
    attn_moment,
    attn_square,
    router_weight,
    router_moment,
    router_square,
    expert_in,
    in_moment,
    in_square,
    expert_out,
    out_moment,
    out_square,
):
    images, length, model_width = block_input.shape
    row_count = images * length
    local_experts = expert_in.shape[0]
    shards = lax.axis_size(SHARD)
    experts = local_experts * shards
    capacity = 9 * row_count // (4 * experts)
    score_scale = HEAD_DIM ** (-0.5)
    full_qkv, full_attn = (
        lax.all_gather(qkv_weight.astype(jnp.bfloat16), (SHARD, TENSOR), axis=0, tiled=True),
        lax.all_gather(attn_weight.astype(jnp.bfloat16), (SHARD, TENSOR), axis=1, tiled=True),
    )
    inputs = block_input.astype(jnp.float32).reshape(row_count, model_width)
    normed, unit_one, inverse_one = norm_forward(inputs, norm_params[0], norm_params[1])
    normed_low = normed.astype(jnp.bfloat16).reshape(images, length, model_width)
    gathered, hidden_in, hidden_out = (
        lax.all_gather(normed_low, HEAD, axis=0, tiled=True),
        lax.all_gather(expert_in.astype(jnp.bfloat16), HEAD, axis=1, tiled=True),
        lax.all_gather(expert_out.astype(jnp.bfloat16), HEAD, axis=2, tiled=True),
    )
    local_heads = full_qkv.shape[2] // HEAD_DIM
    all_images = gathered.shape[0]
    head_shape = (all_images, length, local_heads, HEAD_DIM)
    projected = jnp.einsum(
        "isd,dcn->iscn", gathered, full_qkv, preferred_element_type=jnp.float32
    ).astype(jnp.bfloat16)
    queries = projected[:, :, 0].reshape(head_shape)
    key_rows = projected[:, :, 1].reshape(head_shape)
    value_rows = projected[:, :, 2].reshape(head_shape)
    scores = (
        jnp.einsum("iqhe,ikhe->ihqk", queries, key_rows, preferred_element_type=jnp.float32)
        * score_scale
    )
    score_top = jnp.max(scores, axis=-1, keepdims=True)
    log_total = score_top + jnp.log(jnp.sum(jnp.exp(scores - score_top), axis=-1, keepdims=True))
    probs_low = jnp.exp(scores - log_total).astype(jnp.bfloat16)
    context = jnp.einsum(
        "ihqk,ikhe->iqhe", probs_low, value_rows, preferred_element_type=jnp.float32
    ).astype(jnp.bfloat16)
    context = context.reshape(all_images * length, local_heads * HEAD_DIM)
    attended = lax.psum_scatter(
        jnp.dot(context, full_attn, preferred_element_type=jnp.float32).astype(jnp.bfloat16),
        HEAD,
        scatter_dimension=0,
        tiled=True,
    ).astype(jnp.float32)
    hidden = inputs + attended
    normed_two, unit_two, inverse_two = norm_forward(hidden, norm_params[2], norm_params[3])
    second_low = normed_two.astype(jnp.bfloat16)
    router_low = router_weight.astype(jnp.bfloat16)
    logits = jnp.dot(second_low, router_low, preferred_element_type=jnp.float32)
    route_probs = jax.nn.softmax(logits, axis=-1)
    route_hot = (
        routes.reshape(row_count, 2)[:, :, None]
        == jnp.arange(experts, dtype=jnp.int32)[None, None, :]
    ).astype(jnp.float32)
    gate_values = jnp.sum(route_probs[:, None, :] * route_hot, axis=-1)
    expert_ids = routes.reshape(2 * row_count)
    rank_values = priority[0]
    pair_hot = route_hot.reshape(2 * row_count, experts)
    earlier = (rank_values[None, :] < rank_values[:, None]).astype(jnp.bfloat16)
    counts = jnp.dot(earlier, pair_hot.astype(jnp.bfloat16), preferred_element_type=jnp.float32)
    slot_index = jnp.sum(counts * pair_hot, axis=1).astype(jnp.int32)
    target = jnp.where(
        slot_index < capacity, expert_ids * capacity + slot_index, experts * capacity
    )
    filler = jnp.full((experts * capacity,), 2 * row_count, jnp.int32)
    owner_pair = filler.at[target].set(jnp.arange(2 * row_count, dtype=jnp.int32), mode="drop")
    padded = jnp.concatenate([second_low, jnp.zeros((1, model_width), jnp.bfloat16)], axis=0)
    parcel = padded[owner_pair // 2].reshape(shards, local_experts, capacity, model_width)
    arrived = send_rows(parcel)
    pre_act = jnp.einsum("stecd,edf->stecf", arrived, hidden_in, preferred_element_type=jnp.float32)
    active = jax.nn.gelu(pre_act, approximate=True).astype(jnp.bfloat16)
    part_rows = jnp.einsum(
        "stecf,efd->stecd", active, hidden_out, preferred_element_type=jnp.float32
    )
    expert_rows = return_rows(part_rows).reshape(experts * capacity, model_width)
    padded_out = jnp.concatenate([expert_rows, jnp.zeros((1, model_width), jnp.float32)], axis=0)
    per_pair = padded_out[target].reshape(row_count, 2, model_width)
    block_sum = hidden + jnp.sum(gate_values[:, :, None] * per_pair, axis=1)
    block_output = block_sum.astype(jnp.bfloat16).reshape(images, length, model_width)
    upstream = cotangent.astype(jnp.float32).reshape(row_count, model_width)
    pair_grad = (
        (gate_values[:, :, None] * upstream[:, None, :])
        .astype(jnp.bfloat16)
        .reshape(2 * row_count, model_width)
    )
    gate_grad = jnp.sum(upstream[:, None, :] * per_pair, axis=-1)
    padded_grad = jnp.concatenate([pair_grad, jnp.zeros((1, model_width), jnp.bfloat16)], axis=0)
    grad_parcel = padded_grad[owner_pair].reshape(shards, local_experts, capacity, model_width)
    grad_arrived = send_rows(grad_parcel)
    grad_out_part = jnp.einsum(
        "stecf,stecd->efd", active, grad_arrived, preferred_element_type=jnp.float32
    )
    active_grad = jnp.einsum(
        "stecd,efd->stecf", grad_arrived, hidden_out, preferred_element_type=jnp.float32
    )
    pre_grad = gelu_grad(pre_act, active_grad).astype(jnp.bfloat16)
    grad_in_part = jnp.einsum(
        "stecd,stecf->edf", arrived, pre_grad, preferred_element_type=jnp.float32
    )
    row_grad = jnp.einsum(
        "stecf,edf->stecd", pre_grad, hidden_in, preferred_element_type=jnp.float32
    )
    slot_grad = return_rows(row_grad).reshape(experts * capacity, model_width)
    padded_slot = jnp.concatenate([slot_grad, jnp.zeros((1, model_width), jnp.float32)], axis=0)
    second_grad = jnp.sum(padded_slot[target].reshape(row_count, 2, model_width), axis=1)
    prob_sum = jnp.sum(gate_grad[:, :, None] * route_hot, axis=1)
    logit_grad = (
        route_probs * (prob_sum - jnp.sum(route_probs * prob_sum, axis=-1, keepdims=True))
    ).astype(jnp.bfloat16)
    router_grad = jnp.einsum(
        "rd,re->de", second_low, logit_grad, preferred_element_type=jnp.float32
    )
    second_grad = second_grad + jnp.einsum(
        "re,de->rd", logit_grad, router_low, preferred_element_type=jnp.float32
    )
    hidden_part, gain_two, bias_two = norm_backward(
        second_grad, unit_two, inverse_two, norm_params[2]
    )
    hidden_grad = upstream + hidden_part
    attended_grad = lax.all_gather(hidden_grad.astype(jnp.bfloat16), HEAD, axis=0, tiled=True)
    attn_grad = jnp.einsum("rn,rd->nd", context, attended_grad, preferred_element_type=jnp.float32)
    context_grad = jnp.einsum(
        "rd,nd->rn", attended_grad, full_attn, preferred_element_type=jnp.float32
    ).astype(jnp.bfloat16)
    context_grad = context_grad.reshape(head_shape)
    scores_again = (
        jnp.einsum("iqhe,ikhe->ihqk", queries, key_rows, preferred_element_type=jnp.float32)
        * score_scale
    )
    probs_full = jnp.exp(scores_again - log_total)
    prob_grad = jnp.einsum(
        "iqhe,ikhe->ihqk", context_grad, value_rows, preferred_element_type=jnp.float32
    )
    score_grad = (
        probs_full * (prob_grad - jnp.sum(probs_full * prob_grad, axis=-1, keepdims=True))
    ).astype(jnp.bfloat16)
    query_grad = (
        jnp.einsum("ihqk,ikhe->iqhe", score_grad, key_rows, preferred_element_type=jnp.float32)
        * score_scale
    )
    key_grad = (
        jnp.einsum("ihqk,iqhe->ikhe", score_grad, queries, preferred_element_type=jnp.float32)
        * score_scale
    )
    value_grad = jnp.einsum(
        "ihqk,iqhe->ikhe", probs_low, context_grad, preferred_element_type=jnp.float32
    )
    projected_grad = (
        jnp.stack([query_grad, key_grad, value_grad], axis=2)
        .reshape(all_images, length, 3, local_heads * HEAD_DIM)
        .astype(jnp.bfloat16)
    )
    qkv_grad = jnp.einsum(
        "isd,iscn->dcn", gathered, projected_grad, preferred_element_type=jnp.float32
    )
    normed_part = jnp.einsum(
        "iscn,dcn->isd", projected_grad, full_qkv, preferred_element_type=jnp.float32
    )
    normed_grad, in_grad, out_grad = (
        lax.psum_scatter(
            normed_part.astype(jnp.bfloat16), HEAD, scatter_dimension=0, tiled=True
        ).astype(jnp.float32),
        lax.psum_scatter(
            grad_in_part.astype(jnp.bfloat16), HEAD, scatter_dimension=1, tiled=True
        ).astype(jnp.float32),
        lax.psum_scatter(
            grad_out_part.astype(jnp.bfloat16), HEAD, scatter_dimension=2, tiled=True
        ).astype(jnp.float32),
    )
    input_part, gain_one, bias_one = norm_backward(
        normed_grad.reshape(row_count, model_width), unit_one, inverse_one, norm_params[0]
    )
    input_grad = (hidden_grad + input_part).reshape(images, length, model_width)
    norm_grad = jnp.stack([gain_one, bias_one, gain_two, bias_two])
    norm_grad, router_grad = lax.psum((norm_grad, router_grad), (SHARD, HEAD, TENSOR))
    qkv_grad, attn_grad = (
        lax.psum_scatter(qkv_grad, (SHARD, TENSOR), scatter_dimension=0, tiled=True),
        lax.psum_scatter(attn_grad, (SHARD, TENSOR), scatter_dimension=1, tiled=True),
    )
    norm_new = adam_update(norm_params, norm_grad, norm_moment, norm_square, 0.25, 0.0)
    qkv_new = adam_update(
        qkv_weight, qkv_grad, qkv_moment, qkv_square, 1.3 * model_width ** (-0.5), DECAY_RATE
    )
    attn_new = adam_update(
        attn_weight, attn_grad, attn_moment, attn_square, 3.0 * model_width ** (-0.5), DECAY_RATE
    )
    router_new = adam_update(
        router_weight,
        router_grad,
        router_moment,
        router_square,
        0.75 * model_width ** (-0.5),
        DECAY_RATE,
    )
    in_new = adam_update(
        expert_in, in_grad, in_moment, in_square, 1.0 * model_width ** (-0.5), DECAY_RATE
    )
    out_new = adam_update(
        expert_out, out_grad, out_moment, out_square, 0.8 * experts * FF ** (-0.5), DECAY_RATE
    )
    return (
        block_output,
        input_grad,
        norm_new[0],
        norm_new[1],
        norm_new[2],
        qkv_new[0],
        qkv_new[1],
        qkv_new[2],
        attn_new[0],
        attn_new[1],
        attn_new[2],
        router_new[0],
        router_new[1],
        router_new[2],
        in_new[0],
        in_new[1],
        in_new[2],
        out_new[0],
        out_new[1],
        out_new[2],
    )


PAD = 208
SLOT_PAD = 16
CUTS = (0, 3, 8)
TOGETHER = 2


def kernel_params(megabytes):
    return pltpu.CompilerParams(vmem_limit_bytes=megabytes << 20)


def cost(flops, moved):
    return pl.CostEstimate(flops=int(flops), bytes_accessed=int(moved), transcendentals=0)


def mm(left, right):
    return lax.dot_general(left, right, (((1,), (0,)), ((), ())), preferred_element_type=jnp.float32)


def mm_turned(left, right):
    return lax.dot_general(left, right, (((1,), (1,)), ((), ())), preferred_element_type=jnp.float32)


def mm_rows(left, right):
    return lax.dot_general(left, right, (((0,), (0,)), ((), ())), preferred_element_type=jnp.float32)


def unit_of(values):
    center = jnp.mean(values, axis=-1, keepdims=True)
    shifted = values - center
    inverse = lax.rsqrt(jnp.mean(shifted * shifted, axis=-1, keepdims=True) + EPS_NORM)
    return (shifted * inverse, inverse)


def unit_backward(grad_rows, unit_rows, inverse, gain_row):
    scaled = grad_rows * gain_row
    inner_grad = (
        scaled
        - jnp.mean(scaled, axis=-1, keepdims=True)
        - unit_rows * jnp.mean(scaled * unit_rows, axis=-1, keepdims=True)
    )
    return inner_grad * inverse


def absolute(group):
    tensor = lax.axis_index(TENSOR) ^ (group // 2 % 2)
    head = lax.axis_index(HEAD) ^ (2 * (group % 2) + group // 4)
    return tensor, head


GROUPS = 8


def slot_kernel(experts, capacity, row_ref, column_ref, slot_row_ref, slot_column_ref):
    none = 1 << 20
    tokens = row_ref.shape[1]
    lanes = lax.broadcasted_iota(jnp.int32, (PAD, 128), 1)
    rows_of = lax.broadcasted_iota(jnp.int32, (8, tokens), 0)

    def ranks(named, rank, expert):
        return jnp.where(
            named[0] == expert, rank[0], jnp.where(named[1] == expert, rank[1], none)
        )

    routes_row, ranks_row = (row_ref[0:1], row_ref[1:2]), (row_ref[2:3], row_ref[3:4])
    all_rows = jnp.full((8, tokens), -1, jnp.int32)
    row_of = [ranks(routes_row, ranks_row, e) for e in range(experts)]
    totals = [jnp.zeros((1, tokens), jnp.float32) for e in range(experts)]
    for block in range(tokens // PAD):
        part = column_ref[block * PAD : (block + 1) * PAD]
        routes_col, ranks_col = (part[:, 0:1], part[:, 1:2]), (part[:, 2:3], part[:, 3:4])
        result = jnp.full((PAD, 128), -1, jnp.int32)
        for e in range(experts):
            column = ranks(routes_col, ranks_col, e)
            totals[e] = totals[e] + jnp.sum(
                jnp.where(column < row_of[e], 1.0, 0.0), axis=0, keepdims=True
            )
            before = jnp.sum(
                jnp.where(row_of[e] < column, 1.0, 0.0), axis=1, keepdims=True
            ).astype(jnp.int32)
            slot = jnp.where((column < none) & (before < capacity), before, -1)
            result = jnp.where(lanes == e, slot, result)
        slot_column_ref[block * PAD : (block + 1) * PAD] = result
    for e in range(experts):
        before = totals[e].astype(jnp.int32)
        slot = jnp.where((row_of[e] < none) & (before < capacity), before, -1)
        all_rows = jnp.where(rows_of == e, slot, all_rows)
    slot_row_ref[...] = all_rows


def slot_tables(routes, priority):
    images, length, _ = routes.shape
    tokens = images * PAD
    table = jnp.concatenate([routes, priority.reshape(images, length, 2)], axis=2)
    table = jnp.pad(table, ((0, 0), (0, PAD - length), (0, 0)), constant_values=-1)
    table = table.reshape(tokens, 4)
    columns = jnp.pad(table, ((0, 0), (0, 4)))
    return (columns.T, columns)


def find_slots(tables, experts, capacity):
    tokens = tables[1].shape[0]
    return pl.pallas_call(
        partial(slot_kernel, experts, capacity),
        out_shape=(
            jax.ShapeDtypeStruct((8, tokens), jnp.int32),
            jax.ShapeDtypeStruct((tokens, 128), jnp.int32),
        ),
        compiler_params=kernel_params(32),
        cost_estimate=cost(1e10, 1e6),
        name="find_slots",
    )(*tables)


def dense_window(ref, piece, shards, rows, columns):
    tensor, head = absolute(piece // shards)
    shard = lax.axis_index(SHARD) ^ (piece % shards)
    down = pl.multiple_of((shard * lax.axis_size(TENSOR) + tensor) * rows, rows)
    over = pl.multiple_of(head * columns, columns)
    return ref.at[:, pl.ds(down, rows), pl.ds(over, columns)]


def dense_kernel(*refs):
    groups, (full_ref, sems) = refs[:GROUPS], refs[GROUPS:]
    shards, kinds, rows, columns = groups[0].shape
    copies = []
    for piece in range(GROUPS * shards):
        copies.append(
            pltpu.make_async_copy(
                groups[piece // shards].at[piece % shards],
                dense_window(full_ref, piece, shards, rows, columns),
                sems.at[piece],
            )
        )
    for copy in copies:
        copy.start()
    for copy in copies:
        copy.wait()


def join_dense(groups, model_width):
    shards, kinds = groups[0].shape[:2]
    return pl.pallas_call(
        dense_kernel,
        out_shape=jax.ShapeDtypeStruct((kinds, model_width, model_width), groups[0].dtype),
        in_specs=[pl.BlockSpec(memory_space=pl.ANY)] * GROUPS,
        out_specs=pl.BlockSpec(memory_space=pltpu.VMEM),
        scratch_shapes=[pltpu.SemaphoreType.DMA((GROUPS * shards,))],
        compiler_params=kernel_params(16),
        cost_estimate=cost(1e6, 4e6),
        name="join_dense",
    )(*groups)


def attend_kernel(
    length, experts, input_ref, cotangent_ref, norm_ref, dense_ref, router_ref,
    normed_ref, projected_ref, probs_ref, context_ref, hidden_ref, second_ref, route_ref, upstream_ref, whole,
):
    low = jnp.bfloat16
    count, width = input_ref.shape[0], input_ref.shape[2]
    whole[...] = jnp.zeros_like(whole)
    for i in range(count):
        whole[i * PAD : i * PAD + length] = cotangent_ref[i].astype(jnp.float32)
    upstream_ref[...] = whole[...].astype(low).reshape(upstream_ref.shape)
    for i in range(count):
        whole[i * PAD : i * PAD + length] = input_ref[i].astype(jnp.float32)
    values = whole[...]
    unit, _ = unit_of(values)
    normed = (unit * norm_ref[0:1] + norm_ref[1:2]).astype(low)
    normed_ref[...] = normed.reshape(normed_ref.shape)
    queries, key_rows, value_rows = (mm(normed, dense_ref[c]).astype(low) for c in range(3))
    first_half = lax.broadcasted_iota(jnp.int32, (PAD, 2 * HEAD_DIM), 1) < HEAD_DIM
    is_key = lax.broadcasted_iota(jnp.int32, (PAD, PAD), 0) < length
    zero = jnp.zeros((PAD, 2 * HEAD_DIM), low)
    contexts = []
    for i in range(count):
        rows = slice(i * PAD, (i + 1) * PAD)
        for c, part in enumerate((queries, key_rows, value_rows)):
            projected_ref[i, c] = part[rows]
        pairs = []
        for pair in range(width // (2 * HEAD_DIM)):
            at = slice(pair * 2 * HEAD_DIM, (pair + 1) * 2 * HEAD_DIM)
            query, key, value = queries[rows, at], key_rows[rows, at], value_rows[rows, at]
            halves = []
            for side in range(2):
                mine = jnp.where(first_half == (side == 0), query, zero)
                scores = mm_turned(key, mine) * (HEAD_DIM ** (-0.5))
                scores = jnp.where(is_key, scores, -1e30)
                top = jnp.max(scores, axis=0, keepdims=True)
                raised = jnp.exp(scores - top)
                probs = (raised / jnp.sum(raised, axis=0, keepdims=True)).astype(low)
                probs_ref[i, 2 * pair + side] = probs
                halves.append(mm_rows(value, probs)[side * HEAD_DIM : (side + 1) * HEAD_DIM])
            pairs.append(jnp.concatenate(halves, axis=0).T.astype(low))
        contexts.append(jnp.concatenate(pairs, axis=1))
    context = jnp.concatenate(contexts, axis=0)
    context_ref[...] = context.reshape(context_ref.shape)
    hidden = values + mm_turned(context, dense_ref[3])
    hidden_ref[...] = hidden.reshape(hidden_ref.shape)
    unit, _ = unit_of(hidden)
    second = (unit * norm_ref[2:3] + norm_ref[3:4]).astype(low)
    second_ref[...] = second.reshape(second_ref.shape)
    logits = mm(second, router_ref[...])
    is_expert = lax.broadcasted_iota(jnp.int32, logits.shape, 1) < experts
    logits = jnp.where(is_expert, logits, -1e30)
    raised = jnp.exp(logits - jnp.max(logits, axis=-1, keepdims=True))
    route_probs = raised / jnp.sum(raised, axis=-1, keepdims=True)
    route_ref[...] = route_probs.reshape(route_ref.shape)


def attend(experts, block_input, cotangent, norm_params, dense, router_wide):
    images, length, width = block_input.shape
    heads = width // HEAD_DIM
    low, wide = jnp.bfloat16, jnp.float32

    def per_image(*shape):
        return pl.BlockSpec((TOGETHER,) + shape, lambda i: (i,) + (0,) * len(shape))

    def whole(array):
        return pl.BlockSpec(array.shape, lambda i: (0,) * array.ndim)

    shapes = [
        ((PAD, width), low), ((3, PAD, width), low), ((heads, PAD, PAD), low), ((PAD, width), low),
        ((PAD, width), wide), ((PAD, width), low), ((PAD, 128), wide), ((PAD, width), low),
    ]
    return pl.pallas_call(
        partial(attend_kernel, length, experts),
        grid=(images // TOGETHER,),
        in_specs=[per_image(length, width)] * 2 + [whole(norm_params), whole(dense), whole(router_wide)],
        out_specs=[per_image(*s) for s, _ in shapes],
        out_shape=[jax.ShapeDtypeStruct((images,) + s, t) for s, t in shapes],
        scratch_shapes=[pltpu.VMEM((TOGETHER * PAD, width), wide)],
        compiler_params=kernel_params(56),
        cost_estimate=cost(images * 2.5e9, images * 5e6),
        name="attend",
    )(block_input, cotangent, norm_params, dense, router_wide)


def dispatch_kernel(waits, slot_ref, second_ref, upstream_ref, route_ref, *refs):
    x_ref, g_ref, xt_ref, gt_ref = refs[waits:]
    low = jnp.bfloat16
    expert = pl.program_id(0)
    slots, tokens = x_ref.shape[1], second_ref.shape[0]
    rows_of = lax.broadcasted_iota(jnp.int32, (8, tokens), 0)
    slot_row = jnp.max(jnp.where(rows_of == expert, slot_ref[...], -1), axis=0, keepdims=True)
    hot = lax.broadcasted_iota(jnp.int32, (slots, tokens), 0) == slot_row
    hot = jnp.where(hot, 1.0, 0.0).astype(low)
    lanes = lax.broadcasted_iota(jnp.int32, (tokens, 128), 1)
    gate = jnp.sum(jnp.where(lanes == expert, route_ref[...], 0.0), axis=1, keepdims=True)
    pair_grad = (gate * upstream_ref[...].astype(jnp.float32)).astype(low)
    rows = mm(hot, second_ref[...]).astype(low)
    x_ref[0] = rows
    xt_ref[0] = rows.T
    rows = mm(hot, pair_grad).astype(low)
    g_ref[0] = rows
    gt_ref[0] = rows.T


def dispatch(slot_row, second, upstream, route_probs, experts, slots, waits=()):
    tokens, width = second.shape

    def whole(array):
        return pl.BlockSpec(array.shape, lambda e: (0,) * array.ndim)

    flat = pl.BlockSpec((1, slots, width), lambda e: (e, 0, 0))
    turned = pl.BlockSpec((1, width, slots), lambda e: (e, 0, 0))
    low = jnp.bfloat16
    return pl.pallas_call(
        partial(dispatch_kernel, len(waits)),
        grid=(experts,),
        in_specs=[whole(a) for a in (slot_row, second, upstream, route_probs)]
        + [pl.BlockSpec(memory_space=pl.ANY)] * len(waits),
        out_specs=[flat, flat, turned, turned],
        out_shape=[jax.ShapeDtypeStruct((experts, slots, width), low)] * 2
        + [jax.ShapeDtypeStruct((experts, width, slots), low)] * 2,
        compiler_params=kernel_params(60),
        cost_estimate=cost(4 * slots * tokens * width * experts, 1e7),
        name="dispatch",
    )(slot_row, second, upstream, route_probs, *waits)


def expert_kernel(first, last, split, count, x_ref, g_ref, xt_ref, gt_ref, *refs):
    low = jnp.bfloat16
    if not first:
        made_in, back_in = refs[:2]
        refs = refs[2:]
    sources, refs = refs[:count], refs[count:]
    _, _, rows, columns = sources[0].shape
    made_ref, back_ref, *targets, held, sent, in_sems, out_sems = refs
    expert, experts = pl.program_id(0), pl.num_programs(0)
    shards, heads, tensors = (lax.axis_size(a) for a in (SHARD, HEAD, TENSOR))
    middle = shards // 2

    def window(ref, slot, group, start=0, width=None):
        tensor, head = absolute(group)
        down = pl.multiple_of(head * rows, rows)
        over = pl.multiple_of(tensor * columns + start, 128)
        return ref.at[slot, :, pl.ds(down, rows), pl.ds(over, columns if width is None else width)]

    def fetch(source, slot, group):
        return pltpu.make_async_copy(source, window(held, slot, group), in_sems.at[slot, group])

    def start_fetch(which, slot, group):
        if count == 1:
            tensor, head = absolute(group)
            fetch(sources[0].at[(which * heads + head) * tensors + tensor], slot, group).start()
            return
        z = which ^ lax.axis_index(SHARD)
        place = group % 4 + (group // 4) * 5
        if group % 4 < 3:
            fetch(sources[place].at[z], slot, group).start()
            return

        @pl.when(z < middle)
        def _():
            fetch(sources[place].at[z], slot, group).start()

        @pl.when(z >= middle)
        def _():
            fetch(sources[place + 1].at[z - middle], slot, group).start()

    def puts(which, slot, group):
        z = which ^ lax.axis_index(SHARD)
        tensor, head = absolute(group)
        copies = []
        if split > 0:
            source, target = window(sent, slot, group, 0, split), targets[0].at[(head * tensors + tensor) * shards + z]
            copies.append(pltpu.make_async_copy(source, target, out_sems.at[slot, group, 0]))
        if split < columns:
            source = window(sent, slot, group, split, columns - split)
            target = targets[-2 + group // (GROUPS // 2)].at[group % (GROUPS // 2) * shards + z]
            copies.append(pltpu.make_async_copy(source, target, out_sems.at[slot, group, 1]))
        return copies

    slot = lax.rem(expert, 2)

    @pl.when(expert == 0)
    def _():
        for group in range(GROUPS):
            start_fetch(0, 0, group)

    @pl.when(expert + 1 < experts)
    def _():
        for group in range(GROUPS):
            start_fetch(expert + 1, 1 - slot, group)

    for group in range(GROUPS):
        fetch(sources[0].at[0], slot, group).wait()

    @pl.when(expert >= 2)
    def _():
        for group in range(GROUPS):
            for copy in puts(expert - 2, slot, group):
                copy.wait()

    x, g, xt, gt = x_ref[0], g_ref[0], xt_ref[0], gt_ref[0]
    w_in, w_out = held[slot, 0], held[slot, 1]
    v = mm(x, w_in)
    grad = mm(g, w_out)
    square = v * v
    tanh = jnp.tanh(v * (0.7978845608028654 + 0.035677408136300125 * square))
    half = 0.5 + 0.5 * tanh
    active = (v * half).astype(low)
    slope = half + v * (half * (1.0 - tanh)) * (0.7978845608028654 + 0.10703222440890037 * square)
    pre_grad = (grad * slope).astype(low)
    made = mm_turned(active, w_out)
    back = mm_turned(pre_grad, w_in)
    if not first:
        made, back = made_in[0] + made, back_in[0] + back
    made_ref[0], back_ref[0] = made.astype(made_ref.dtype), back.astype(back_ref.dtype)
    sent[slot, 0] = mm(xt, pre_grad).astype(low)
    sent[slot, 1] = mm(gt, active).astype(low)
    for group in range(GROUPS):
        for copy in puts(expert, slot, group):
            copy.start()

    @pl.when(expert == experts - 1)
    def _():
        for group in range(GROUPS):
            for copy in puts(expert - 1, 1 - slot, group):
                copy.wait()
        for group in range(GROUPS):
            for copy in puts(expert, slot, group):
                copy.wait()


def run_experts(x, g, xt, gt, sums, sources, last, split):
    experts, slots, width = x.shape
    _, kinds, rows, columns = sources[0].shape
    shards = lax.axis_size(SHARD)
    units = GROUPS * rows * columns // width
    low = jnp.bfloat16
    flat = pl.BlockSpec((1, slots, width), lambda e: (e, 0, 0))
    turned = pl.BlockSpec((1, width, slots), lambda e: (e, 0, 0))
    anywhere = pl.BlockSpec(memory_space=pl.ANY)
    kept = low if last else jnp.float32
    first = sums is None
    given = () if first else tuple(sums)
    pieces = []
    if split > 0:
        pieces += [(GROUPS * shards, kinds, rows, split)]
    if split < columns:
        pieces += [(GROUPS // 2 * shards, kinds, rows, columns - split)] * 2
    return pl.pallas_call(
        partial(expert_kernel, first, last, split, len(sources)),
        grid=(experts,),
        in_specs=[flat, flat, turned, turned] + [flat] * len(given) + [anywhere] * len(sources),
        out_specs=[flat, flat] + [anywhere] * len(pieces),
        out_shape=[jax.ShapeDtypeStruct((experts, slots, width), kept)] * 2
        + [jax.ShapeDtypeStruct(piece, low) for piece in pieces],
        scratch_shapes=[
            pltpu.VMEM((2, kinds, width, units), low),
            pltpu.VMEM((2, kinds, width, units), low),
            pltpu.SemaphoreType.DMA((2, GROUPS)),
            pltpu.SemaphoreType.DMA((2, GROUPS, 2)),
        ],
        compiler_params=kernel_params(60),
        cost_estimate=cost(12 * experts * slots * width * units, 3e7),
        name="experts",
    )(x, g, xt, gt, *given, *sources)


def combine_kernel(
    first, experts, slot_ref, made_ref, back_ref, hidden_ref, upstream_ref, second_ref, route_ref,
    norm_ref, router_ref, *refs
):
    output_ref, grad_ref, small_ref = refs if first else refs[3:]
    low = jnp.bfloat16
    image = pl.program_id(0)
    count, _, width = hidden_ref.shape
    tokens = count * PAD
    hidden = hidden_ref[...].reshape(tokens, width)
    upstream = upstream_ref[...].reshape(tokens, width).astype(jnp.float32)
    route_probs = route_ref[...].reshape(tokens, 128)
    slot_of = slot_ref[...].reshape(tokens, 128)
    slots = made_ref.shape[1]
    lanes = lax.broadcasted_iota(jnp.int32, (tokens, slots), 1)
    wide_lanes = lax.broadcasted_iota(jnp.int32, (tokens, 128), 1)
    total = hidden
    second_grad = jnp.zeros_like(hidden)
    prob_sum = jnp.zeros((tokens, 128), jnp.float32)
    gates = route_probs
    for e in range(experts):
        hot = jnp.where(lanes == slot_of[:, e : e + 1], 1.0, 0.0).astype(low)
        made = mm(hot, made_ref[e])
        second_grad = second_grad + mm(hot, back_ref[e])
        total = total + route_probs[:, e : e + 1] * made
        gate_grad = jnp.sum(upstream * made, axis=-1, keepdims=True)
        prob_sum = jnp.where(wide_lanes == e, gate_grad, prob_sum)
        gates = jnp.where(wide_lanes == experts + e, route_probs[:, e : e + 1], gates)
        prob_sum = jnp.where(wide_lanes == experts + e, gate_grad, prob_sum)
    length = output_ref.shape[1]
    for i in range(count):
        output_ref[i] = total[i * PAD : (i + 1) * PAD].astype(low)[:length]
    inner = jnp.sum(route_probs * prob_sum, axis=-1, keepdims=True)
    logit_grad = (gates * (prob_sum - inner)).astype(low)
    second_grad = second_grad + mm_turned(logit_grad, router_ref[...])
    unit, inverse = unit_of(hidden)
    grad = upstream + unit_backward(second_grad, unit, inverse, norm_ref[2:3])
    grad_ref[...] = grad.reshape(grad_ref.shape)
    router_grad = mm_rows(logit_grad, second_ref[...].reshape(tokens, width))[:8]
    gain = jnp.sum(second_grad * unit, axis=0, keepdims=True)
    bias = jnp.sum(second_grad, axis=0, keepdims=True)
    rows_of = lax.broadcasted_iota(jnp.int32, (8, hidden.shape[1]), 0)
    small = jnp.where(
        rows_of == 2, gain, jnp.where(rows_of == 3, bias, jnp.where(rows_of >= experts, router_grad, 0.0))
    )

    @pl.when(image == 0)
    def _():
        small_ref[...] = small if first else small + refs[0][...]

    @pl.when(image > 0)
    def _():
        small_ref[...] += small


def combine(which, count, length, experts, slot_column, made, back, hidden, upstream, second, route_probs, norm_params, router_wide, before):
    images, _, width = hidden.shape
    low, wide = jnp.bfloat16, jnp.float32
    first = before is None
    given = () if first else tuple(before)

    def per_image(*shape):
        return pl.BlockSpec((TOGETHER,) + shape, lambda i: (i + which // TOGETHER,) + (0,) * len(shape))

    def whole(array):
        return pl.BlockSpec(array.shape, lambda i: (0,) * array.ndim)

    small = pl.BlockSpec((8, width), lambda i: (0, 0))
    return pl.pallas_call(
        partial(combine_kernel, first, experts),
        grid=(count // TOGETHER,),
        in_specs=[
            per_image(PAD, 128), whole(made), whole(back), per_image(PAD, width), per_image(PAD, width),
            per_image(PAD, width), per_image(PAD, 128), whole(norm_params), whole(router_wide),
        ]
        + ([] if first else [small] + [pl.BlockSpec(memory_space=pl.ANY)] * 2),
        input_output_aliases={} if first else {10: 0, 11: 1},
        out_specs=[per_image(length, width), per_image(PAD, width), small],
        out_shape=[
            jax.ShapeDtypeStruct((images, length, width), low),
            jax.ShapeDtypeStruct((images, PAD, width), wide),
            jax.ShapeDtypeStruct((8, width), wide),
        ],
        compiler_params=kernel_params(60),
        cost_estimate=cost(4 * count * PAD * experts * made.shape[1] * width, 2e7),
        name="combine",
    )(slot_column, made, back, hidden, upstream, second, route_probs, norm_params, router_wide, *given)


def regroup(rows):
    return jnp.concatenate([rows[:, k : k + 128] for k in range(0, rows.shape[1], 128)], axis=0)


def two_terms(value):
    high = value.astype(jnp.bfloat16).astype(jnp.float32)
    less = (value - high).astype(jnp.bfloat16).astype(jnp.float32)
    return jnp.concatenate([high, less], axis=0).astype(jnp.bfloat16), high + less


def term_sum(terms):
    terms = terms.astype(jnp.float32)
    half = terms.shape[0] // 2
    return terms[:half] + terms[half:]


def attend_back_kernel(
    first, last, input_ref, norm_ref, dense_ref, normed_ref, projected_ref, probs_ref,
    context_ref, grad_ref, norm_grad_in, *refs
):
    low = jnp.bfloat16
    image, images = pl.program_id(0), pl.num_programs(0)
    if not first:
        sums_in = refs[0]
        refs = refs[2:]
    input_grad_ref, norm_grad_ref = refs[:2]
    if last:
        keep_ref, give_ref, sums, low_sums, packed, sems = refs[2:]
    else:
        sums = refs[2]

    @pl.when(image == 0)
    def _():
        sums[...] = jnp.zeros_like(sums) if first else sums_in[...]
        norm_grad_ref[...] = norm_grad_in[...]

    count, _, width = grad_ref.shape
    tokens = count * PAD
    hidden_grad = grad_ref[...].reshape(tokens, width)
    attended_low = hidden_grad.astype(low)
    context_grad = mm(attended_low, dense_ref[3]).astype(low)
    sums[3] += mm_rows(attended_low, context_ref[...].reshape(tokens, width))
    first_half = lax.broadcasted_iota(jnp.int32, (PAD, 2 * HEAD_DIM), 1) < HEAD_DIM
    zero = jnp.zeros((PAD, 2 * HEAD_DIM), low)
    scale = HEAD_DIM ** (-0.5)
    whole = [[], [], []]
    for i in range(count):
        parts = [[], [], []]
        for pair in range(width // (2 * HEAD_DIM)):
            at = slice(pair * 2 * HEAD_DIM, (pair + 1) * 2 * HEAD_DIM)
            query, key, value = (projected_ref[i, c, :, at] for c in range(3))
            grad = context_grad[i * PAD : (i + 1) * PAD, at]
            halves = []
            for side in range(2):
                mine = jnp.where(first_half == (side == 0), grad, zero)
                probs = probs_ref[i, 2 * pair + side]
                wide = probs.astype(jnp.float32)
                prob_grad = mm_turned(value, mine)
                weighted = wide * prob_grad
                score_grad = (
                    weighted - wide * jnp.sum(weighted, axis=0, keepdims=True)
                ).astype(low)
                query_grad = mm_rows(key, score_grad)[side * HEAD_DIM : (side + 1) * HEAD_DIM]
                halves.append((query_grad, mm(score_grad, query), mm(probs, grad)))
            parts[0].append((jnp.concatenate([halves[0][0], halves[1][0]], axis=0) * scale).T.astype(low))
            parts[1].append((jnp.where(first_half, halves[0][1], halves[1][1]) * scale).astype(low))
            parts[2].append(jnp.where(first_half, halves[0][2], halves[1][2]).astype(low))
        for kind in range(3):
            whole[kind].append(jnp.concatenate(parts[kind], axis=1))
    normed = normed_ref[...].reshape(tokens, width)
    normed_grad = None
    for kind in range(3):
        projected_grad = jnp.concatenate(whole[kind], axis=0)
        sums[kind] += mm_rows(normed, projected_grad)
        part = mm_turned(projected_grad, dense_ref[kind])
        normed_grad = part if normed_grad is None else normed_grad + part
    length = input_grad_ref.shape[1]
    gain, bias = 0.0, 0.0
    for i in range(count):
        unit, inverse = unit_of(input_ref[i].astype(jnp.float32))
        part = normed_grad[i * PAD : (i + 1) * PAD][:length]
        input_grad_ref[i] = hidden_grad[i * PAD : (i + 1) * PAD][:length] + unit_backward(
            part, unit, inverse, norm_ref[0:1]
        )
        gain = gain + jnp.sum(part * unit, axis=0, keepdims=True)
        bias = bias + jnp.sum(part, axis=0, keepdims=True)
    rows_of = lax.broadcasted_iota(jnp.int32, (8, width), 0)
    norm_grad_ref[...] += jnp.where(rows_of == 0, gain, jnp.where(rows_of == 1, bias, 0.0))

    if not last:
        return

    @pl.when(image == images - 1)
    def _():
        kinds, rows, columns = sums.shape[0], *keep_ref.shape[1:]
        near = keep_ref.shape[0] // kinds
        shards = near * 2 // GROUPS
        low_sums[...] = sums[...].astype(low)
        packed[...] = two_terms(regroup(norm_grad_ref[...]))[0]
        copies = [pltpu.make_async_copy(packed, give_ref.at[kinds * near], sems.at[2 * near])]
        for piece in range(2 * near):
            target = keep_ref if piece < near else give_ref
            copies.append(
                pltpu.make_async_copy(
                    dense_window(low_sums, piece, shards, rows, columns),
                    target.at[pl.ds(piece % near * kinds, kinds)],
                    sems.at[piece],
                )
            )
        for copy in copies:
            copy.start()
        for copy in copies:
            copy.wait()


def attend_back(which, count, block_input, norm_params, dense, kept, hidden_grad, norm_grad, carried, near_shape):
    images, length, width = block_input.shape
    heads = width // HEAD_DIM
    low, wide = jnp.bfloat16, jnp.float32
    first, last = carried is None, which + count == images
    near, kinds, rows, columns = near_shape

    def per_image(*shape):
        return pl.BlockSpec((1,) + shape, lambda i: (i + which,) + (0,) * len(shape))

    def whole(array):
        return pl.BlockSpec(array.shape, lambda i: (0,) * array.ndim)

    anywhere = pl.BlockSpec(memory_space=pl.ANY)
    small = pl.BlockSpec((8, width), lambda i: (0, 0))
    sum_shape = (4, width, width)
    given = () if first else tuple(carried)
    out_specs = [per_image(length, width), small]
    out_shape = [
        jax.ShapeDtypeStruct((images, length, width), wide),
        jax.ShapeDtypeStruct((8, width), wide),
    ]
    scratch = []
    if last:
        out_specs += [anywhere] * 2
        out_shape += [jax.ShapeDtypeStruct((near * kinds + k, rows, columns), low) for k in (0, 1)]
        scratch = [
            pltpu.VMEM(sum_shape, wide),
            pltpu.VMEM(sum_shape, low),
            pltpu.VMEM((rows, columns), low),
            pltpu.SemaphoreType.DMA((2 * near + 1,)),
        ]
    else:
        out_specs += [pl.BlockSpec(sum_shape, lambda i: (0, 0, 0))]
        out_shape += [jax.ShapeDtypeStruct(sum_shape, wide)]
    given_specs = [] if first else [whole(carried[0]), anywhere]
    return pl.pallas_call(
        partial(attend_back_kernel, first, last),
        grid=(count,),
        in_specs=[
            per_image(length, width), whole(norm_params), whole(dense),
            per_image(PAD, width), per_image(3, PAD, width), per_image(heads, PAD, PAD),
            per_image(PAD, width), per_image(PAD, width), small,
        ]
        + given_specs,
        out_specs=out_specs,
        out_shape=out_shape,
        scratch_shapes=scratch,
        input_output_aliases={} if first else {10: 0},
        compiler_params=kernel_params(60),
        cost_estimate=cost(count * 5e9, count * 6e6),
        name="attend_back",
    )(block_input, norm_params, dense, *kept, hidden_grad, norm_grad, *given)


def fold_core_kernel(quarter, keep_ref, come_ref, small_ref, x_ref, y_ref, both_ref, own_ref, own_small_ref):
    small = two_terms(regroup(small_ref[...]))[1] + term_sum(come_ref[4 * quarter])
    packed, own_small_ref[...] = two_terms(small)
    for k, target in enumerate((own_ref, x_ref, y_ref, both_ref)):
        at = slice(k * quarter, (k + 1) * quarter)
        total = keep_ref[at].astype(jnp.float32) + come_ref[at].astype(jnp.float32)
        target[:quarter] = total.astype(target.dtype)
        if k:
            target[quarter] = packed


def fold_core(keep, come, small):
    count, rows, columns = keep.shape
    quarter = count // 4
    message = jax.ShapeDtypeStruct((quarter + 1, rows, columns), jnp.bfloat16)
    return pl.pallas_call(
        partial(fold_core_kernel, quarter),
        out_shape=[message] * 3
        + [
            jax.ShapeDtypeStruct((quarter, rows, columns), jnp.float32),
            jax.ShapeDtypeStruct((rows // 2, columns), jnp.float32),
        ],
        compiler_params=kernel_params(24),
        cost_estimate=cost(1e6, 4e6),
        name="fold_core",
    )(keep, come, small)


def fold_sides_kernel(own_ref, small_ref, x_ref, y_ref, both_ref, *refs):
    messages, (total_ref, total_small_ref) = refs[:-2], refs[-2:]
    count = own_ref.shape[0]
    each = count // (len(messages) + 1)
    small = (small_ref[...] + term_sum(x_ref[count])) + (term_sum(y_ref[count]) + term_sum(both_ref[count]))
    packed, total_small_ref[...] = two_terms(small)
    for k, target in enumerate((total_ref, *messages)):
        at = slice(k * each, (k + 1) * each)
        total = own_ref[at] + sum(r[at].astype(jnp.float32) for r in (x_ref, y_ref, both_ref))
        target[:each] = total.astype(target.dtype)
        if k:
            target[each] = packed


def fold_sides(own, small, arrived, shards):
    count, rows, columns = own.shape
    each = count // shards
    message = jax.ShapeDtypeStruct((each + 1, rows, columns), jnp.bfloat16)
    return pl.pallas_call(
        fold_sides_kernel,
        out_shape=[message] * (shards - 1)
        + [jax.ShapeDtypeStruct((each, rows, columns), jnp.float32), jax.ShapeDtypeStruct(small.shape, jnp.float32)],
        compiler_params=kernel_params(24),
        cost_estimate=cost(1e6, 2e6),
        name="fold_sides",
    )(own, small, *arrived)


def dense_update_kernel(shards, own_ref, small_ref, *refs):
    arrived, refs = refs[: shards - 1], refs[shards - 1 :]
    kept, made = refs[:12], refs[12:]
    kinds = own_ref.shape[0]
    width = kept[0].shape[1]

    def update(group, at, gradient, rate, decay):
        old = [ref[at] for ref in kept[3 * group : 3 * group + 3]]
        new = adam_update(old[0], gradient, old[1], old[2], rate, decay)
        for ref, value in zip(made[3 * group : 3 * group + 3], new):
            ref[at] = value

    sums = [small_ref[...]] + [term_sum(r[kinds]) for r in arrived]
    while len(sums) > 1:
        sums = [a + b for a, b in zip(sums[::2], sums[1::2])]
    for k in range(width // 128):
        at = (slice(None), slice(k * 128, (k + 1) * 128))
        block = sums[0][k * 8 : (k + 1) * 8]
        update(0, at, block[:4], 0.25, 0.0)
        update(3, at, block[4:], 0.75 * width ** (-0.5), DECAY_RATE)
    for kind in range(kinds):
        gradient = own_ref[kind] + sum(r[kind].astype(jnp.float32) for r in arrived)
        if kind < kinds - 1:
            update(1, kind, gradient, 1.3 * width ** (-0.5), DECAY_RATE)
        else:
            update(2, (slice(None), slice(None)), gradient, 3.0 * width ** (-0.5), DECAY_RATE)


def dense_update(own, small, arrived, kept):
    return pl.pallas_call(
        partial(dense_update_kernel, len(arrived) + 1),
        out_shape=[jax.ShapeDtypeStruct(a.shape, a.dtype) for a in kept],
        compiler_params=kernel_params(24),
        cost_estimate=cost(1e6, 4e6),
        name="dense_update",
    )(own, small, *arrived, *kept)


def expert_update_kernel(first, experts, terms, *refs):
    parts, refs = refs[:terms], refs[terms:]
    kept, made = refs[:6], refs[6 if first else 12 :]
    width = 4 * kept[0].shape[1]
    rates = (1.0 * width ** (-0.5), 0.8 * experts * FF ** (-0.5))
    for kind in range(2):
        gradient = sum(r[kind].astype(jnp.float32) for r in parts)
        gradient = gradient if kind == 0 else gradient.T
        old = [ref[0] for ref in kept[3 * kind : 3 * kind + 3]]
        new = adam_update(old[0], gradient, old[1], old[2], rates[kind], DECAY_RATE)
        for ref, value in zip(made[3 * kind : 3 * kind + 3], new):
            ref[0] = value


def expert_update(parts, start, kept, before):
    _, rows, columns = parts[0].shape
    offset = start // 128
    anywhere = pl.BlockSpec(memory_space=pl.ANY)
    part = pl.BlockSpec((2, rows, 128), lambda j: (0, 0, j))
    into = pl.BlockSpec((1, rows, 128), lambda j: (0, 0, j + offset))
    out = pl.BlockSpec((1, 128, rows), lambda j: (0, j + offset, 0))
    specs = [into] * 3 + [out] * 3
    before = () if before is None else tuple(before)
    return pl.pallas_call(
        partial(expert_update_kernel, not before, lax.axis_size(SHARD), len(parts)),
        grid=(columns // 128,),
        in_specs=[part] * len(parts) + specs + [anywhere] * len(before),
        out_specs=specs,
        out_shape=[jax.ShapeDtypeStruct(a.shape, a.dtype) for a in kept],
        input_output_aliases={len(parts) + 6 + k: k for k in range(len(before))},
        compiler_params=kernel_params(24),
        cost_estimate=cost(1e6, 12 * 4 * rows * columns),
        name="expert_update",
    )(*parts, *kept, *before)


def join_sides_kernel(quarter, keep_x, keep_y, come_x, come_y, from_x, from_y, over_x, over_y):
    late = pl.program_id(0) >= quarter // 2
    x = keep_x[...].astype(jnp.float32) + come_x[...].astype(jnp.float32)
    y = keep_y[...].astype(jnp.float32) + come_y[...].astype(jnp.float32)
    over_x[...] = (x + jnp.where(late, from_y[...].astype(jnp.float32), 0.0)).astype(over_x.dtype)
    over_y[...] = (y + jnp.where(late, 0.0, from_x[...].astype(jnp.float32))).astype(over_y.dtype)


def join_sides(keep, come, from_x, from_y):
    count, *rest = keep.shape
    quarter = count // 4
    half = quarter // 2
    block = (1, *rest)

    def group(k):
        return pl.BlockSpec(block, lambda j: (k * quarter + j, 0, 0, 0))

    first = pl.BlockSpec(block, lambda j: (jnp.minimum(j, half - 1), 0, 0, 0))
    second = pl.BlockSpec(block, lambda j: (jnp.maximum(j - half, 0), 0, 0, 0))
    return pl.pallas_call(
        partial(join_sides_kernel, quarter),
        grid=(quarter,),
        in_specs=[group(1), group(2), group(1), group(2), first, second],
        out_specs=[pl.BlockSpec(block, lambda j: (j, 0, 0, 0))] * 2,
        out_shape=[jax.ShapeDtypeStruct((quarter, *rest), keep.dtype)] * 2,
        compiler_params=kernel_params(60),
        cost_estimate=cost(1e6, 8e6),
        name="join_sides",
    )(keep, keep, come, come, from_x, from_y)


def relay(block, axis, mask):
    size = lax.axis_size(axis)
    return lax.ppermute(block, axis, [(i, i ^ mask) for i in range(size)])


def relay_core(block):
    return relay(block, HEAD, 1)


def relay_x(block):
    return relay(block, HEAD, 2)


def relay_y(block):
    return relay(block, TENSOR, 1)


def relay_both(block):
    heads, tensors = lax.axis_size(HEAD), lax.axis_size(TENSOR)
    pairs = [
        (h * tensors + t, (h ^ 2) * tensors + (t ^ 1)) for h in range(heads) for t in range(tensors)
    ]
    return lax.ppermute(block, (HEAD, TENSOR), pairs)


def relay_line(blocks):
    return [relay(block, SHARD, k + 1) for k, block in enumerate(blocks)]


def ordered(values, *others):
    return lax.optimization_barrier((values, others))[0]


def wide_sum(*parts):
    return sum(p.astype(jnp.float32) for p in parts)


def local_plan(
    block_input,
    cotangent,
    routes,
    priority,
    norm_params,
    norm_moment,
    norm_square,
    qkv_weight,
    qkv_moment,
    qkv_square,
    attn_weight,
    attn_moment,
    attn_square,
    router_weight,
    router_moment,
    router_square,
    expert_in,
    in_moment,
    in_square,
    expert_out,
    out_moment,
    out_square,
):
    images, length, model_width = block_input.shape
    shards = experts = lax.axis_size(SHARD)
    capacity = 9 * images * length // (4 * experts)
    slots = -(-capacity // SLOT_PAD) * SLOT_PAD
    low = jnp.bfloat16

    dense_low = jnp.concatenate(
        [qkv_weight.transpose(1, 0, 2), attn_weight.T[None]], axis=0
    ).astype(low)
    dense_column = jnp.stack([dense_low] + relay_line([dense_low] * (shards - 1)))
    expert_low = jnp.stack([expert_in[0], expert_out[0].T]).astype(low)
    edges = [expert_low.shape[2] * edge // CUTS[-1] for edge in CUTS]
    chunks = [expert_low[:, :, i:j] for i, j in zip(edges, edges[1:])]
    tables = slot_tables(routes, priority)
    router_wide = jnp.pad(router_weight, ((0, 0), (0, 128 - experts))).astype(low)

    def line_of(block):
        return jnp.stack([block] + relay_line([block] * (shards - 1)))

    def across(column):
        return (relay_x(column), relay_y(column), relay_both(column))

    dense_column, tables, chunks[0] = ordered((dense_column, tables, chunks[0]))
    dense_sides, dense_far = across(dense_column), (relay_core(dense_column),)
    column = line_of(chunks[0])
    later = lax.all_gather(chunks[1], (SHARD, HEAD, TENSOR))
    slot_row, slot_column = find_slots(tables, experts, capacity)
    slot_column = slot_column.reshape(images, PAD, 128)
    dense_sides, dense_far, slot_row = ordered((dense_sides, dense_far, slot_row))
    dense_far += tuple(relay_core(s) for s in dense_sides)
    dense = join_dense((dense_column, *dense_sides, *dense_far), model_width)

    half = shards // 2
    column, dense = ordered((column, dense))
    over_x, over_y, far_column = relay_x(column), relay_y(column), relay_core(column)
    normed, projected, probs, context, hidden, second, route_probs, upstream = attend(
        experts, block_input, cotangent, norm_params, dense, router_wide
    )

    over_x, over_y, far_column, second = ordered((over_x, over_y, far_column, second))
    corners = (relay_y(over_x[:half]), relay_x(over_y[half:]))
    near, far = (column, over_x, over_y), (far_column, relay_core(over_x), relay_core(over_y))
    tokens = images * PAD
    slot_rows = dispatch(
        slot_row, second.reshape(tokens, model_width), upstream.reshape(tokens, model_width),
        route_probs.reshape(tokens, 128), experts, slots,
    )

    corners, far, slot_rows = ordered((corners, far, slot_rows))
    weights_a = (*near, *corners, *far, *(relay_core(c) for c in corners))
    quarter = shards

    class Returning:
        def __init__(self, keep, give):
            self.keep, self.come = keep, relay_core(give)

        def some(self, first, count):
            at = slice(first, first + count)
            return wide_sum(self.keep[at], self.come[at])

        def part(self, k):
            return self.some(k * quarter, quarter)

        def corner(self):
            half = quarter // 2
            self.corners = (
                relay_x(self.some(3 * quarter, half).astype(low)),
                relay_y(self.some(3 * quarter + half, quarter - half).astype(low)),
            )

        def sides(self):
            self.joined = join_sides(self.keep, self.come, *self.corners)
            self.over = (relay_x(self.joined[0]), relay_y(self.joined[1]))

        def line(self):
            total = self.part(0) + wide_sum(*self.over)
            self.own = total[0]
            self.others = relay_line([total[k].astype(low) for k in range(1, quarter)])

        def result(self):
            return self.own + wide_sum(*self.others)

    made, backed, grads = run_experts(*slot_rows, None, weights_a, False, edges[1])

    made, grads, later = ordered((made, grads, later))
    own_a = lax.psum_scatter(grads, (HEAD, TENSOR), scatter_dimension=0, tiled=True)
    made, backed, keep, give = run_experts(*slot_rows, (made, backed), (later,), True, 0)

    made, keep, give = ordered((made, keep, give))
    sum_b = Returning(keep, give)
    rest = (slot_column, made, backed, hidden, upstream, second, route_probs, norm_params, router_wide)
    early = TOGETHER
    block_output, hidden_grad, norm_grad = combine(0, early, length, experts, *rest, None)

    sum_b.keep, sum_b.come, norm_grad = ordered((sum_b.keep, sum_b.come, norm_grad))
    sum_b.corner()
    block_output, hidden_grad, norm_grad = combine(
        early, images - early, length, experts, *rest, (norm_grad, block_output, hidden_grad)
    )
    kept = (normed, projected, probs, context)
    half = images // 3
    dense_shape = (4 * quarter, *dense_low.shape)
    input_grad, norm_grad, dense_sums = attend_back(
        0, half, block_input, norm_params, dense, kept, hidden_grad, norm_grad, None, (4 * quarter, *dense_low.shape)
    )

    sum_b.corners, own_a, norm_grad, dense_sums = ordered((sum_b.corners, own_a, norm_grad, dense_sums))
    sum_b.sides()
    own_a = ordered(own_a, sum_b.joined)
    others_a = relay_line([own_a[k] for k in range(1, quarter)])
    input_grad, norm_grad, keep, give = attend_back(
        half, images - half, block_input, norm_params, dense, kept, hidden_grad, norm_grad,
        (dense_sums, input_grad), (4 * quarter, *dense_low.shape),
    )

    sum_b.over, others_a, keep, give = ordered((sum_b.over, others_a, keep, give))
    come = relay_core(give)
    sum_b.line()
    come, sum_b.own = ordered((come, sum_b.own))
    *messages, own, own_small = fold_core(keep, come, norm_grad)
    arrived = [send(m) for m, send in zip(messages, (relay_x, relay_y, relay_both))]
    messages, own_a, others_a = ordered((messages, own_a, others_a))
    expert_kept = (expert_in, in_moment, in_square, expert_out, out_moment, out_square)
    updated = expert_update([own_a[0], *others_a], 0, expert_kept, None)
    arrived, updated = ordered((arrived, updated))
    *messages, own, own_small = fold_sides(own, own_small, arrived, shards)
    arrived = relay_line(messages)
    updated = expert_update([sum_b.own, *sum_b.others], edges[1], expert_kept, updated)
    arrived, updated = ordered((arrived, updated))
    turns = ((0, 1), (1, 0, 2), (1, 0), (1, 0))
    dense_kept = (
        (norm_params, norm_moment, norm_square),
        (qkv_weight, qkv_moment, qkv_square),
        (attn_weight, attn_moment, attn_square),
        (router_weight, router_moment, router_square),
    )
    flat = [a.transpose(t) for t, group in zip(turns, dense_kept) for a in group]
    dense_new = dense_update(own, own_small, arrived, flat)
    dense_new = [a.transpose(turns[k // 3]) for k, a in enumerate(dense_new)]
    return (block_output, input_grad, *dense_new, *updated)


def solution(mesh):
    fits = mesh.shape[SHARD] <= 4
    return jax.shard_map(
        local_plan if fits else slot_plan,
        mesh=mesh,
        in_specs=(
            P((SHARD, HEAD, TENSOR), None, None),
            P((SHARD, HEAD, TENSOR), None, None),
            P((SHARD, HEAD, TENSOR), None, None),
            P((SHARD, HEAD, TENSOR), None),
            P(),
            P(),
            P(),
            P((SHARD, TENSOR), None, HEAD),
            P((SHARD, TENSOR), None, HEAD),
            P((SHARD, TENSOR), None, HEAD),
            P(HEAD, (SHARD, TENSOR)),
            P(HEAD, (SHARD, TENSOR)),
            P(HEAD, (SHARD, TENSOR)),
            P(),
            P(),
            P(),
            P(SHARD, HEAD, TENSOR),
            P(SHARD, HEAD, TENSOR),
            P(SHARD, HEAD, TENSOR),
            P(SHARD, TENSOR, HEAD),
            P(SHARD, TENSOR, HEAD),
            P(SHARD, TENSOR, HEAD),
        ),
        out_specs=(
            P((SHARD, HEAD, TENSOR), None, None),
            P((SHARD, HEAD, TENSOR), None, None),
            P(),
            P(),
            P(),
            P((SHARD, TENSOR), None, HEAD),
            P((SHARD, TENSOR), None, HEAD),
            P((SHARD, TENSOR), None, HEAD),
            P(HEAD, (SHARD, TENSOR)),
            P(HEAD, (SHARD, TENSOR)),
            P(HEAD, (SHARD, TENSOR)),
            P(),
            P(),
            P(),
            P(SHARD, HEAD, TENSOR),
            P(SHARD, HEAD, TENSOR),
            P(SHARD, HEAD, TENSOR),
            P(SHARD, TENSOR, HEAD),
            P(SHARD, TENSOR, HEAD),
            P(SHARD, TENSOR, HEAD),
        ),
        check_vma=False,
    )
```
